128 devices in a mesh: dp: 4 (over z), seq: 32 (over x, y, core).
Axes of the slice: x: 4, y: 4, z: 4, core: 2. Of those that a mesh axis runs over, the one named last changes fastest.
Arguments:
- image: bfloat16 [8, 192, 40, 256], P('dp', 'seq'), may hold values from -20 to 20
- embedding: bfloat16 [8, 512], P('dp'), may hold values from -6 to 6
- cotangent: bfloat16 [8, 192, 40, 256], P('dp', 'seq'), may hold values from -6 to 6
- valid_rows: int32 [8], P('dp'), may hold values from 48 to 192, as said below
- orientation: int32 [8], P('dp'), may hold values from 0 to 1
- gn1_gain: float32 [256], replicated, may hold values from 0.1 to 1.9
- gn1_bias: float32 [256], replicated, may hold values from -1.75 to 1.75
- conv1_weight: bfloat16 [3, 3, 256, 256], replicated, may hold values from -0.125 to 0.125
- conv1_bias: float32 [256], replicated, may hold values from -1.75 to 1.75
- time_weight: bfloat16 [512, 512], replicated, may hold values from -0.25 to 0.25
- time_bias: float32 [512], replicated, may hold values from -1.75 to 1.75
- gn2_gain: float32 [256], replicated, may hold values from 0.1 to 1.9
- gn2_bias: float32 [256], replicated, may hold values from -1.75 to 1.75
- conv2_weight: bfloat16 [3, 3, 256, 256], replicated, may hold values from -0.125 to 0.125
- conv2_bias: float32 [256], replicated, may hold values from -1.75 to 1.75
- gn3_gain: float32 [256], replicated, may hold values from 0.1 to 1.9
- gn3_bias: float32 [256], replicated, may hold values from -1.75 to 1.75
- qkv_weight: bfloat16 [256, 768], replicated, may hold values from -0.5 to 0.5
- qv_bias: float32 [512], replicated, may hold values from -1.75 to 1.75
- proj_weight: bfloat16 [256, 256], replicated, may hold values from -1.5 to 1.5
- proj_bias: float32 [256], replicated, may hold values from -1.75 to 1.75
Outputs:
- output: bfloat16 [8, 192, 40, 256], P('dp', 'seq')
- image_grad: bfloat16 [8, 192, 40, 256], P('dp', 'seq')
- embedding_grad: float32 [8, 512], P('dp')
- gn1_gain_grad: float32 [256], replicated
- gn1_bias_grad: float32 [256], replicated
- conv1_weight_grad: float32 [3, 3, 256, 256], replicated
- conv1_bias_grad: float32 [256], replicated
- time_weight_grad: float32 [512, 512], replicated
- time_bias_grad: float32 [512], replicated
- gn2_gain_grad: float32 [256], replicated
- gn2_bias_grad: float32 [256], replicated
- conv2_weight_grad: float32 [3, 3, 256, 256], replicated
- conv2_bias_grad: float32 [256], replicated
- gn3_gain_grad: float32 [256], replicated
- gn3_bias_grad: float32 [256], replicated
- qkv_weight_grad: float32 [256, 768], replicated
- qv_bias_grad: float32 [512], replicated
- proj_weight_grad: float32 [256, 256], replicated
- proj_bias_grad: float32 [256], replicated
The draws below stay inside these ranges and needn't reach their ends.
Inputs may be any that keep to these rules, and one draw needn't show every extreme that they name: `valid_rows`: in every run of 2 consecutive images (one index of dp) one image has all 192 rows valid.
All inputs are finite; a program needn't handle non-finite values.
Results may differ from the reference program's by a relative error of at most 0.025.
The reference program's roundings to bfloat16 on the way count: a program that leaves them out, or rounds other values in their place, can miss the bound.
Values may be sent and summed in bfloat16 or wider, within the bound.
No kernel may reach another device: no remote copies, remote signals or barrier semaphores. Data moves between devices by JAX's collectives and lax.ppermute only.
A program may use at most 256 MiB of HBM per device.

```python
import math
import jax
import jax.numpy as jnp
from jax import lax

CHANNELS = 256
GROUPS = 32
HEAD_COUNT = 4
HEAD_DIM = 64
EMB_DIM = 512
COLUMNS = 40
IMG_GRP = 2
HEIGHT = 192
IMAGES = 8


def draw_image(key, part):
    key = jax.random.fold_in(key, 3)
    chan_key, noise_key = jax.random.split(key, 2)
    rising = 10.0 ** ((jnp.arange(HEIGHT, dtype=jnp.float32) / (HEIGHT - 1) - 0.5) * 0.66)
    channel_scale = 10.0 ** jax.random.uniform(chan_key, (CHANNELS,), minval=-0.3, maxval=0.3)
    shape = (IMAGES, HEIGHT, COLUMNS, CHANNELS)
    noise = jnp.clip(jax.random.normal(noise_key, shape), -4.0, 4.0)
    return (noise * rising[None, :, None, None] * channel_scale).astype(jnp.bfloat16)


def draw_valid_rows(key, part):
    key = jax.random.fold_in(key, 7)
    rows_key, pick_key, short_key = jax.random.split(key, 3)
    counts = jax.random.randint(rows_key, (IMAGES,), HEIGHT // 4, HEIGHT + 1)
    groups_total = IMAGES // IMG_GRP
    chosen = jax.random.randint(pick_key, (groups_total,), 0, IMG_GRP)
    slots = jnp.arange(IMAGES, dtype=jnp.int32)
    full_image = slots % IMG_GRP == jnp.repeat(chosen, IMG_GRP)
    short_group = jax.random.randint(short_key, (), 0, groups_total)
    short_image = short_group * IMG_GRP + (chosen[short_group] + 1) % IMG_GRP
    counts = jnp.where(slots == short_image, HEIGHT // 4, counts)
    return jnp.where(full_image, HEIGHT, counts).astype(jnp.int32)


def place_ends(result, key, smallest, high):
    longest = result.shape.index(max(result.shape))
    spots = []
    for shift in (0, 1):
        where = [jax.random.randint(jax.random.fold_in(key, axis), (), 0, length) for axis, length in enumerate(result.shape)]
        where[longest] = (where[longest] + shift) % result.shape[longest]
        spots.append(tuple(where))
    return result.at[spots[0]].set(smallest).at[spots[1]].set(high)


def shard_levels(stream_key, extent, cuts, smallest, top_value):
    loudness = 1.0
    for dim, blocks in cuts:
        heights = jax.random.uniform(jax.random.fold_in(jax.random.fold_in(stream_key, 6), dim), (blocks,), jnp.float32, smallest / len(cuts), top_value / len(cuts))
        loudness = loudness * jnp.repeat(jnp.exp(heights), extent[dim] // blocks).reshape((-1,) + (1,) * (len(extent) - 1 - dim))
    return loudness


def bell_draw(own_key, shape, deviation, limit, shards=(), kind=jnp.bfloat16):
    level = shard_levels(own_key, shape, shards, -0.22, 0.18) if shards else 1.0
    drawn = jax.random.normal(own_key, shape, jnp.float32) * deviation * level
    return jnp.minimum(jnp.maximum(drawn, -limit), limit).astype(kind)


def setup_inputs(seed: int = 0) -> dict:
    seeds = jax.random.split(jax.random.key(seed), 22)
    image = draw_image(jax.random.fold_in(seeds[21], 71), 0)
    embedding = bell_draw(seeds[1], (IMAGES, EMB_DIM), 1.0, 6.0, ((0, 4),))
    cotangent = bell_draw(seeds[2], (IMAGES, HEIGHT, COLUMNS, CHANNELS), 1.0, 6.0, ((0, 4), (1, 32)))
    valid_rows = draw_valid_rows(jax.random.fold_in(seeds[21], 71), 0)
    orientation = place_ends(jax.random.randint(seeds[4], (IMAGES,), 0, 2), jax.random.fold_in(seeds[4], 1), 0, 1).astype(jnp.int32)
    gn1_gain = jnp.clip(1.0 + 0.18 * jax.random.normal(seeds[5], (CHANNELS,), jnp.float32), 0.1, 1.9)
    gn1_bias = bell_draw(seeds[6], (CHANNELS,), 0.3, 1.75, (), jnp.float32)
    conv1_weight = bell_draw(seeds[7], (3, 3, CHANNELS, CHANNELS), (9 * CHANNELS) ** -0.5, 0.125)
    conv1_bias = bell_draw(seeds[8], (CHANNELS,), 0.3, 1.75, (), jnp.float32)
    time_weight = bell_draw(seeds[9], (EMB_DIM, 2 * CHANNELS), EMB_DIM ** -0.5, 0.25)
    time_bias = bell_draw(seeds[10], (2 * CHANNELS,), 0.3, 1.75, (), jnp.float32)
    gn2_gain = jnp.clip(1.0 + 0.18 * jax.random.normal(seeds[11], (CHANNELS,), jnp.float32), 0.1, 1.9)
    gn2_bias = bell_draw(seeds[12], (CHANNELS,), 0.3, 1.75, (), jnp.float32)
    conv2_weight = bell_draw(seeds[13], (3, 3, CHANNELS, CHANNELS), (9 * CHANNELS) ** -0.5, 0.125)
    conv2_bias = bell_draw(seeds[14], (CHANNELS,), 0.3, 1.75, (), jnp.float32)
    gn3_gain = jnp.clip(1.0 + 0.18 * jax.random.normal(seeds[15], (CHANNELS,), jnp.float32), 0.1, 1.9)
    gn3_bias = bell_draw(seeds[16], (CHANNELS,), 0.3, 1.75, (), jnp.float32)
    qkv_weight = bell_draw(seeds[17], (CHANNELS, 3 * CHANNELS), (CHANNELS // 2) ** -0.5, 0.5)
    qv_bias = bell_draw(seeds[18], (2 * CHANNELS,), 0.3, 1.75, (), jnp.float32)
    proj_weight = bell_draw(seeds[19], (CHANNELS, CHANNELS), (CHANNELS // 16) ** -0.5, 1.5)
    proj_bias = bell_draw(seeds[20], (CHANNELS,), 0.3, 1.75, (), jnp.float32)
    return {"image": image, "embedding": embedding, "cotangent": cotangent, "valid_rows": valid_rows, "orientation": orientation, "gn1_gain": gn1_gain, "gn1_bias": gn1_bias, "conv1_weight": conv1_weight, "conv1_bias": conv1_bias, "time_weight": time_weight, "time_bias": time_bias, "gn2_gain": gn2_gain, "gn2_bias": gn2_bias, "conv2_weight": conv2_weight, "conv2_bias": conv2_bias, "gn3_gain": gn3_gain, "gn3_bias": gn3_bias, "qkv_weight": qkv_weight, "qv_bias": qv_bias, "proj_weight": proj_weight, "proj_bias": proj_bias}


EPS = 1e-05
LOWEST = -1e+30

@jax.custom_vjp
def low(v):
    return lax.optimization_barrier(v.astype(jnp.bfloat16)).astype(jnp.float32)

@jax.custom_vjp
def low_back(v):
    return v

def low_keep(v):
    return (low(v), None)

def low_pass(kept, grad):
    return (grad,)

def back_keep(v):
    return (v, None)

def back_low(kept, grad):
    return (low(grad),)
low.defvjp(low_keep, low_pass)
low_back.defvjp(back_keep, back_low)

def matmul(left, right):
    return jnp.dot(left, right, precision=lax.Precision.HIGHEST)

def group_norm(values, counts, norm_gain, norm_bias):
    grouped = values.reshape(-1, GROUPS, CHANNELS // GROUPS)
    first_mean = lax.optimization_barrier(jnp.sum(grouped, axis=(0, 2))) / counts
    second_mean = lax.optimization_barrier(jnp.sum(grouped * grouped, axis=(0, 2))) / counts
    spread = lax.rsqrt(second_mean - first_mean * first_mean + EPS)
    normed = (grouped - first_mean[None, :, None]) * spread[None, :, None]
    return normed.reshape(values.shape) * norm_gain + norm_bias

def convolve(active, weight):
    return lax.conv_general_dilated(active[None], weight, (1, 1), 'SAME', dimension_numbers=('NHWC', 'HWIO', 'NHWC'), precision=lax.Precision.HIGHEST)[0]

def attention(third, keymask, qkv_weight, qv_bias):
    tokens = third.reshape(HEIGHT * COLUMNS, CHANNELS)
    mixture = matmul(tokens, qkv_weight)
    queries = low_back(low(mixture[:, :CHANNELS] + qv_bias[:CHANNELS]))
    key_rows = low_back(low(mixture[:, CHANNELS:2 * CHANNELS]))
    value_rows = low_back(low(mixture[:, 2 * CHANNELS:] + qv_bias[CHANNELS:]))
    key_rows = key_rows.reshape(-1, HEAD_COUNT, HEAD_DIM)
    value_rows = value_rows.reshape(-1, HEAD_COUNT, HEAD_DIM)
    block_rows = math.gcd(HEIGHT, 16) * COLUMNS
    blocks = queries.reshape(-1, block_rows, HEAD_COUNT, HEAD_DIM)
    factor = HEAD_DIM ** (-0.5)

    @jax.checkpoint
    def one_block(query_block):
        scores = jnp.einsum('qhd,khd->hqk', query_block, key_rows, precision=lax.Precision.HIGHEST)
        scores = low_back(scores) * factor
        scores = jnp.where(keymask[None, None, :], scores, LOWEST)
        peak_value = lax.optimization_barrier(jnp.max(scores, axis=-1, keepdims=True))
        weights = jnp.where(keymask[None, None, :], jnp.exp(scores - peak_value), 0.0)
        weights = weights / lax.optimization_barrier(jnp.sum(weights, axis=-1, keepdims=True))
        return jnp.einsum('hqk,khd->qhd', low(weights), value_rows, precision=lax.Precision.HIGHEST)
    attended = lax.map(one_block, blocks)
    return attended.reshape(HEIGHT * COLUMNS, CHANNELS)

def forward(picture, vector, valid_mask, keymask, counts, params):
    gn1_gain, gn1_bias, conv1_weight, conv1_bias, time_weight, time_bias, gn2_gain, gn2_bias, conv2_weight, conv2_bias, gn3_gain, gn3_bias, qkv_weight, qv_bias, proj_weight, proj_bias = params
    masked_input = valid_mask * picture
    first_active = low(jax.nn.silu(valid_mask * group_norm(masked_input, counts, gn1_gain, gn1_bias)))
    hidden = valid_mask * low_back(convolve(first_active, conv1_weight) + conv1_bias)
    shifts = low_back(matmul(low(jax.nn.silu(vector))[None], time_weight)[0] + time_bias)
    scaling = shifts[:CHANNELS]
    offset = shifts[CHANNELS:]
    second_norm = valid_mask * (group_norm(hidden, counts, gn2_gain, gn2_bias) * (1.0 + scaling) + offset)
    second_active = low(jax.nn.silu(second_norm))
    branch = valid_mask * low_back(convolve(second_active, conv2_weight) + conv2_bias)
    residual = masked_input + branch
    third = low(valid_mask * group_norm(residual, counts, gn3_gain, gn3_bias))
    attended = attention(third, keymask, qkv_weight, qv_bias)
    projected = low_back(matmul(low(low_back(attended)), proj_weight) + proj_bias)
    return residual + valid_mask * projected.reshape(residual.shape)

def reference(image, embedding, cotangent, valid_rows, orientation, gn1_gain, gn1_bias, conv1_weight, conv1_bias, time_weight, time_bias, gn2_gain, gn2_bias, conv2_weight, conv2_bias, gn3_gain, gn3_bias, qkv_weight, qv_bias, proj_weight, proj_bias):
    params = tuple((item.astype(jnp.float32) for item in (gn1_gain, gn1_bias, conv1_weight, conv1_bias, time_weight, time_bias, gn2_gain, gn2_bias, conv2_weight, conv2_bias, gn3_gain, gn3_bias, qkv_weight, qv_bias, proj_weight, proj_bias)))
    row_ids = jnp.arange(HEIGHT, dtype=jnp.int32)
    col_ids = jnp.arange(COLUMNS, dtype=jnp.int32)

    def one_image(totals, inputs):
        picture, vector, cotan_image, row_count, turned = inputs
        col_count = COLUMNS - 2 * COLUMNS // 5 * turned
        valid_grid = (row_ids[:, None] < row_count) & (col_ids[None, :] < col_count)
        valid_mask = valid_grid.astype(jnp.float32)[:, :, None]
        keymask = valid_grid.reshape(-1)
        counts = (row_count * col_count).astype(jnp.float32) * (CHANNELS // GROUPS)

        def apply_layer(picture_in, vector_in, params_in):
            return forward(picture_in, vector_in, valid_mask, keymask, counts, params_in)
        output, pullback = jax.vjp(apply_layer, picture, vector, params)
        picture_grad, vector_grad, param_grads = pullback(cotan_image)
        totals = jax.tree.map(lambda left, right: left + right, totals, param_grads)
        return (totals, (output.astype(jnp.bfloat16), picture_grad.astype(jnp.bfloat16), vector_grad))
    zero_grads = jax.tree.map(jnp.zeros_like, params)
    totals, (outputs, image_grads, embedding_grads) = lax.scan(one_image, zero_grads, (image.astype(jnp.float32), embedding.astype(jnp.float32), cotangent.astype(jnp.float32), valid_rows, orientation))
    return (outputs, image_grads, embedding_grads, totals[0], totals[1], totals[2], totals[3], totals[4], totals[5], totals[6], totals[7], totals[8], totals[9], totals[10], totals[11], totals[12], totals[13], totals[14], totals[15])
```

```python
import jax
import jax.numpy as jnp
from jax import lax
from jax.sharding import PartitionSpec as P

GROUPS = 32
HEAD_COUNT = 4


EPS = 1e-05
LOWEST = -1e30


def padded_2(block, sides, width):
    for axis, dim in sides:
        count = lax.axis_size(axis)
        forward = [(i, i + 1) for i in range(count - 1)]
        backward = [(target, source) for source, target in forward]
        low = lax.ppermute(
            lax.slice_in_dim(block, block.shape[dim] - width, None, axis=dim), axis, forward
        )
        high = lax.ppermute(lax.slice_in_dim(block, 0, width, axis=dim), axis, backward)
        block = jnp.concatenate([low, block, high], axis=dim)
    return block


def silu_slope(values):
    sigmoid = jax.nn.sigmoid(values)
    return sigmoid * (1.0 + values * (1.0 - sigmoid))


def by_group(values):
    return values.reshape(values.shape[0], -1, GROUPS, values.shape[-1] // GROUPS)


def seq_shift(value, dx, dy, dc):
    pairs = []
    for place in range(32):
        x, y, c = place // 8, place // 2 % 4, place % 2
        pairs.append((place, (x + dx) % 4 * 8 + (y + dy) % 4 * 2 + (c + dc) % 2))
    return lax.ppermute(value, "seq", pairs)


def seq_total(value):
    value = value + seq_shift(value, 0, 0, 1)
    value = (value + seq_shift(value, 0, 2, 0)) + (seq_shift(value, 0, 1, 0) + seq_shift(value, 0, 3, 0))
    return (value + seq_shift(value, 2, 0, 0)) + (seq_shift(value, 1, 0, 0) + seq_shift(value, 3, 0, 0))


def group_totals(first_part, second_part):
    both = seq_total(jnp.concatenate([first_part, second_part], axis=-1))
    return both[:, :GROUPS], both[:, GROUPS:]


def group_parts(values, normed):
    return (jnp.sum(by_group(values), axis=(1, 3)), jnp.sum(by_group(values * normed), axis=(1, 3)))


def norm_forward(values, valid_mask, counts):
    grouped = by_group(values)
    first_sum, second_sum = group_totals(
        jnp.sum(grouped, axis=(1, 3)), jnp.sum(grouped * grouped, axis=(1, 3))
    )
    average = first_sum / counts[:, None]
    spread = lax.rsqrt(second_sum / counts[:, None] - average * average + EPS)
    normed = (grouped - average[:, None, :, None]) * spread[:, None, :, None]
    return (valid_mask * normed.reshape(values.shape), spread)


def norm_input_grad(grad_hat, normed, spread, valid_mask, counts, first_sum, second_sum):
    first_mean = (first_sum / counts[:, None])[:, None, :, None]
    second_mean = (second_sum / counts[:, None])[:, None, :, None]
    result = spread[:, None, :, None] * (
        by_group(grad_hat) - first_mean - by_group(normed) * second_mean
    )
    return valid_mask * result.reshape(grad_hat.shape)


def patches(padded, shard_rows, columns):
    widened = jnp.pad(padded, ((0, 0), (0, 0), (1, 1), (0, 0)))
    return jnp.concatenate(
        [
            widened[:, row_off : row_off + shard_rows, col_off : col_off + columns, :]
            for row_off in range(3)
            for col_off in range(3)
        ],
        axis=-1,
    )


def conv_forward(active, weight):
    padded = padded_2(active, (("seq", 1),), 1)
    gathered = patches(padded, active.shape[1], active.shape[2])
    flat_weight = weight.reshape(-1, weight.shape[-1])
    return (jnp.dot(gathered, flat_weight, preferred_element_type=jnp.float32), gathered)


def conv_backward(grad_low, gathered, weight):
    weight_grad = jnp.einsum(
        "nrwk,nrwo->ko", gathered, grad_low, preferred_element_type=jnp.float32
    ).reshape(weight.shape)
    bias_grad = jnp.sum(grad_low, axis=(0, 1, 2), dtype=jnp.float32)
    padded = padded_2(grad_low, (("seq", 1),), 1)
    flipped = jnp.transpose(weight[::-1, ::-1], (0, 1, 3, 2)).reshape(-1, weight.shape[-1])
    input_grad = jnp.dot(
        patches(padded, grad_low.shape[1], grad_low.shape[2]),
        flipped,
        preferred_element_type=jnp.float32,
    )
    return (input_grad, weight_grad, bias_grad)


def key_valid(first_row, length, valid_rows, col_valid, columns):
    positions = first_row + jnp.arange(length, dtype=jnp.int32)
    row_ok = (positions // columns)[None, :] < valid_rows[:, None]
    col_ok = (positions % columns)[None, :] < col_valid[:, None]
    return row_ok & col_ok


def split_heads(values):
    return values.reshape(values.shape[0], values.shape[1], HEAD_COUNT, -1)


def attend_piece(carried, pieces, first_row, query_heads, valid_rows, col_valid, columns):
    maxima, totals, accumulated = carried
    key_heads = split_heads(pieces[0])
    value_heads = split_heads(pieces[1])
    keymask = key_valid(first_row, key_heads.shape[1], valid_rows, col_valid, columns)[
        :, None, None, :
    ]
    factor = query_heads.shape[-1] ** (-0.5)
    scores = (
        jnp.einsum("iqhd,ikhd->ihqk", query_heads, key_heads, preferred_element_type=jnp.float32)
        * factor
    )
    scores = jnp.where(keymask, scores, LOWEST)
    new_max = jnp.maximum(maxima, jnp.max(scores, axis=-1))
    weights = jnp.where(keymask, jnp.exp(scores - new_max[..., None]), 0.0)
    totals = jnp.sum(weights, axis=-1)
    accumulated = jnp.einsum(
        "ihqk,ikhd->ihqd",
        weights.astype(jnp.bfloat16),
        value_heads,
        preferred_element_type=jnp.float32,
    )
    return (new_max, totals, accumulated)


def full_grads(query_heads, grad_heads, key_heads, value_heads, keymask, logsum, delta_rows):
    factor = query_heads.shape[-1] ** (-0.5)
    scores = (
        jnp.einsum("iqhd,ikhd->ihqk", query_heads, key_heads, preferred_element_type=jnp.float32)
        * factor
    )
    scores = jnp.where(keymask, scores, LOWEST)
    weights = jnp.where(keymask, jnp.exp(scores - logsum[..., None]), 0.0)
    weight_grad = jnp.einsum(
        "iqhd,ikhd->ihqk", grad_heads, value_heads, preferred_element_type=jnp.float32
    )
    score_grad = (weights * (weight_grad - delta_rows[..., None]) * factor).astype(jnp.bfloat16)
    return (weights.astype(jnp.bfloat16), score_grad)


def per_device(
    image,
    embedding,
    cotangent,
    valid_rows,
    orientation,
    gn1_gain,
    gn1_bias,
    conv1_weight,
    conv1_bias,
    time_weight,
    time_bias,
    gn2_gain,
    gn2_bias,
    conv2_weight,
    conv2_bias,
    gn3_gain,
    gn3_bias,
    qkv_weight,
    qv_bias,
    proj_weight,
    proj_bias,
):
    images, shard_rows, columns, channels = image.shape
    tokens = shard_rows * columns
    head_width = channels // HEAD_COUNT
    seq_index = lax.axis_index("seq")
    row_ids = seq_index * shard_rows + jnp.arange(shard_rows, dtype=jnp.int32)
    col_valid = columns - 2 * columns // 5 * orientation
    pixel_ok = (row_ids[None, :, None] < valid_rows[:, None, None]) & (
        jnp.arange(columns, dtype=jnp.int32)[None, None, :] < col_valid[:, None, None]
    )
    valid_mask = pixel_ok.astype(jnp.float32)[..., None]
    counts = (valid_rows * col_valid).astype(jnp.float32) * (channels // GROUPS)
    masked_input = valid_mask * image.astype(jnp.float32)
    first_hat, first_spread = norm_forward(masked_input, valid_mask, counts)
    first_norm = valid_mask * (first_hat * gn1_gain + gn1_bias)
    first_active = jax.nn.silu(first_norm).astype(jnp.bfloat16)
    first_conv, first_patch = conv_forward(first_active, conv1_weight)
    hidden = valid_mask * (first_conv + conv1_bias)
    time_input = jax.nn.silu(embedding.astype(jnp.float32)).astype(jnp.bfloat16)
    shifts = jnp.dot(time_input, time_weight, preferred_element_type=jnp.float32) + time_bias
    scaling = shifts[:, None, None, :channels]
    offset = shifts[:, None, None, channels:]
    second_hat, second_spread = norm_forward(hidden, valid_mask, counts)
    second_base = valid_mask * (second_hat * gn2_gain + gn2_bias)
    second_norm = valid_mask * (second_base * (1.0 + scaling) + offset)
    second_active = jax.nn.silu(second_norm).astype(jnp.bfloat16)
    second_conv, second_patch = conv_forward(second_active, conv2_weight)
    residual = masked_input + valid_mask * (second_conv + conv2_bias)
    third_hat, third_spread = norm_forward(residual, valid_mask, counts)
    third_low = (
        (valid_mask * (third_hat * gn3_gain + gn3_bias))
        .astype(jnp.bfloat16)
        .reshape(images, tokens, channels)
    )
    mixture = jnp.dot(third_low, qkv_weight, preferred_element_type=jnp.float32)
    queries = (mixture[..., :channels] + qv_bias[:channels]).astype(jnp.bfloat16)
    keys_low = mixture[..., channels : 2 * channels].astype(jnp.bfloat16)
    values_low = (mixture[..., 2 * channels :] + qv_bias[channels:]).astype(jnp.bfloat16)
    query_heads = split_heads(queries)
    initial = (
        jnp.full((images, HEAD_COUNT, tokens), LOWEST, jnp.float32),
        jnp.zeros((images, HEAD_COUNT, tokens), jnp.float32),
        jnp.zeros((images, HEAD_COUNT, tokens, head_width), jnp.float32),
    )
    maxima, totals, accumulated = attend_piece(
        initial,
        (
            lax.all_gather(keys_low, "seq", axis=1, tiled=True),
            lax.all_gather(values_low, "seq", axis=1, tiled=True),
        ),
        jnp.int32(0),
        query_heads,
        valid_rows,
        col_valid,
        columns,
    )
    attended = jnp.transpose(accumulated / totals[..., None], (0, 2, 1, 3))
    logsum = maxima + jnp.log(totals)
    attended_low = attended.reshape(images, tokens, channels).astype(jnp.bfloat16)
    projected = jnp.dot(attended_low, proj_weight, preferred_element_type=jnp.float32) + proj_bias
    output = (residual + valid_mask * projected.reshape(residual.shape)).astype(jnp.bfloat16)
    cotan_full = cotangent.astype(jnp.float32)
    proj_grad = (valid_mask * cotan_full).astype(jnp.bfloat16).reshape(images, tokens, channels)
    proj_weight_grad = jnp.einsum(
        "itc,itd->cd", attended_low, proj_grad, preferred_element_type=jnp.float32
    )
    proj_bias_grad = jnp.sum(proj_grad, axis=(0, 1), dtype=jnp.float32)
    attended_grad = jnp.einsum(
        "itd,cd->itc", proj_grad, proj_weight, preferred_element_type=jnp.float32
    ).astype(jnp.bfloat16)
    grad_heads = split_heads(attended_grad)
    delta_rows = jnp.transpose(
        jnp.sum(grad_heads.astype(jnp.float32) * attended, axis=-1), (0, 2, 1)
    )
    every_key, every_value = (
        lax.all_gather(keys_low, "seq", axis=1, tiled=True),
        lax.all_gather(values_low, "seq", axis=1, tiled=True),
    )
    every_key_heads = split_heads(every_key)
    every_value_heads = split_heads(every_value)
    all_mask = key_valid(0, every_key.shape[1], valid_rows, col_valid, columns)[:, None, None, :]
    weights_low, score_grad = full_grads(
        query_heads, grad_heads, every_key_heads, every_value_heads, all_mask, logsum, delta_rows
    )
    query_grad = (
        jnp.einsum(
            "ihqk,ikhd->iqhd", score_grad, every_key_heads, preferred_element_type=jnp.float32
        )
        .astype(jnp.bfloat16)
        .reshape(images, tokens, channels)
    )
    key_term = jnp.einsum(
        "ihqk,iqhd->kihd", score_grad, query_heads, preferred_element_type=jnp.float32
    )
    value_term = jnp.einsum(
        "ihqk,iqhd->kihd", weights_low, grad_heads, preferred_element_type=jnp.float32
    )
    term_rows = jnp.transpose(
        lax.psum_scatter(
            jnp.concatenate([key_term, value_term], axis=2)
            .reshape(tokens * lax.axis_size("seq"), images, 2 * channels)
            .astype(jnp.bfloat16),
            "seq",
            scatter_dimension=0,
            tiled=True,
        ).astype(jnp.float32),
        (1, 0, 2),
    )
    key_grad = term_rows[..., :channels].astype(jnp.bfloat16)
    value_grad = term_rows[..., channels:].astype(jnp.bfloat16)
    mixture_grad = jnp.concatenate([query_grad, key_grad, value_grad], axis=-1)
    third_grad = jnp.einsum(
        "itk,ck->itc", mixture_grad, qkv_weight, preferred_element_type=jnp.float32
    ).reshape(residual.shape)
    qkv_weight_grad = jnp.einsum(
        "itc,itk->ck", third_low, mixture_grad, preferred_element_type=jnp.float32
    )
    qv_bias_grad = jnp.concatenate(
        [
            jnp.sum(query_grad, axis=(0, 1), dtype=jnp.float32),
            jnp.sum(value_grad, axis=(0, 1), dtype=jnp.float32),
        ]
    )
    third_up = valid_mask * third_grad
    gn3_gain_grad = jnp.sum(third_up * third_hat, axis=(0, 1, 2))
    gn3_bias_grad = jnp.sum(third_up, axis=(0, 1, 2))
    third_dhat = third_up * gn3_gain
    first_part, second_part = group_parts(third_dhat, third_hat)
    first_sum, second_sum = group_totals(first_part, second_part)
    residual_grad = cotan_full + norm_input_grad(
        third_dhat, third_hat, third_spread, valid_mask, counts, first_sum, second_sum
    )
    branch_low = (valid_mask * residual_grad).astype(jnp.bfloat16)
    active2_grad, conv2_weight_grad, conv2_bias_grad = conv_backward(
        branch_low, second_patch, conv2_weight
    )
    norm2_grad = valid_mask * active2_grad * silu_slope(second_norm)
    scale_part = jnp.sum(norm2_grad * second_base, axis=(1, 2))
    offset_part = jnp.sum(norm2_grad, axis=(1, 2))
    base_grad = norm2_grad * (1.0 + scaling)
    gn2_gain_grad = jnp.sum(base_grad * second_hat, axis=(0, 1, 2))
    gn2_bias_grad = jnp.sum(base_grad, axis=(0, 1, 2))
    second_dhat = base_grad * gn2_gain
    first_part, second_part = group_parts(second_dhat, second_hat)
    sums = seq_total(jnp.concatenate([first_part, second_part, scale_part, offset_part], axis=-1))
    first_sum, second_sum, scale_total, offset_total = jnp.split(
        sums, (GROUPS, 2 * GROUPS, 2 * GROUPS + channels), axis=-1
    )
    hidden_grad = norm_input_grad(
        second_dhat, second_hat, second_spread, valid_mask, counts, first_sum, second_sum
    )
    shift_low = jnp.concatenate([scale_total, offset_total], axis=-1).astype(jnp.bfloat16)
    first_seq = seq_index == 0
    time_weight_grad = jnp.where(
        first_seq,
        jnp.einsum("ie,ik->ek", time_input, shift_low, preferred_element_type=jnp.float32),
        0.0,
    )
    time_bias_grad = jnp.where(first_seq, jnp.sum(shift_low, axis=0, dtype=jnp.float32), 0.0)
    embedding_grad = jnp.einsum(
        "ik,ek->ie", shift_low, time_weight, preferred_element_type=jnp.float32
    ) * silu_slope(embedding.astype(jnp.float32))
    hidden_low = (valid_mask * hidden_grad).astype(jnp.bfloat16)
    active1_grad, conv1_weight_grad, conv1_bias_grad = conv_backward(
        hidden_low, first_patch, conv1_weight
    )
    norm1_grad = valid_mask * active1_grad * silu_slope(first_norm)
    gn1_gain_grad = jnp.sum(norm1_grad * first_hat, axis=(0, 1, 2))
    gn1_bias_grad = jnp.sum(norm1_grad, axis=(0, 1, 2))
    first_dhat = norm1_grad * gn1_gain
    first_part, second_part = group_parts(first_dhat, first_hat)
    first_sum, second_sum = group_totals(first_part, second_part)
    input_grad = residual_grad + norm_input_grad(
        first_dhat, first_hat, first_spread, valid_mask, counts, first_sum, second_sum
    )
    image_grad = (valid_mask * input_grad).astype(jnp.bfloat16)
    summed = lax.psum(
        (
            gn1_gain_grad,
            gn1_bias_grad,
            conv1_weight_grad,
            conv1_bias_grad,
            time_weight_grad,
            time_bias_grad,
            gn2_gain_grad,
            gn2_bias_grad,
            conv2_weight_grad,
            conv2_bias_grad,
            gn3_gain_grad,
            gn3_bias_grad,
            qkv_weight_grad,
            qv_bias_grad,
            proj_weight_grad,
            proj_bias_grad,
        ),
        ("dp", "seq"),
    )
    return (output, image_grad, embedding_grad) + tuple(summed)


def solution(mesh):
    return jax.shard_map(
        per_device,
        mesh=mesh,
        in_specs=(
            P("dp", "seq", None, None),
            P("dp", None),
            P("dp", "seq", None, None),
            P("dp"),
            P("dp"),
            P(),
            P(),
            P(),
            P(),
            P(),
            P(),
            P(),
            P(),
            P(),
            P(),
            P(),
            P(),
            P(),
            P(),
            P(),
            P(),
        ),
        out_specs=(
            P("dp", "seq", None, None),
            P("dp", "seq", None, None),
            P("dp", None),
            P(),
            P(),
            P(),
            P(),
            P(),
            P(),
            P(),
            P(),
            P(),
            P(),
            P(),
            P(),
            P(),
            P(),
            P(),
            P(),
        ),
        check_vma=False,
    )
```

```python
import functools

import jax
import jax.numpy as jnp
from jax import lax
from jax.experimental import pallas as pl
from jax.experimental.pallas import tpu as pltpu
from jax.sharding import PartitionSpec as P

GROUPS = 32
HEAD_COUNT = 4


EPS = 1e-05
LOWEST = -1e30
LOG2E = 1.4426950408889634

LEFT = 24


def seq_shift(value, dx, dy, dc):
    pairs = []
    for place in range(32):
        x, y, c = place // 8, place // 2 % 4, place % 2
        pairs.append((place, (x + dx) % 4 * 8 + (y + dy) % 4 * 2 + (c + dc) % 2))
    return lax.ppermute(value, "seq", pairs)


def axis_shift(value, axis, step):
    if axis == "x":
        return seq_shift(value, step, 0, 0)
    if axis == "y":
        return seq_shift(value, 0, step, 0)
    return lax.ppermute(value, "dp", [(i, (i + step) % 4) for i in range(4)])


def ring_total(value, axis):
    return (value + axis_shift(value, axis, 2)) + (
        axis_shift(value, axis, 1) + axis_shift(value, axis, 3)
    )


def seq_total(value):
    value = value + seq_shift(value, 0, 0, 1)
    return ring_total(ring_total(value, "y"), "x")


def low_total(value, axis):
    wide = [value.astype(jnp.float32)] + [
        axis_shift(value, axis, step).astype(jnp.float32) for step in (1, 2, 3)
    ]
    return ((wide[0] + wide[2]) + (wide[1] + wide[3])).astype(value.dtype)


def take_slot(value, slot):
    return lax.dynamic_index_in_dim(value, slot, 0, keepdims=False)


def low_sum(*parts):
    total = parts[0].astype(jnp.float32)
    for part in parts[1:]:
        total = total + part.astype(jnp.float32)
    return total.astype(jnp.bfloat16)


def scatter_core(value, c):
    return low_sum(take_slot(value, c), seq_shift(take_slot(value, 1 - c), 0, 0, 1))


def scatter_ring(value, axis, place):
    return low_sum(
        take_slot(value, place),
        *(axis_shift(take_slot(value, (place + step) % 4), axis, step) for step in (1, 3, 2)),
    )


def gather_ring(value, axis, place):
    result = jnp.zeros((4,) + value.shape, value.dtype)
    result = lax.dynamic_update_index_in_dim(result, value, place, 0)
    for step in (1, 3, 2):
        result = lax.dynamic_update_index_in_dim(
            result, axis_shift(value, axis, step), (place - step) % 4, 0
        )
    return result


def gather_core(value, c):
    other = seq_shift(value, 0, 0, 1)
    return jnp.where(c == 0, jnp.stack([value, other]), jnp.stack([other, value]))


def all_total(value, places, first, second):
    rows, width = value.shape
    value = scatter_core(value.reshape(2, -1, width), places["c"])
    value = scatter_ring(value.reshape(4, -1, width), first, places[first])
    value = scatter_ring(value.reshape(4, -1, width), second, places[second])
    value = low_total(value, "z")
    value = gather_ring(value, second, places[second]).reshape(-1, width)
    value = gather_ring(value, first, places[first]).reshape(-1, width)
    return gather_core(value, places["c"]).reshape(rows, width)


def padded_2(block, sides, width):
    for axis, dim in sides:
        count = lax.axis_size(axis)
        forward = [(i, i + 1) for i in range(count - 1)]
        backward = [(target, source) for source, target in forward]
        low = lax.ppermute(
            lax.slice_in_dim(block, block.shape[dim] - width, None, axis=dim), axis, forward
        )
        high = lax.ppermute(lax.slice_in_dim(block, 0, width, axis=dim), axis, backward)
        block = jnp.concatenate([low, block, high], axis=dim)
    return block


def silu_slope(values):
    sigmoid = jax.nn.sigmoid(values)
    return sigmoid * (1.0 + values * (1.0 - sigmoid))


def by_group(values):
    return values.reshape(values.shape[0], -1, GROUPS, values.shape[-1] // GROUPS)


def group_totals(first_part, second_part):
    both = seq_total(jnp.concatenate([first_part, second_part], axis=-1))
    return both[:, :GROUPS], both[:, GROUPS:]


def group_parts(values, normed):
    return (jnp.sum(by_group(values), axis=(1, 3)), jnp.sum(by_group(values * normed), axis=(1, 3)))


def norm_forward(values, valid_mask, counts):
    grouped = by_group(values)
    first_sum, second_sum = group_totals(
        jnp.sum(grouped, axis=(1, 3)), jnp.sum(grouped * grouped, axis=(1, 3))
    )
    average = first_sum / counts[:, None]
    spread = lax.rsqrt(second_sum / counts[:, None] - average * average + EPS)
    normed = (grouped - average[:, None, :, None]) * spread[:, None, :, None]
    return (valid_mask * normed.reshape(values.shape), spread)


def norm_input_grad(grad_hat, normed, spread, valid_mask, counts, first_sum, second_sum):
    first_mean = (first_sum / counts[:, None])[:, None, :, None]
    second_mean = (second_sum / counts[:, None])[:, None, :, None]
    result = spread[:, None, :, None] * (
        by_group(grad_hat) - first_mean - by_group(normed) * second_mean
    )
    return valid_mask * result.reshape(grad_hat.shape)


def patches(padded, shard_rows, columns):
    widened = jnp.pad(padded, ((0, 0), (0, 0), (1, 1), (0, 0)))
    return jnp.concatenate(
        [
            widened[:, row_off : row_off + shard_rows, col_off : col_off + columns, :]
            for row_off in range(3)
            for col_off in range(3)
        ],
        axis=-1,
    )


def conv_forward(active, weight):
    padded = padded_2(active, (("seq", 1),), 1)
    gathered = patches(padded, active.shape[1], active.shape[2])
    flat_weight = weight.reshape(-1, weight.shape[-1])
    return (jnp.dot(gathered, flat_weight, preferred_element_type=jnp.float32), gathered)


def conv_backward(grad_low, gathered, weight):
    weight_grad = jnp.einsum(
        "nrwk,nrwo->ko", gathered, grad_low, preferred_element_type=jnp.float32
    )
    bias_grad = jnp.sum(grad_low, axis=(0, 1, 2), dtype=jnp.float32)
    padded = padded_2(grad_low, (("seq", 1),), 1)
    flipped = jnp.transpose(weight[::-1, ::-1], (0, 1, 3, 2)).reshape(-1, weight.shape[-1])
    input_grad = jnp.dot(
        patches(padded, grad_low.shape[1], grad_low.shape[2]),
        flipped,
        preferred_element_type=jnp.float32,
    )
    return (input_grad, weight_grad, bias_grad)


def to_parts(values):
    images, shard_rows, columns, channels = values.shape
    return jnp.concatenate(
        [
            values[:, :, :LEFT].reshape(images, -1, channels),
            values[:, :, LEFT:].reshape(images, -1, channels),
        ],
        axis=1,
    )


def from_parts(values, shard_rows, columns):
    images, tokens, channels = values.shape
    edge = shard_rows * LEFT
    return jnp.concatenate(
        [
            values[:, :edge].reshape(images, shard_rows, LEFT, channels),
            values[:, edge:].reshape(images, shard_rows, columns - LEFT, channels),
        ],
        axis=2,
    )


def attention_kernel(pieces, block, plan_ref, qg_ref, *refs):
    kv_refs = refs[:pieces]
    rows_ref, dkv_refs = refs[pieces], refs[pieces + 1 : pieces + 3]
    kv_ref, bias_ref, kvt_ref, qgs_ref, s_ref, p_ref, acc_ref = refs[pieces + 3 :]
    tokens, width = qg_ref.shape[1:]
    half = width // 2
    whole = 8 * tokens
    edge = tokens * LEFT // 40
    left = 8 * edge
    place = plan_ref[0]
    valid_rows = plan_ref[1]
    sizes = ((whole, plan_ref[2]), (left, plan_ref[3]))
    scale = half ** (-0.5)
    pair = block // 2

    def slot_of(part):
        return lax.rem(place - part + 4, 4)

    def rows_of(chunk, size):
        return pl.ds(pl.multiple_of(slot_of(chunk) * whole, whole), size)

    def spans(slot, which):
        return (
            (0, edge, pl.ds(pl.multiple_of(slot * whole + which * edge, 16), edge)),
            (
                edge,
                tokens,
                pl.ds(
                    pl.multiple_of(slot * whole + left + which * (tokens - edge), 16),
                    tokens - edge,
                ),
            ),
        )

    number = 0
    for ref in kv_refs:
        for piece in range(ref.shape[0]):
            which = plan_ref[4 + number]
            number += 1
            for slot in range(4):
                for low, high, span in spans(slot, which):
                    kv_ref[span, :] = ref[piece, slot, low:high, :]
    token_ids = lax.broadcasted_iota(jnp.int32, (whole, width), 0)
    for slot in range(4):
        span = slice(slot * whole, (slot + 1) * whole)
        kvt_ref[:, span] = kv_ref[span, :].T
        acc_ref[span, :] = jnp.zeros((whole, width), jnp.float32)
        room = valid_rows - slot_of(slot) * (whole // 40)
        bound = jnp.where(token_ids < left, room * LEFT, left + room * (40 - LEFT))
        bias_ref[span, :] = jnp.where(token_ids < bound, 0.0, LOWEST).astype(jnp.bfloat16)
    for part in range(4):
        qgs_ref[part * pair : part * pair + tokens, :] = qg_ref[slot_of(part)]
        qgs_ref[part * pair + tokens : (part + 1) * pair, :] = jnp.zeros(
            (pair - tokens, width), jnp.bfloat16
        )
    rows_ref[...] = jnp.zeros(rows_ref.shape, jnp.bfloat16)

    lane = lax.broadcasted_iota(jnp.int32, (block, width), 1)
    ones = (lax.broadcasted_iota(jnp.int32, (width, block), 0) == 0).astype(jnp.bfloat16)
    zeros = jnp.zeros((half, block), jnp.bfloat16)

    def query_block(number, _):
        qg = qgs_ref[pl.ds(pl.multiple_of(number * block, block), block), :]
        qgt = qg.T
        grad_t = qgt[half:] * jnp.bfloat16(scale)
        score_rhs = jnp.concatenate([qgt[:half], zeros, ones], axis=0)
        grad_rhs = jnp.concatenate([zeros, grad_t], axis=0)
        blank = jnp.zeros_like(qg)
        out_rhs = jnp.concatenate(
            [jnp.where(lane < half, qg, blank), jnp.where(lane < half, blank, qg)], axis=0
        )

        def score_pass(size, chunk, best):
            rows = rows_of(chunk, size)
            lhs = jnp.concatenate([kv_ref[rows, :], bias_ref[rows, :]], axis=1)
            scores = jnp.dot(lhs, score_rhs, preferred_element_type=jnp.float32)
            s_ref[rows, :] = scores
            return jnp.maximum(best, jnp.max(scores.reshape(size // 8, 8, block), axis=0))

        best = jnp.full((8, block), LOWEST, jnp.float32)
        for size, trips in sizes:
            best = lax.fori_loop(0, trips, functools.partial(score_pass, size), best)
        peak = jnp.max(best, axis=0, keepdims=True) * (scale * LOG2E)

        def weight_pass(size, chunk, carried):
            total, out_t = carried
            rows = rows_of(chunk, size)
            weights = jnp.exp2(s_ref[rows, :] * (scale * LOG2E) - peak)
            total = total + jnp.sum(weights.reshape(size // 8, 8, block), axis=0)
            weights = weights.astype(jnp.bfloat16)
            p_ref[rows, :] = weights
            out_t = out_t + jnp.dot(
                kvt_ref[half:, rows], weights, preferred_element_type=jnp.float32
            )
            return total, out_t

        carried = (jnp.zeros((8, block), jnp.float32), jnp.zeros((half, block), jnp.float32))
        for size, trips in sizes:
            carried = lax.fori_loop(0, trips, functools.partial(weight_pass, size), carried)
        total, out_t = carried
        inverse = 1.0 / jnp.sum(total, axis=0, keepdims=True)
        out_t = out_t * inverse
        delta = jnp.sum(out_t * grad_t.astype(jnp.float32), axis=0, keepdims=True)

        def grad_pass(size, chunk, dq_t):
            rows = rows_of(chunk, size)
            prob_grad = jnp.dot(kv_ref[rows, :], grad_rhs, preferred_element_type=jnp.float32)
            probs = p_ref[rows, :].astype(jnp.float32) * inverse
            score_grad = (probs * (prob_grad - delta)).astype(jnp.bfloat16)
            acc_ref[rows, :] += jnp.dot(
                jnp.concatenate([score_grad, probs.astype(jnp.bfloat16)], axis=1),
                out_rhs,
                preferred_element_type=jnp.float32,
            )
            return dq_t + jnp.dot(
                kvt_ref[:half, rows], score_grad, preferred_element_type=jnp.float32
            )

        dq_t = jnp.zeros((half, block), jnp.float32)
        for size, trips in sizes:
            dq_t = lax.fori_loop(0, trips, functools.partial(grad_pass, size), dq_t)
        result = jnp.concatenate([dq_t, out_t], axis=0).T.astype(jnp.bfloat16)
        rows_ref[slot_of(2 * number)] = result[:tokens]
        rows_ref[slot_of(2 * number + 1)] = result[pair : pair + tokens]
        return 0

    lax.fori_loop(0, jnp.where(plan_ref[2] + plan_ref[3] > 2, 2, 1), query_block, 0)
    number = 0
    for ref in dkv_refs:
        for piece in range(ref.shape[0]):
            which = plan_ref[12 + number]
            number += 1
            for slot in range(4):
                for low, high, span in spans(slot, which):
                    ref[piece, slot, low:high, :] = acc_ref[span, :].astype(jnp.bfloat16)


def attend(plan, qg, *kvs):
    slots, tokens, width = qg.shape
    keys = 8 * slots * tokens
    block = 512
    vmem = pl.BlockSpec(memory_space=pltpu.VMEM)
    half_keys = jax.ShapeDtypeStruct((4, slots, tokens, width), jnp.bfloat16)
    return pl.pallas_call(
        functools.partial(attention_kernel, len(kvs), block),
        out_shape=(jax.ShapeDtypeStruct(qg.shape, jnp.bfloat16), half_keys, half_keys),
        in_specs=[pl.BlockSpec(memory_space=pltpu.SMEM)] + [vmem] * (1 + len(kvs)),
        out_specs=(vmem, vmem, vmem),
        scratch_shapes=[
            pltpu.VMEM((keys, width), jnp.bfloat16),
            pltpu.VMEM((keys, width), jnp.bfloat16),
            pltpu.VMEM((width, keys), jnp.bfloat16),
            pltpu.VMEM((2 * block, width), jnp.bfloat16),
            pltpu.VMEM((keys, block), jnp.float32),
            pltpu.VMEM((keys, block), jnp.bfloat16),
            pltpu.VMEM((keys, width), jnp.float32),
        ],
        compiler_params=pltpu.CompilerParams(vmem_limit_bytes=52 * 2**20),
        cost_estimate=pl.CostEstimate(
            flops=6 * 2 * 1024 * keys * 256,
            bytes_accessed=8 * 2**20,
            transcendentals=1024 * keys,
        ),
        name="attention",
    )(plan, qg, *kvs)


def per_device(
    image,
    embedding,
    cotangent,
    valid_rows,
    orientation,
    gn1_gain,
    gn1_bias,
    conv1_weight,
    conv1_bias,
    time_weight,
    time_bias,
    gn2_gain,
    gn2_bias,
    conv2_weight,
    conv2_bias,
    gn3_gain,
    gn3_bias,
    qkv_weight,
    qv_bias,
    proj_weight,
    proj_bias,
):
    images, shard_rows, columns, channels = image.shape
    tokens = shard_rows * columns
    head_width = channels // HEAD_COUNT
    seq_index = lax.axis_index("seq")
    dp_index = lax.axis_index("dp")
    places = {"x": seq_index // 8, "y": seq_index // 2 % 4, "c": seq_index % 2, "z": dp_index}
    place_x, place_y, place_c = places["x"], places["y"], places["c"]
    row_ids = seq_index * shard_rows + jnp.arange(shard_rows, dtype=jnp.int32)
    col_valid = columns - 2 * columns // 5 * orientation
    pixel_ok = (row_ids[None, :, None] < valid_rows[:, None, None]) & (
        jnp.arange(columns, dtype=jnp.int32)[None, None, :] < col_valid[:, None, None]
    )
    valid_mask = pixel_ok.astype(jnp.float32)[..., None]
    counts = (valid_rows * col_valid).astype(jnp.float32) * (channels // GROUPS)

    def heads_first(weight, parts):
        rows = weight.shape[0]
        heads = jnp.transpose(
            weight.reshape(rows, parts, HEAD_COUNT, head_width), (2, 0, 1, 3)
        ).reshape(HEAD_COUNT, rows, parts * head_width)
        return to_slots(heads)

    def to_slots(heads):
        return lax.dynamic_slice_in_dim(
            jnp.concatenate([heads, heads], axis=0), place_x, HEAD_COUNT, axis=0
        )

    def to_heads(slots):
        return lax.dynamic_slice_in_dim(
            jnp.concatenate([slots, slots], axis=0),
            (HEAD_COUNT - place_x) % HEAD_COUNT,
            HEAD_COUNT,
            axis=0,
        )

    slot_qkv = heads_first(qkv_weight, 3)
    bias_all = jnp.concatenate([qv_bias[:channels], jnp.zeros((channels,), jnp.float32), qv_bias[channels:]])
    slot_bias = heads_first(bias_all[None], 3)
    slot_proj = to_slots(proj_weight.reshape(HEAD_COUNT, head_width, channels))

    cotan_full = cotangent.astype(jnp.float32)
    proj_grad = to_parts((valid_mask * cotan_full).astype(jnp.bfloat16))
    slot_grad = jnp.einsum(
        "itc,dhc->dith", proj_grad, slot_proj, preferred_element_type=jnp.float32
    ).astype(jnp.bfloat16)
    grad_heads = jnp.stack(
        [slot_grad[0]] + [seq_shift(slot_grad[d], d, 0, 0) for d in range(1, 4)]
    )

    masked_input = valid_mask * image.astype(jnp.float32)
    first_hat, first_spread = norm_forward(masked_input, valid_mask, counts)
    first_norm = valid_mask * (first_hat * gn1_gain + gn1_bias)
    first_active = jax.nn.silu(first_norm).astype(jnp.bfloat16)
    first_conv, first_patch = conv_forward(first_active, conv1_weight)
    hidden = valid_mask * (first_conv + conv1_bias)
    hidden, grad_heads = lax.optimization_barrier((hidden, grad_heads))
    time_input = jax.nn.silu(embedding.astype(jnp.float32)).astype(jnp.bfloat16)
    shifts = jnp.dot(time_input, time_weight, preferred_element_type=jnp.float32) + time_bias
    scaling = shifts[:, None, None, :channels]
    offset = shifts[:, None, None, channels:]
    second_hat, second_spread = norm_forward(hidden, valid_mask, counts)
    second_base = valid_mask * (second_hat * gn2_gain + gn2_bias)
    second_norm = valid_mask * (second_base * (1.0 + scaling) + offset)
    second_active = jax.nn.silu(second_norm).astype(jnp.bfloat16)
    second_conv, second_patch = conv_forward(second_active, conv2_weight)
    residual = masked_input + valid_mask * (second_conv + conv2_bias)
    third_hat, third_spread = norm_forward(residual, valid_mask, counts)
    third_low = to_parts(
        (valid_mask * (third_hat * gn3_gain + gn3_bias)).astype(jnp.bfloat16)
    )

    slot_mix = (
        jnp.einsum("itc,dck->ditk", third_low, slot_qkv, preferred_element_type=jnp.float32)
        + slot_bias[:, None]
    ).astype(jnp.bfloat16)
    mix = jnp.stack([slot_mix[0]] + [seq_shift(slot_mix[d], d, 0, 0) for d in range(1, 4)])
    qg = jnp.concatenate([mix[..., :head_width], grad_heads], axis=-1)
    key_values = mix[..., head_width:]

    trips = (valid_rows + 47) // 48
    own_first = [
        2 * ((place_y + step) % 4) + (place_c if same else 1 - place_c)
        for same in (True, False)
        for step in range(4)
    ]
    as_gathered = [
        2 * ((place_y + step) % 4) + (place_c if same else 1 - place_c)
        for same in (True, False)
        for step in (0, 3, 1, 2)
    ]

    def plan_of(which, key_order, grad_order):
        whole = jnp.where(orientation[which] == 0, trips[which], 0)
        left = jnp.where(orientation[which] == 0, 0, trips[which])
        numbers = [place_x, valid_rows[which], whole, left] + key_order + grad_order
        return jnp.stack([jnp.asarray(n, jnp.int32) for n in numbers])

    groups = [[x * 8 + place for place in range(8)] for x in range(4)]
    own_a = key_values[:, 0]
    gathered_b = lax.all_gather(key_values[:, 1], "seq", axis_index_groups=groups)
    up = seq_shift(own_a, 0, 1, 0)
    down = seq_shift(own_a, 0, 3, 0)
    far = jnp.concatenate([seq_shift(up[:2], 0, 1, 0), seq_shift(down[2:], 0, 3, 0)])
    column = jnp.stack([own_a, up, down, far])
    beside = seq_shift(column, 0, 0, 1)
    rows_a, *dkv_a = attend(
        plan_of(0, as_gathered, list(range(8))), qg[:, 0], column, beside
    )
    scattered_a = lax.psum_scatter(
        jnp.concatenate(dkv_a), "seq", scatter_dimension=0, axis_index_groups=groups
    )
    rows_b, own_b, beside_b = attend(
        plan_of(1, list(range(8)), own_first), qg[:, 1], gathered_b
    )

    rows_ab = jnp.stack([rows_a, rows_b], axis=1)
    back = jnp.stack([rows_ab[0]] + [seq_shift(rows_ab[d], 4 - d, 0, 0) for d in range(1, 4)])
    slot_query_grad = back[..., :head_width]
    slot_attended = back[..., head_width:]

    column_b = low_sum(own_b, seq_shift(beside_b, 0, 0, 1))
    scattered_b = low_sum(
        column_b[0], *(seq_shift(column_b[step], 0, step, 0) for step in (1, 3, 2))
    )
    dkv_ab = jnp.stack([scattered_a, scattered_b], axis=1)
    slot_kv_grad = jnp.stack([dkv_ab[0]] + [seq_shift(dkv_ab[d], 4 - d, 0, 0) for d in range(1, 4)])

    projected = (
        jnp.einsum("dith,dhc->itc", slot_attended, slot_proj, preferred_element_type=jnp.float32)
        + proj_bias
    )
    output = (residual + valid_mask * from_parts(projected, shard_rows, columns)).astype(
        jnp.bfloat16
    )
    proj_weight_grad = to_heads(
        jnp.einsum("dith,itc->dhc", slot_attended, proj_grad, preferred_element_type=jnp.float32)
    ).reshape(channels, channels)
    proj_bias_grad = jnp.sum(proj_grad, axis=(0, 1), dtype=jnp.float32)

    slot_mix_grad = jnp.concatenate([slot_query_grad, slot_kv_grad], axis=-1)
    third_grad = from_parts(
        jnp.einsum("ditk,dck->itc", slot_mix_grad, slot_qkv, preferred_element_type=jnp.float32),
        shard_rows,
        columns,
    )
    qkv_weight_grad = to_heads(
        jnp.einsum("itc,ditk->dck", third_low, slot_mix_grad, preferred_element_type=jnp.float32)
    )
    qkv_weight_grad = jnp.transpose(
        qkv_weight_grad.reshape(HEAD_COUNT, channels, 3, head_width), (1, 2, 0, 3)
    ).reshape(channels, 3 * channels)
    mix_sums = to_heads(jnp.sum(slot_mix_grad, axis=(1, 2), dtype=jnp.float32))
    qv_bias_grad = jnp.concatenate(
        [
            mix_sums[:, :head_width].reshape(-1),
            mix_sums[:, 2 * head_width :].reshape(-1),
        ]
    )
    third_up = valid_mask * third_grad
    gn3_gain_grad = jnp.sum(third_up * third_hat, axis=(0, 1, 2))
    gn3_bias_grad = jnp.sum(third_up, axis=(0, 1, 2))
    third_dhat = third_up * gn3_gain
    first_part, second_part = group_parts(third_dhat, third_hat)
    first_sum, second_sum = group_totals(first_part, second_part)
    residual_grad = cotan_full + norm_input_grad(
        third_dhat, third_hat, third_spread, valid_mask, counts, first_sum, second_sum
    )
    branch_low = (valid_mask * residual_grad).astype(jnp.bfloat16)
    active2_grad, conv2_weight_grad, conv2_bias_grad = conv_backward(
        branch_low, second_patch, conv2_weight
    )
    early = jnp.concatenate(
        [conv2_weight_grad, qkv_weight_grad.reshape(-1, channels), proj_weight_grad]
    ).astype(jnp.bfloat16)
    early = lax.psum_scatter(
        early.reshape(8, -1, channels), "seq", scatter_dimension=0, axis_index_groups=groups
    )
    early = scatter_ring(early.reshape(4, -1, channels), "x", place_x)
    early = gather_ring(low_total(early, "z"), "x", place_x).reshape(-1, channels)
    early = (
        lax.all_gather(early, "seq", axis_index_groups=groups)
        .reshape(-1, channels)
        .astype(jnp.float32)
    )

    norm2_grad = valid_mask * active2_grad * silu_slope(second_norm)
    scale_part = jnp.sum(norm2_grad * second_base, axis=(1, 2))
    offset_part = jnp.sum(norm2_grad, axis=(1, 2))
    base_grad = norm2_grad * (1.0 + scaling)
    gn2_gain_grad = jnp.sum(base_grad * second_hat, axis=(0, 1, 2))
    gn2_bias_grad = jnp.sum(base_grad, axis=(0, 1, 2))
    second_dhat = base_grad * gn2_gain
    first_part, second_part = group_parts(second_dhat, second_hat)
    sums = seq_total(jnp.concatenate([first_part, second_part, scale_part, offset_part], axis=-1))
    first_sum, second_sum, scale_total, offset_total = jnp.split(
        sums, (GROUPS, 2 * GROUPS, 2 * GROUPS + channels), axis=-1
    )
    hidden_grad = norm_input_grad(
        second_dhat, second_hat, second_spread, valid_mask, counts, first_sum, second_sum
    )
    hidden_low = (valid_mask * hidden_grad).astype(jnp.bfloat16)
    active1_grad, conv1_weight_grad, conv1_bias_grad = conv_backward(
        hidden_low, first_patch, conv1_weight
    )
    late = all_total(conv1_weight_grad.astype(jnp.bfloat16), places, "x", "y").astype(jnp.float32)

    shift_low = jnp.concatenate([scale_total, offset_total], axis=-1).astype(jnp.bfloat16)
    time_pair = gather_ring(jnp.concatenate([time_input, shift_low], axis=-1), "z", dp_index)
    time_pair = time_pair.reshape(-1, time_pair.shape[-1])
    every_input, every_shift = jnp.split(time_pair, (time_input.shape[-1],), axis=-1)
    time_weight_grad = jnp.einsum(
        "ie,ik->ek", every_input, every_shift, preferred_element_type=jnp.float32
    )
    time_bias_grad = jnp.sum(every_shift, axis=0, dtype=jnp.float32)
    embedding_grad = jnp.einsum(
        "ik,ek->ie", shift_low, time_weight, preferred_element_type=jnp.float32
    ) * silu_slope(embedding.astype(jnp.float32))

    norm1_grad = valid_mask * active1_grad * silu_slope(first_norm)
    gn1_gain_grad = jnp.sum(norm1_grad * first_hat, axis=(0, 1, 2))
    gn1_bias_grad = jnp.sum(norm1_grad, axis=(0, 1, 2))
    first_dhat = norm1_grad * gn1_gain
    first_part, second_part = group_parts(first_dhat, first_hat)
    small = (
        gn1_gain_grad,
        gn1_bias_grad,
        conv1_bias_grad,
        gn2_gain_grad,
        gn2_bias_grad,
        conv2_bias_grad,
        gn3_gain_grad,
        gn3_bias_grad,
        qv_bias_grad,
        proj_bias_grad,
    )
    cuts = []
    for part in (first_part.reshape(-1), second_part.reshape(-1)) + small[:-1]:
        cuts.append((cuts[-1] if cuts else 0) + part.size)
    sums = seq_total(
        jnp.concatenate([first_part.reshape(-1), second_part.reshape(-1)] + list(small))
    )
    first_sum, second_sum = (
        part.reshape(first_part.shape) for part in jnp.split(sums[: cuts[1]], 2)
    )
    sums = ring_total(sums, "z")
    small = jnp.split(sums, cuts)[2:]
    input_grad = residual_grad + norm_input_grad(
        first_dhat, first_hat, first_spread, valid_mask, counts, first_sum, second_sum
    )
    image_grad = (valid_mask * input_grad).astype(jnp.bfloat16)
    taps = conv1_weight.shape
    patch_rows = conv2_weight_grad.shape[0]
    return (
        output,
        image_grad,
        embedding_grad,
        small[0],
        small[1],
        late.reshape(taps),
        small[2],
        time_weight_grad,
        time_bias_grad,
        small[3],
        small[4],
        early[:patch_rows].reshape(taps),
        small[5],
        small[6],
        small[7],
        early[patch_rows:-channels].reshape(channels, 3 * channels),
        small[8],
        early[-channels:],
        small[9],
    )


def solution(mesh):
    return jax.shard_map(
        per_device,
        mesh=mesh,
        in_specs=(
            P("dp", "seq", None, None),
            P("dp", None),
            P("dp", "seq", None, None),
            P("dp"),
            P("dp"),
            P(),
            P(),
            P(),
            P(),
            P(),
            P(),
            P(),
            P(),
            P(),
            P(),
            P(),
            P(),
            P(),
            P(),
            P(),
            P(),
        ),
        out_specs=(
            P("dp", "seq", None, None),
            P("dp", "seq", None, None),
            P("dp", None),
            P(),
            P(),
            P(),
            P(),
            P(),
            P(),
            P(),
            P(),
            P(),
            P(),
            P(),
            P(),
            P(),
            P(),
            P(),
            P(),
        ),
        check_vma=False,
    )
```

```python
import functools

import jax
import jax.numpy as jnp
from jax import lax
from jax.experimental import pallas as pl
from jax.experimental.pallas import tpu as pltpu
from jax.sharding import PartitionSpec as P

GROUPS = 32
HEAD_COUNT = 4


EPS = 1e-05
LOWEST = -1e30
LOG2E = 1.4426950408889634

LEFT = 24


def seq_shift(value, dx, dy, dc):
    pairs = []
    for place in range(32):
        x, y, c = place // 8, place // 2 % 4, place % 2
        pairs.append((place, (x + dx) % 4 * 8 + (y + dy) % 4 * 2 + (c + dc) % 2))
    return lax.ppermute(value, "seq", pairs)


def axis_shift(value, axis, step):
    if axis == "x":
        return seq_shift(value, step, 0, 0)
    if axis == "y":
        return seq_shift(value, 0, step, 0)
    return lax.ppermute(value, "dp", [(i, (i + step) % 4) for i in range(4)])


def row_shift(value, step):
    return lax.ppermute(value, "seq", [(i, (i + step) % 32) for i in range(32)])


def seq_total(value):
    value = value + seq_shift(value, 0, 0, 1)
    groups = [[place * 2 + core for place in range(16)] for core in range(2)]
    copies = jnp.broadcast_to(value[None], (16,) + value.shape)
    return jnp.sum(lax.all_to_all(copies, "seq", 0, 0, axis_index_groups=groups), axis=0)


def take_slot(value, slot):
    return lax.dynamic_index_in_dim(value, slot, 0, keepdims=False)


def low_sum(*parts):
    total = parts[0].astype(jnp.float32)
    for part in parts[1:]:
        total = total + part.astype(jnp.float32)
    return total.astype(jnp.bfloat16)


def gather_ring(value, axis, place):
    result = jnp.zeros((4,) + value.shape, value.dtype)
    result = lax.dynamic_update_index_in_dim(result, value, place, 0)
    for step in (1, 3, 2):
        result = lax.dynamic_update_index_in_dim(
            result, axis_shift(value, axis, step), (place - step) % 4, 0
        )
    return result


def split_low(value):
    high = value.astype(jnp.bfloat16)
    return jnp.concatenate([high, (value - high.astype(jnp.float32)).astype(jnp.bfloat16)])


def join_low(value):
    high, rest = jnp.split(value.astype(jnp.float32), 2)
    return high + rest


def paired(parts):
    return (parts[0] + parts[2]) + (parts[1] + parts[3])


def exchange(slots, vector, axis, places):
    place = places[axis]
    low = split_low(vector)
    sent = [jnp.concatenate([take_slot(slots, (place + step) % 4), low]) for step in range(4)]
    got = [sent[0]] + [axis_shift(sent[step], axis, step) for step in (1, 2, 3)]
    count = slots.shape[1]
    chunk = paired([part[:count].astype(jnp.float32) for part in got]).astype(jnp.bfloat16)
    return chunk, paired([join_low(part[count:]) for part in got])


def sums_over_seq(late, early, vector, places):
    width = late.shape[-1]
    halves = late.reshape(2, -1, width)
    low = split_low(vector)
    got = seq_shift(
        jnp.concatenate([take_slot(halves, 1 - places["c"]), low]), 0, 0, 1
    )
    count = halves.shape[1]
    late = low_sum(take_slot(halves, places["c"]), got[:count])
    vector = join_low(low) + join_low(got[count:])
    late, vector = exchange(late.reshape(4, -1, width), vector, "y", places)
    both = jnp.concatenate([late.reshape(4, -1, width), early.reshape(4, -1, width)], axis=1)
    both, vector = exchange(both, vector, "x", places)
    return both, vector


def sums_over_dp(both, vector, extra, places):
    low = split_low(vector)
    sent = jnp.concatenate([both, low, extra])
    got = [sent] + [axis_shift(sent, "z", step) for step in (1, 2, 3)]
    count = both.shape[0]
    both = paired([part[:count].astype(jnp.float32) for part in got]).astype(jnp.bfloat16)
    count += low.shape[0]
    vector = paired([join_low(part[count - low.shape[0] : count]) for part in got])
    extras = jnp.zeros((4,) + extra.shape, extra.dtype)
    for step in range(4):
        extras = lax.dynamic_update_index_in_dim(
            extras, got[step][count:], (places["z"] - step) % 4, 0
        )
    return both, vector, extras


def gathered_over_seq(both, cut, places):
    width = both.shape[-1]
    both = gather_ring(both, "x", places["x"])
    both = jnp.concatenate([both[:, :cut].reshape(-1, width), both[:, cut:].reshape(-1, width)])
    both = gather_ring(both, "y", places["y"])
    late = both[:, : 4 * cut].reshape(-1, width)
    early = both[:, 4 * cut :].reshape(-1, width)
    return late, seq_shift(late, 0, 0, 1), early, seq_shift(early, 0, 0, 1)


def silu_slope(values):
    sigmoid = jax.nn.sigmoid(values)
    return sigmoid * (1.0 + values * (1.0 - sigmoid))


def same_group(channels):
    size = channels // GROUPS
    rows = lax.broadcasted_iota(jnp.int32, (channels, channels), 0) // size
    cols = lax.broadcasted_iota(jnp.int32, (channels, channels), 1) // size
    return (rows == cols).astype(jnp.float32)


def over_group(sums, channels):
    return jnp.dot(
        sums, same_group(channels), precision=lax.Precision.HIGHEST, preferred_element_type=jnp.float32
    )


def norm_terms(sums, counts_ref):
    totals = over_group(sums, sums.shape[-1])
    terms = []
    for i in range(2):
        average = totals[i : i + 1] / counts_ref[i]
        spread = lax.rsqrt(totals[2 + i : 3 + i] / counts_ref[i] - average * average + EPS)
        terms.append((average, spread))
    return terms


def mask_of(info_ref, i, shape, border):
    rows = lax.broadcasted_iota(jnp.int32, shape, 0) + (info_ref[0] - border)
    cols = lax.broadcasted_iota(jnp.int32, shape, 1)
    valid = (rows >= 0) & (rows < info_ref[1 + i]) & (cols < info_ref[3 + i])
    return valid.astype(jnp.float32)


def extended(low_ref, own_ref, high_ref, i):
    return jnp.concatenate([low_ref[i], own_ref[i], high_ref[i]], axis=0).astype(jnp.float32)


def shifted(values):
    rows, columns, channels = values.shape
    cols = lax.broadcasted_iota(jnp.int32, values.shape, 1).reshape(-1, channels)
    flat = values.reshape(-1, channels)
    before = jnp.where(cols == 0, 0.0, pltpu.roll(flat, 1, 0))
    after = jnp.where(cols == columns - 1, 0.0, pltpu.roll(flat, rows * columns - 1, 0))
    return before, flat, after


def tap_rows(images, a, b, rows, columns=40):
    return jnp.concatenate(
        [image[b][a * columns : (a + rows) * columns] for image in images], axis=0
    ).astype(jnp.bfloat16)


def conv_taps(images, weight_ref, rows):
    patches = jnp.concatenate(
        [tap_rows(images, a, b, rows) for a in range(3) for b in range(3)], axis=1
    )
    return jnp.dot(patches, weight_ref[...], preferred_element_type=jnp.float32)


def conv_grads(images, rows, actives, weight_ref, low, weight_grad_ref):
    total = None
    channels = low.shape[-1]
    for a in range(3):
        for b in range(3):
            span = slice((3 * a + b) * channels, (3 * a + b + 1) * channels)
            weight_grad_ref[span, :] = lax.dot_general(
                tap_rows(actives, a, b, 6),
                low,
                (((0,), (0,)), ((), ())),
                preferred_element_type=jnp.float32,
            ).astype(jnp.bfloat16)
            part = lax.dot_general(
                tap_rows(images, 2 - a, 2 - b, rows),
                weight_ref[span, :],
                (((1,), (1,)), ((), ())),
                preferred_element_type=jnp.float32,
            )
            total = part if total is None else total + part
    return total


def put_sums(ref, rows):
    ref[...] = jnp.zeros(ref.shape, jnp.float32)
    for place, row in enumerate(rows):
        ref[place : place + 1, :] = row


def column_sum(values):
    return jnp.sum(values.reshape(-1, values.shape[-1]), axis=0, keepdims=True)


def hidden_kernel(
    info_ref, counts_ref, low_ref, own_ref, high_ref, sums_ref, gain_ref, bias_ref, conv_bias_ref, weight_ref,
    active_ref, hidden_ref, out_sums_ref,
):
    terms = norm_terms(sums_ref[...], counts_ref)
    images = []
    for i in range(2):
        values = extended(low_ref, own_ref, high_ref, i)
        mask = mask_of(info_ref, i, values.shape, 2)
        average, spread = terms[i]
        hat = mask * ((mask * values - average) * spread)
        active = jax.nn.silu(mask * (hat * gain_ref[...] + bias_ref[...])).astype(jnp.bfloat16)
        active_ref[i] = active[1:-1]
        images.append(shifted(active.astype(jnp.float32)))
    conv = conv_taps(images, weight_ref, 8)
    first, second = [], []
    for i in range(2):
        shape = hidden_ref.shape[1:]
        mask = mask_of(info_ref, i, shape, 1)
        half = conv.shape[0] // 2
        hidden = mask * (conv[i * half : (i + 1) * half].reshape(shape) + conv_bias_ref[...])
        hidden_ref[i] = hidden
        hidden = hidden[1:-1]
        first.append(column_sum(hidden))
        second.append(column_sum(hidden * hidden))
    put_sums(out_sums_ref, first + second)


def second_norm_of(values, mask, term, gain, bias, shifts_ref, i):
    channels = values.shape[-1]
    average, spread = term
    hat = mask * ((values - average) * spread)
    base = mask * (hat * gain + bias)
    scaling = shifts_ref[i : i + 1, :channels]
    offset = shifts_ref[i : i + 1, channels:]
    return hat, mask * (base * (1.0 + scaling) + offset)


def residual_kernel(
    info_ref, counts_ref, hidden_ref, sums_ref, gain_ref, bias_ref, shifts_ref, conv_bias_ref, weight_ref, image_ref,
    active_ref, residual_ref, first_ref, last_ref, out_sums_ref,
):
    terms = norm_terms(sums_ref[...], counts_ref)
    images = []
    for i in range(2):
        values = hidden_ref[i]
        mask = mask_of(info_ref, i, values.shape, 1)
        _, norm = second_norm_of(
            values, mask, terms[i], gain_ref[...], bias_ref[...], shifts_ref, i
        )
        active = jax.nn.silu(norm).astype(jnp.bfloat16)
        active_ref[i] = active
        images.append(shifted(active.astype(jnp.float32)))
    conv = conv_taps(images, weight_ref, 6)
    first, second = [], []
    for i in range(2):
        shape = residual_ref.shape[1:]
        mask = mask_of(info_ref, i, shape, 0)
        half = conv.shape[0] // 2
        residual = mask * image_ref[i].astype(jnp.float32) + mask * (
            conv[i * half : (i + 1) * half].reshape(shape) + conv_bias_ref[...]
        )
        residual_ref[i] = residual
        first_ref[i] = residual[:2]
        last_ref[i] = residual[-2:]
        first.append(column_sum(residual))
        second.append(column_sum(residual * residual))
    put_sums(out_sums_ref, first + second)


def to_parts(values):
    channels = values.shape[-1]
    return jnp.concatenate(
        [values[:, :LEFT].reshape(-1, channels), values[:, LEFT:].reshape(-1, channels)], axis=0
    )


def from_parts(values, shape):
    rows, columns, channels = shape
    edge = rows * LEFT
    return jnp.concatenate(
        [
            values[:edge].reshape(rows, LEFT, channels),
            values[edge:].reshape(rows, columns - LEFT, channels),
        ],
        axis=1,
    )


def mixture_kernel(
    info_ref, counts_ref, residual_ref, cotangent_ref, sums_ref, gain_ref, bias_ref, key_weight_ref,
    query_weight_ref, key_bias_ref, query_bias_ref, third_ref, grad_ref, *slot_refs,
):
    terms = norm_terms(sums_ref[...], counts_ref)
    tokens = third_ref.shape[0] // 2
    for i in range(2):
        values = residual_ref[i]
        mask = mask_of(info_ref, i, values.shape, 0)
        average, spread = terms[i]
        hat = mask * ((values - average) * spread)
        span = slice(i * tokens, (i + 1) * tokens)
        third_ref[span, :] = to_parts(mask * (hat * gain_ref[...] + bias_ref[...])).astype(
            jnp.bfloat16
        )
        grad_ref[span, :] = to_parts(mask * cotangent_ref[i].astype(jnp.float32)).astype(
            jnp.bfloat16
        )
    third = third_ref[...]
    both = jnp.concatenate([third, grad_ref[...]], axis=1)
    for slot, ref in enumerate(slot_refs):
        head = lax.rem(info_ref[5] + slot, HEAD_COUNT)
        keys = (
            jnp.dot(third, key_weight_ref[head], preferred_element_type=jnp.float32)
            + key_bias_ref[head]
        ).astype(jnp.bfloat16)
        queries = (
            jnp.dot(both, query_weight_ref[head], preferred_element_type=jnp.float32)
            + query_bias_ref[head]
        ).astype(jnp.bfloat16)
        for i in range(2):
            span = slice(i * tokens, (i + 1) * tokens)
            ref[i, :tokens, :] = keys[span]
            ref[i, tokens:, :] = queries[span]


def output_kernel(
    info_ref, counts_ref, residual_ref, sums_ref, gain_ref, third_ref, grad_ref, query_weight_ref, key_weight_ref,
    proj_weight_ref, proj_bias_ref, *refs,
):
    row_refs, key_refs = refs[:4], refs[4:8]
    output_ref, third_grad_ref, first_ref, last_ref, out_sums_ref, early_ref, columns_ref = refs[8:]
    tokens, channels = third_ref.shape
    width = channels // 2
    head_width = channels // HEAD_COUNT
    third = third_ref[...]
    proj_grad = grad_ref[...]
    ones = jnp.ones((tokens, width), jnp.bfloat16)
    row_rhs = jnp.concatenate([third, proj_grad, ones], axis=1)
    key_rhs = jnp.concatenate([third, ones], axis=1)
    projected = None
    third_grad = None
    transposed = (((0,), (0,)), ((), ()))
    for slot in range(HEAD_COUNT):
        head = lax.rem(info_ref[5] + slot, HEAD_COUNT)
        rows = row_refs[slot][...].reshape(tokens, width)
        keys = key_refs[slot][...].reshape(tokens, width)
        part = jnp.dot(rows, proj_weight_ref[head], preferred_element_type=jnp.float32)
        projected = part if projected is None else projected + part
        part = jnp.dot(
            jnp.concatenate([rows, keys], axis=1),
            jnp.concatenate([query_weight_ref[head], key_weight_ref[head]], axis=0),
            preferred_element_type=jnp.float32,
        )
        third_grad = part if third_grad is None else third_grad + part
        row_grad = lax.dot_general(rows, row_rhs, transposed, preferred_element_type=jnp.float32)
        key_grad = lax.dot_general(keys, key_rhs, transposed, preferred_element_type=jnp.float32)
        start = pl.multiple_of(head * head_width, head_width)
        for place, block in (
            (0, row_grad[:head_width, :channels]),
            (channels, key_grad[:head_width, :channels]),
            (2 * channels, key_grad[head_width:, :channels]),
            (3 * channels, row_grad[head_width:, channels : 2 * channels]),
        ):
            early_ref[pl.ds(place + start, head_width), :] = block.astype(jnp.bfloat16)
        columns_ref[pl.ds(start, head_width), :] = row_grad[:head_width, 2 * channels :]
        columns_ref[pl.ds(channels + start, head_width), :] = key_grad[head_width:, channels:]
    terms = norm_terms(sums_ref[...], counts_ref)
    first, second = [], []
    for i in range(2):
        shape = residual_ref.shape[1:]
        span = slice(i * (tokens // 2), (i + 1) * (tokens // 2))
        values = residual_ref[i]
        mask = mask_of(info_ref, i, shape, 0)
        output_ref[i] = (
            values + mask * from_parts(projected[span] + proj_bias_ref[...], shape)
        ).astype(jnp.bfloat16)
        average, spread = terms[i]
        hat = mask * ((values - average) * spread)
        grad = mask * from_parts(third_grad[span], shape)
        third_grad_ref[i] = grad
        first_ref[i] = grad[:2]
        last_ref[i] = grad[-2:]
        first.append(column_sum(grad))
        second.append(column_sum(grad * hat))
    query_row = columns_ref[:channels, :].T[:1]
    value_row = columns_ref[channels:, :].T[:1]
    put_sums(
        out_sums_ref,
        first + second + [query_row, value_row, column_sum(proj_grad.astype(jnp.float32))],
    )


def norm_grad_means(grad_sums, counts_ref, factors):
    rows = [grad_sums[i : i + 1] * factors[i] for i in range(2)]
    rows += [grad_sums[2 + i : 3 + i] * factors[i] for i in range(2)]
    totals = over_group(
        jnp.concatenate(rows + [jnp.zeros_like(rows[0])] * 4, axis=0), rows[0].shape[-1]
    )
    return [
        (totals[i : i + 1] / counts_ref[i], totals[2 + i : 3 + i] / counts_ref[i])
        for i in range(2)
    ]


def branch_kernel(
    info_ref, counts_ref, grad_low_ref, grad_ref, grad_high_ref, residual_low_ref, residual_ref, residual_high_ref,
    cot_low_ref, cot_ref, cot_high_ref, sums3_ref, gain3_ref, sums4_ref, hidden_ref, sums2_ref, gain2_ref, bias2_ref,
    shifts_ref, active_ref, weight_ref,
    residual_grad_ref, weight_grad_ref, norm_grad_ref, out_sums_ref,
):
    terms = norm_terms(sums3_ref[...], counts_ref)
    gain = gain3_ref[...]
    means = norm_grad_means(sums4_ref[...], counts_ref, [gain, gain])
    images, actives, lows = [], [], []
    shape = hidden_ref.shape[1:]
    channels = shape[-1]
    for i in range(2):
        grad = extended(grad_low_ref, grad_ref, grad_high_ref, i)
        values = extended(residual_low_ref, residual_ref, residual_high_ref, i)
        mask = mask_of(info_ref, i, values.shape, 2)
        average, spread = terms[i]
        hat = mask * ((values - average) * spread)
        first_mean, second_mean = means[i]
        residual_grad = extended(cot_low_ref, cot_ref, cot_high_ref, i) + mask * (
            spread * (grad * gain - first_mean - hat * second_mean)
        )
        residual_grad_ref[i] = residual_grad[2:-2]
        low = (mask * residual_grad).astype(jnp.bfloat16).astype(jnp.float32)
        images.append(shifted(low))
        lows.append(low[2:-2].reshape(-1, channels))
        actives.append(shifted(active_ref[i].astype(jnp.float32)))
    low = jnp.concatenate(lows, axis=0)
    total = conv_grads(images, 8, actives, weight_ref, low.astype(jnp.bfloat16), weight_grad_ref)
    terms = norm_terms(sums2_ref[...], counts_ref)
    first, second = [], []
    for i in range(2):
        mask = mask_of(info_ref, i, shape, 1)
        hat, norm = second_norm_of(
            hidden_ref[i], mask, terms[i], gain2_ref[...], bias2_ref[...], shifts_ref, i
        )
        half = total.shape[0] // 2
        grad = mask * total[i * half : (i + 1) * half].reshape(shape) * silu_slope(norm)
        norm_grad_ref[i] = grad
        grad, hat = grad[1:-1], hat[1:-1]
        first.append(column_sum(grad))
        second.append(column_sum(grad * hat))
    put_sums(out_sums_ref, first + second + [column_sum(low)])


def hidden_grad_kernel(
    info_ref, counts_ref, grad_ref, hidden_ref, sums2_ref, gain2_ref, shifts_ref, sums5_ref, image_ref, sums1_ref, gain1_ref, bias1_ref, active_ref, weight_ref,
    weight_grad_ref, norm_grad_ref, out_sums_ref,
):
    terms = norm_terms(sums2_ref[...], counts_ref)
    shape = image_ref.shape[1:]
    channels = shape[-1]
    factors = [(1.0 + shifts_ref[i : i + 1, :channels]) * gain2_ref[...] for i in range(2)]
    means = norm_grad_means(sums5_ref[...], counts_ref, factors)
    images, actives, lows = [], [], []
    for i in range(2):
        grad = grad_ref[i]
        values = hidden_ref[i]
        mask = mask_of(info_ref, i, values.shape, 1)
        average, spread = terms[i]
        hat = mask * ((values - average) * spread)
        first_mean, second_mean = means[i]
        low = mask * (spread * (grad * factors[i] - first_mean - hat * second_mean))
        low = low.astype(jnp.bfloat16).astype(jnp.float32)
        images.append(shifted(low))
        lows.append(low[1:-1].reshape(-1, channels))
        actives.append(shifted(active_ref[i].astype(jnp.float32)))
    low = jnp.concatenate(lows, axis=0)
    total = conv_grads(images, 6, actives, weight_ref, low.astype(jnp.bfloat16), weight_grad_ref)
    terms = norm_terms(sums1_ref[...], counts_ref)
    first, second = [], []
    for i in range(2):
        mask = mask_of(info_ref, i, shape, 0)
        average, spread = terms[i]
        hat = mask * ((mask * image_ref[i].astype(jnp.float32) - average) * spread)
        norm = mask * (hat * gain1_ref[...] + bias1_ref[...])
        half = total.shape[0] // 2
        grad = mask * total[i * half : (i + 1) * half].reshape(shape) * silu_slope(norm)
        norm_grad_ref[i] = grad
        first.append(column_sum(grad))
        second.append(column_sum(grad * hat))
    put_sums(out_sums_ref, first + second + [column_sum(low)])


def image_grad_kernel(
    info_ref, counts_ref, image_ref, grad_ref, residual_grad_ref, sums1_ref, gain1_ref, sums6_ref, out_ref
):
    terms = norm_terms(sums1_ref[...], counts_ref)
    gain = gain1_ref[...]
    means = norm_grad_means(sums6_ref[...], counts_ref, [gain, gain])
    for i in range(2):
        shape = image_ref.shape[1:]
        mask = mask_of(info_ref, i, shape, 0)
        average, spread = terms[i]
        hat = mask * ((mask * image_ref[i].astype(jnp.float32) - average) * spread)
        first_mean, second_mean = means[i]
        result = residual_grad_ref[i] + mask * (
            spread * (grad_ref[i] * gain - first_mean - hat * second_mean)
        )
        out_ref[i] = (mask * result).astype(jnp.bfloat16)


def weights_kernel(
    info_ref, late_ref, late_beside_ref, early_ref, early_beside_ref, conv1_ref, conv2_ref, qkv_ref, proj_ref
):
    def write(late, early):
        count = late[0].shape[0]
        conv1_ref[:count, :] = late[0][...].astype(jnp.float32)
        conv1_ref[count:, :] = late[1][...].astype(jnp.float32)
        count = early[0].shape[0]
        rest = conv2_ref.shape[0] - count
        width = proj_ref.shape[0]
        conv2_ref[:count, :] = early[0][...].astype(jnp.float32)
        conv2_ref[count:, :] = early[1][:rest, :].astype(jnp.float32)
        for part in range(3):
            span = slice(rest + part * width, rest + (part + 1) * width)
            qkv_ref[:, part * width : (part + 1) * width] = early[1][span, :].astype(jnp.float32).T
        proj_ref[...] = early[1][rest + 3 * width :, :].astype(jnp.float32)

    @pl.when(info_ref[6] == 0)
    def _():
        write((late_ref, late_beside_ref), (early_ref, early_beside_ref))

    @pl.when(info_ref[6] != 0)
    def _():
        write((late_beside_ref, late_ref), (early_beside_ref, early_ref))


def run_kernel(kernel, scalars, arrays, outs, scratch=(), flops=2 * 10**9):
    vmem = pl.BlockSpec(memory_space=pltpu.VMEM)
    smem = pl.BlockSpec(memory_space=pltpu.SMEM)
    return pl.pallas_call(
        kernel,
        out_shape=tuple(jax.ShapeDtypeStruct(shape, kind) for shape, kind in outs),
        in_specs=[smem] * len(scalars) + [vmem] * len(arrays),
        out_specs=(vmem,) * len(outs),
        scratch_shapes=list(scratch),
        compiler_params=pltpu.CompilerParams(vmem_limit_bytes=40 * 2**20),
        cost_estimate=pl.CostEstimate(flops=flops, bytes_accessed=4 * 2**20, transcendentals=0),
        name=kernel.__name__,
    )(*scalars, *arrays)


def attention_kernel(which_image, pieces, block, plan_ref, *refs):
    mix_refs, refs = refs[:4], refs[4:]
    kv_refs, refs = refs[:pieces], refs[pieces:]
    rows_refs, dkv_refs, refs = refs[:4], refs[4:6], refs[6:]
    kv_ref, bias_ref, kvt_ref, qgs_ref, rows_ref, s_ref, p_ref, acc_ref = refs
    tokens, width = rows_refs[0].shape
    half = width // 2
    whole = 8 * tokens
    edge = tokens * LEFT // 40
    left = 8 * edge
    place = plan_ref[0]
    valid_rows = plan_ref[1]
    sizes = ((whole, plan_ref[2]), (left, plan_ref[3]))
    scale = half ** (-0.5)
    pair = block // 2

    def slot_of(part):
        return lax.rem(place - part + 4, 4)

    def rows_of(chunk, size):
        return pl.ds(pl.multiple_of(slot_of(chunk) * whole, whole), size)

    def spans(slot, which):
        return (
            (0, edge, pl.ds(pl.multiple_of(slot * whole + which * edge, 16), edge)),
            (
                edge,
                tokens,
                pl.ds(
                    pl.multiple_of(slot * whole + left + which * (tokens - edge), 16),
                    tokens - edge,
                ),
            ),
        )

    number = 0
    for ref in kv_refs:
        for piece in range(ref.shape[0]):
            which = plan_ref[4 + number]
            number += 1
            for slot in range(4):
                for low, high, span in spans(slot, which):
                    kv_ref[span, :] = ref[piece, slot, low:high, :]
    token_ids = lax.broadcasted_iota(jnp.int32, (whole, width), 0)
    for slot in range(4):
        span = slice(slot * whole, (slot + 1) * whole)
        kvt_ref[:, span] = kv_ref[span, :].T
        acc_ref[span, :] = jnp.zeros((whole, width), jnp.float32)
        room = valid_rows - slot_of(slot) * (whole // 40)
        bound = jnp.where(token_ids < left, room * LEFT, left + room * (40 - LEFT))
        bias_ref[span, :] = jnp.where(token_ids < bound, 0.0, LOWEST).astype(jnp.bfloat16)
    qgs_ref[...] = jnp.zeros(qgs_ref.shape, jnp.bfloat16)
    rows_ref[...] = jnp.zeros(rows_ref.shape, jnp.bfloat16)
    for slot in range(4):
        start = pl.multiple_of(slot_of(slot) * pair, pair)
        qgs_ref[pl.ds(start, tokens), :] = mix_refs[slot][which_image, tokens:, :]

    lane = lax.broadcasted_iota(jnp.int32, (block, width), 1)
    ones = (lax.broadcasted_iota(jnp.int32, (width, block), 0) == 0).astype(jnp.bfloat16)
    zeros = jnp.zeros((half, block), jnp.bfloat16)

    def query_block(number, _):
        qg = qgs_ref[pl.ds(pl.multiple_of(number * block, block), block), :]
        qgt = qg.T
        grad_t = qgt[half:] * jnp.bfloat16(scale)
        score_rhs = jnp.concatenate([qgt[:half], zeros, ones], axis=0)
        grad_rhs = jnp.concatenate([zeros, grad_t], axis=0)
        blank = jnp.zeros_like(qg)
        out_rhs = jnp.concatenate(
            [jnp.where(lane < half, qg, blank), jnp.where(lane < half, blank, qg)], axis=0
        )

        def score_pass(size, chunk, best):
            rows = rows_of(chunk, size)
            lhs = jnp.concatenate([kv_ref[rows, :], bias_ref[rows, :]], axis=1)
            scores = jnp.dot(lhs, score_rhs, preferred_element_type=jnp.float32)
            s_ref[rows, :] = scores
            return jnp.maximum(best, jnp.max(scores.reshape(size // 8, 8, block), axis=0))

        best = jnp.full((8, block), LOWEST, jnp.float32)
        for size, trips in sizes:
            best = lax.fori_loop(0, trips, functools.partial(score_pass, size), best)
        peak = jnp.max(best, axis=0, keepdims=True) * (scale * LOG2E)

        def weight_pass(size, chunk, carried):
            total, out_t = carried
            rows = rows_of(chunk, size)
            weights = jnp.exp2(s_ref[rows, :] * (scale * LOG2E) - peak)
            total = total + jnp.sum(weights.reshape(size // 8, 8, block), axis=0)
            weights = weights.astype(jnp.bfloat16)
            p_ref[rows, :] = weights
            out_t = out_t + jnp.dot(
                kvt_ref[half:, rows], weights, preferred_element_type=jnp.float32
            )
            return total, out_t

        carried = (jnp.zeros((8, block), jnp.float32), jnp.zeros((half, block), jnp.float32))
        for size, trips in sizes:
            carried = lax.fori_loop(0, trips, functools.partial(weight_pass, size), carried)
        total, out_t = carried
        inverse = 1.0 / jnp.sum(total, axis=0, keepdims=True)
        out_t = out_t * inverse
        delta = jnp.sum(out_t * grad_t.astype(jnp.float32), axis=0, keepdims=True)

        def grad_pass(size, chunk, dq_t):
            rows = rows_of(chunk, size)
            prob_grad = jnp.dot(kv_ref[rows, :], grad_rhs, preferred_element_type=jnp.float32)
            probs = p_ref[rows, :].astype(jnp.float32) * inverse
            score_grad = (probs * (prob_grad - delta)).astype(jnp.bfloat16)
            acc_ref[rows, :] += jnp.dot(
                jnp.concatenate([score_grad, probs.astype(jnp.bfloat16)], axis=1),
                out_rhs,
                preferred_element_type=jnp.float32,
            )
            return dq_t + jnp.dot(
                kvt_ref[:half, rows], score_grad, preferred_element_type=jnp.float32
            )

        dq_t = jnp.zeros((half, block), jnp.float32)
        for size, trips in sizes:
            dq_t = lax.fori_loop(0, trips, functools.partial(grad_pass, size), dq_t)
        result = jnp.concatenate([dq_t, out_t], axis=0).T.astype(jnp.bfloat16)
        rows_ref[pl.ds(pl.multiple_of(number * block, block), block), :] = result
        return 0

    lax.fori_loop(0, jnp.where(plan_ref[2] + plan_ref[3] > 2, 2, 1), query_block, 0)
    for slot in range(4):
        start = pl.multiple_of(slot_of(slot) * pair, pair)
        rows_refs[slot][...] = rows_ref[pl.ds(start, tokens), :]
    number = 0
    for ref in dkv_refs:
        for piece in range(ref.shape[0]):
            which = plan_ref[12 + number]
            number += 1
            for slot in range(4):
                for low, high, span in spans(slot, which):
                    ref[piece, slot, low:high, :] = acc_ref[span, :].astype(jnp.bfloat16)


def attend(which_image, plan, mix, *kvs):
    width = mix[0].shape[-1]
    tokens = mix[0].shape[1] // 2
    keys = 8 * 4 * tokens
    block = 512
    vmem = pl.BlockSpec(memory_space=pltpu.VMEM)
    rows = jax.ShapeDtypeStruct((tokens, width), jnp.bfloat16)
    half_keys = jax.ShapeDtypeStruct((4, 4, tokens, width), jnp.bfloat16)
    outs = pl.pallas_call(
        functools.partial(attention_kernel, which_image, len(kvs), block),
        out_shape=(rows,) * 4 + (half_keys,) * 2,
        in_specs=[pl.BlockSpec(memory_space=pltpu.SMEM)] + [vmem] * (4 + len(kvs)),
        out_specs=(vmem,) * 6,
        scratch_shapes=[
            pltpu.VMEM((keys, width), jnp.bfloat16),
            pltpu.VMEM((keys, width), jnp.bfloat16),
            pltpu.VMEM((width, keys), jnp.bfloat16),
            pltpu.VMEM((2 * block, width), jnp.bfloat16),
            pltpu.VMEM((2 * block, width), jnp.bfloat16),
            pltpu.VMEM((keys, block), jnp.float32),
            pltpu.VMEM((keys, block), jnp.bfloat16),
            pltpu.VMEM((keys, width), jnp.float32),
        ],
        compiler_params=pltpu.CompilerParams(vmem_limit_bytes=52 * 2**20),
        cost_estimate=pl.CostEstimate(
            flops=6 * 2 * 1024 * keys * 256,
            bytes_accessed=8 * 2**20,
            transcendentals=1024 * keys,
        ),
        name="attention",
    )(plan, *mix, *kvs)
    return outs[:4], outs[4], outs[5]


def per_device(
    image,
    embedding,
    cotangent,
    valid_rows,
    orientation,
    gn1_gain,
    gn1_bias,
    conv1_weight,
    conv1_bias,
    time_weight,
    time_bias,
    gn2_gain,
    gn2_bias,
    conv2_weight,
    conv2_bias,
    gn3_gain,
    gn3_bias,
    qkv_weight,
    qv_bias,
    proj_weight,
    proj_bias,
):
    images, shard_rows, columns, channels = image.shape
    tokens = shard_rows * columns
    head_width = channels // HEAD_COUNT
    seq_index = lax.axis_index("seq")
    dp_index = lax.axis_index("dp")
    places = {"x": seq_index // 8, "y": seq_index // 2 % 4, "c": seq_index % 2, "z": dp_index}
    place_x, place_y, place_c = places["x"], places["y"], places["c"]
    col_valid = columns - 2 * columns // 5 * orientation
    info = jnp.stack(
        [
            jnp.asarray(number, jnp.int32)
            for number in (
                seq_index * shard_rows,
                valid_rows[0],
                valid_rows[1],
                col_valid[0],
                col_valid[1],
                place_x,
                place_c,
                0,
            )
        ]
    )
    counts = (valid_rows * col_valid).astype(jnp.float32) * (channels // GROUPS)
    scalars = (info, counts)
    gain1, bias1, gain2, bias2, gain3, bias3, conv1_bias, conv2_bias, proj_bias = (
        value[None]
        for value in (
            gn1_gain, gn1_bias, gn2_gain, gn2_bias, gn3_gain, gn3_bias, conv1_bias, conv2_bias, proj_bias,
        )
    )
    taps = conv1_weight.shape
    conv1_weight = conv1_weight.reshape(-1, channels)
    conv2_weight = conv2_weight.reshape(-1, channels)
    wide, low_kind = jnp.float32, jnp.bfloat16
    field = (images, shard_rows, columns, channels)
    edge = (images, 2, columns, channels)
    extended_field = (images, shard_rows + 2, columns, channels)
    sums_shape = (8, channels)

    by_head = jnp.transpose(
        qkv_weight.reshape(channels, 3, HEAD_COUNT, head_width), (2, 1, 0, 3)
    )
    proj_heads = proj_weight.reshape(HEAD_COUNT, head_width, channels)
    blank = jnp.zeros((HEAD_COUNT, channels, head_width), low_kind)
    key_weight = jnp.concatenate([by_head[:, 1], by_head[:, 2]], axis=2)
    query_weight = jnp.concatenate(
        [
            jnp.concatenate([by_head[:, 0], blank], axis=2),
            jnp.concatenate([blank, jnp.swapaxes(proj_heads, 1, 2)], axis=2),
        ],
        axis=1,
    )
    blank_rows = jnp.swapaxes(blank, 1, 2)
    turned = jnp.swapaxes(by_head, 2, 3)
    key_weight_t = jnp.concatenate([turned[:, 1], turned[:, 2]], axis=1)
    query_weight_t = jnp.concatenate([turned[:, 0], blank_rows], axis=1)
    proj_weight_t = jnp.concatenate([blank_rows, proj_heads], axis=1)
    head_bias = qv_bias.reshape(2, HEAD_COUNT, 1, head_width)
    blank_bias = jnp.zeros((HEAD_COUNT, 1, head_width), wide)
    query_bias = jnp.concatenate([head_bias[0], blank_bias], axis=2)
    key_bias = jnp.concatenate([blank_bias, head_bias[1]], axis=2)

    time_input = jax.nn.silu(embedding.astype(wide)).astype(low_kind)
    shifts = jnp.dot(time_input, time_weight, preferred_element_type=wide) + time_bias

    low_edges = row_shift(jnp.stack([image[:, -2:], cotangent[:, -2:]]), 1)
    high_edges = row_shift(jnp.stack([image[:, :2], cotangent[:, :2]]), -1)

    row_ids = seq_index * shard_rows + jnp.arange(shard_rows, dtype=jnp.int32)
    pixel_ok = (row_ids[None, :, None] < valid_rows[:, None, None]) & (
        jnp.arange(columns, dtype=jnp.int32)[None, None, :] < col_valid[:, None, None]
    )
    masked_input = pixel_ok.astype(wide)[..., None] * image.astype(wide)
    sums1 = seq_total(
        jnp.concatenate(
            [
                jnp.sum(masked_input, axis=(1, 2)),
                jnp.sum(masked_input * masked_input, axis=(1, 2)),
                jnp.zeros((4, channels), wide),
            ]
        )
    )
    active1, hidden, sums2 = run_kernel(
        hidden_kernel,
        scalars,
        (low_edges[0], image, high_edges[0], sums1, gain1, bias1, conv1_bias, conv1_weight),
        ((extended_field, low_kind), (extended_field, wide), (sums_shape, wide)),
    )
    sums2 = seq_total(sums2)
    active2, residual, residual_first, residual_last, sums3 = run_kernel(
        residual_kernel,
        scalars,
        (hidden, sums2, gain2, bias2, shifts, conv2_bias, conv2_weight, image),
        ((extended_field, low_kind), (field, wide), (edge, wide), (edge, wide), (sums_shape, wide)),
    )
    sums3 = seq_total(sums3)

    third, proj_grad, *slots = run_kernel(
        mixture_kernel,
        scalars,
        (residual, cotangent, sums3, gain3, bias3, key_weight, query_weight, key_bias, query_bias),
        (((images * tokens, channels), low_kind),) * 2
        + (((images, 2 * tokens, 2 * head_width), low_kind),) * HEAD_COUNT,
    )
    mix = [slots[0]] + [seq_shift(slots[d], d, 0, 0) for d in range(1, 4)]

    trips = (valid_rows + 47) // 48
    own_first = [
        2 * ((place_y + step) % 4) + (place_c if same else 1 - place_c)
        for same in (True, False)
        for step in range(4)
    ]
    as_gathered = [
        2 * ((place_y + step) % 4) + (place_c if same else 1 - place_c)
        for same in (True, False)
        for step in (0, 3, 1, 2)
    ]

    def plan_of(which, key_order, grad_order):
        whole = jnp.where(orientation[which] == 0, trips[which], 0)
        left = jnp.where(orientation[which] == 0, 0, trips[which])
        numbers = [place_x, valid_rows[which], whole, left] + key_order + grad_order
        return jnp.stack([jnp.asarray(n, jnp.int32) for n in numbers])

    groups = [[x * 8 + place for place in range(8)] for x in range(4)]
    own_a, own_b = (jnp.stack([part[which, :tokens] for part in mix]) for which in range(2))
    gathered_b = lax.all_gather(own_b, "seq", axis_index_groups=groups)
    up = seq_shift(own_a, 0, 1, 0)
    down = seq_shift(own_a, 0, 3, 0)
    far = seq_shift(own_a, 0, 2, 0)
    column = jnp.stack([own_a, up, down, far])
    beside = seq_shift(column, 0, 0, 1)
    rows_a, *dkv_a = attend(0, plan_of(0, as_gathered, list(range(8))), mix, column, beside)
    scattered_a = lax.psum_scatter(
        jnp.concatenate(dkv_a), "seq", scatter_dimension=0, axis_index_groups=groups
    )
    rows_b, own_b, beside_b = attend(1, plan_of(1, list(range(8)), own_first), mix, gathered_b)

    def back(parts):
        pairs = [jnp.stack(pair) for pair in zip(*parts)]
        return [pairs[0]] + [seq_shift(pairs[d], 4 - d, 0, 0) for d in range(1, 4)]

    rows_back = back((rows_a, rows_b))
    column_b = low_sum(own_b, seq_shift(beside_b, 0, 0, 1))
    scattered_b = low_sum(
        column_b[0], *(seq_shift(column_b[step], 0, step, 0) for step in (1, 3, 2))
    )
    keys_back = back((scattered_a, scattered_b))
    output, third_grad, third_first, third_last, sums4, early_rest = run_kernel(
        output_kernel,
        scalars,
        (
            residual, sums3, gain3, third, proj_grad, query_weight_t, key_weight_t, proj_weight_t, proj_bias,
            *rows_back, *keys_back,
        ),
        (
            (field, low_kind), (field, wide), (edge, wide), (edge, wide), (sums_shape, wide),
            ((4 * channels, channels), low_kind),
        ),
        scratch=(pltpu.VMEM((2 * channels, 2 * head_width), wide),),
    )
    third_low, residual_low = row_shift(jnp.stack([third_last, residual_last]), 1)
    third_high, residual_high = row_shift(jnp.stack([third_first, residual_first]), -1)
    sums4 = seq_total(sums4)
    residual_grad, conv2_grad, norm2_grad, sums5 = run_kernel(
        branch_kernel,
        scalars,
        (
            third_low, third_grad, third_high, residual_low, residual, residual_high, low_edges[1], cotangent,
            high_edges[1], sums3, gain3, sums4, hidden, sums2, gain2, bias2, shifts, active2, conv2_weight,
        ),
        (
            (field, wide), (conv2_weight.shape, low_kind), (extended_field, wide), (sums_shape, wide),
        ),
    )
    early = jnp.concatenate([conv2_grad, early_rest])
    early = lax.psum_scatter(
        jnp.swapaxes(early.reshape(2, 4, -1, channels), 0, 1).reshape(8, -1, channels),
        "seq",
        scatter_dimension=0,
        axis_index_groups=groups,
    )
    sums5 = seq_total(sums5)
    conv1_grad, norm1_grad, sums6 = run_kernel(
        hidden_grad_kernel,
        scalars,
        (
            norm2_grad, hidden, sums2, gain2, shifts, sums5, image, sums1, gain1, bias1, active1, conv1_weight,
        ),
        ((conv1_weight.shape, low_kind), (field, wide), (sums_shape, wide)),
    )
    both, sums6 = sums_over_seq(conv1_grad, early, sums6, places)
    (image_grad,) = run_kernel(
        image_grad_kernel,
        scalars,
        (image, norm1_grad, residual_grad, sums1, gain1, sums6),
        ((field, low_kind),),
    )

    scaling = shifts[:, :channels]
    scale_total = gain2 * sums5[2:4] + bias2 * sums5[:2]
    shift_low = jnp.concatenate([scale_total, sums5[:2]], axis=-1).astype(low_kind)
    embedding_grad = jnp.einsum(
        "ik,ek->ie", shift_low, time_weight, preferred_element_type=wide
    ) * silu_slope(embedding.astype(wide))
    rows = [
        sums6[2] + sums6[3],
        sums6[0] + sums6[1],
        sums6[4],
        jnp.sum((1.0 + scaling) * sums5[2:4], axis=0),
        jnp.sum((1.0 + scaling) * sums5[:2], axis=0),
        sums5[4],
        sums4[2] + sums4[3],
        sums4[0] + sums4[1],
        sums4[4],
        sums4[5],
        sums4[6],
    ]
    time_pair = jnp.concatenate([time_input, shift_low], axis=-1)
    both, totals, every_pair = sums_over_dp(
        both, jnp.stack(rows), time_pair.reshape(-1, channels), places
    )
    every_input, every_shift = jnp.split(
        every_pair.reshape(-1, time_pair.shape[-1]), (time_input.shape[-1],), axis=-1
    )
    time_weight_grad = jnp.einsum(
        "ie,ik->ek", every_input, every_shift, preferred_element_type=wide
    )
    time_bias_grad = jnp.sum(every_shift, axis=0, dtype=wide)
    parts = gathered_over_seq(both, conv1_weight.shape[0] // 32, places)
    conv1_total, conv2_total, qkv_total, proj_total = run_kernel(
        weights_kernel,
        (info,),
        parts,
        (
            (conv1_weight.shape, wide), (conv2_weight.shape, wide), ((channels, 3 * channels), wide),
            ((channels, channels), wide),
        ),
    )
    return (
        output,
        image_grad,
        embedding_grad,
        totals[0],
        totals[1],
        conv1_total.reshape(taps),
        totals[2],
        time_weight_grad,
        time_bias_grad,
        totals[3],
        totals[4],
        conv2_total.reshape(taps),
        totals[5],
        totals[6],
        totals[7],
        qkv_total,
        jnp.concatenate([totals[8], totals[9]]),
        proj_total,
        totals[10],
    )


def solution(mesh):
    return jax.shard_map(
        per_device,
        mesh=mesh,
        in_specs=(
            P("dp", "seq", None, None),
            P("dp", None),
            P("dp", "seq", None, None),
            P("dp"),
            P("dp"),
            P(),
            P(),
            P(),
            P(),
            P(),
            P(),
            P(),
            P(),
            P(),
            P(),
            P(),
            P(),
            P(),
            P(),
            P(),
            P(),
        ),
        out_specs=(
            P("dp", "seq", None, None),
            P("dp", "seq", None, None),
            P("dp", None),
            P(),
            P(),
            P(),
            P(),
            P(),
            P(),
            P(),
            P(),
            P(),
            P(),
            P(),
            P(),
            P(),
            P(),
            P(),
            P(),
        ),
        check_vma=False,
    )
```

```python
import functools

import jax
import jax.numpy as jnp
from jax import lax
from jax.experimental import pallas as pl
from jax.experimental.pallas import tpu as pltpu
from jax.sharding import PartitionSpec as P

GROUPS = 32
HEAD_COUNT = 4


EPS = 1e-05
LOWEST = -1e30
LOG2E = 1.4426950408889634

LEFT = 24

VMEM_CONV = 24 * 2**20
VMEM_ATTENTION = 44 * 2**20


def seq_shift(value, dx, dy, dc):
    pairs = []
    for place in range(32):
        x, y, c = place // 8, place // 2 % 4, place % 2
        pairs.append((place, (x + dx) % 4 * 8 + (y + dy) % 4 * 2 + (c + dc) % 2))
    return lax.ppermute(value, "seq", pairs)


def axis_shift(value, axis, step):
    if axis == "x":
        return seq_shift(value, step, 0, 0)
    if axis == "y":
        return seq_shift(value, 0, step, 0)
    return lax.ppermute(value, "dp", [(i, (i + step) % 4) for i in range(4)])


def row_shift(value, step):
    return lax.ppermute(value, "seq", [(i, (i + step) % 32) for i in range(32)])


def swap_places(value):
    groups = [[place * 2 + core for place in range(16)] for core in range(2)]
    return lax.all_to_all(value, "seq", 0, 0, axis_index_groups=groups)


def places_total(value):
    return jnp.sum(swap_places(jnp.broadcast_to(value[None], (16,) + value.shape)), axis=0)


def seq_total(value):
    return places_total(value + seq_shift(value, 0, 0, 1))


def core_total(value, c):
    return low_sum(take_slot(value, c), seq_shift(take_slot(value, 1 - c), 0, 0, 1))


def place_total(value):
    return jnp.sum(swap_places(value).astype(jnp.float32), axis=0)


def take_slot(value, slot):
    return lax.dynamic_index_in_dim(value, slot, 0, keepdims=False)


def low_sum(*parts):
    total = parts[0].astype(jnp.float32)
    for part in parts[1:]:
        total = total + part.astype(jnp.float32)
    return total.astype(jnp.bfloat16)


def scatter_ring(value, axis, place):
    return low_sum(
        take_slot(value, place),
        *(axis_shift(take_slot(value, (place + step) % 4), axis, step) for step in (1, 3, 2)),
    )


def gather_ring(value, axis, place):
    result = jnp.zeros((4,) + value.shape, value.dtype)
    result = lax.dynamic_update_index_in_dim(result, value, place, 0)
    for step in (1, 3, 2):
        result = lax.dynamic_update_index_in_dim(
            result, axis_shift(value, axis, step), (place - step) % 4, 0
        )
    return result


def split_low(value):
    high = value.astype(jnp.bfloat16)
    both = jnp.concatenate([high, (value - high.astype(jnp.float32)).astype(jnp.bfloat16)])
    both = both.reshape(-1, 128)
    return jnp.pad(both, ((0, -both.shape[0] % 16), (0, 0)))


def join_low(value, rows):
    value = value[: 4 * rows].astype(jnp.float32).reshape(2, rows, 256)
    return value[0] + value[1]


def paired(parts):
    return (parts[0] + parts[2]) + (parts[1] + parts[3])


def sums_over_seq(late, vector, places):
    late = core_total(late, places["c"])
    low = split_low(vector + seq_shift(vector, 0, 0, 1))
    total = place_total(
        jnp.concatenate([late, jnp.broadcast_to(low[None], (16,) + low.shape)], axis=1)
    )
    count = late.shape[1]
    return total[:count].astype(jnp.bfloat16), join_low(total[count:], vector.shape[0])


def sums_over_dp(both, vector, extra, places):
    low = split_low(vector)
    sent = jnp.concatenate([both, low, extra])
    got = [sent] + [axis_shift(sent, "z", step) for step in (1, 2, 3)]
    count = both.shape[0]
    both = paired([part[:count].astype(jnp.float32) for part in got]).astype(jnp.bfloat16)
    count += low.shape[0]
    vector = paired(
        [join_low(part[count - low.shape[0] : count], vector.shape[0]) for part in got]
    )
    extras = jnp.zeros((4,) + extra.shape, extra.dtype)
    for step in range(4):
        extras = lax.dynamic_update_index_in_dim(
            extras, got[step][count:], (places["z"] - step) % 4, 0
        )
    return both, vector, extras


def gathered_over_seq(both, places):
    both = gather_ring(both, "y", places["y"])
    both = gather_ring(both, "x", places["x"]).reshape((16, -1) + both.shape[2:])
    return both, seq_shift(both, 0, 0, 1)


def silu_slope(values):
    sigmoid = jax.nn.sigmoid(values)
    return sigmoid * (1.0 + values * (1.0 - sigmoid))


def same_group(channels):
    size = channels // GROUPS
    rows = lax.broadcasted_iota(jnp.int32, (channels, channels), 0) // size
    cols = lax.broadcasted_iota(jnp.int32, (channels, channels), 1) // size
    return (rows == cols).astype(jnp.float32)


def over_group(sums, channels):
    return jnp.dot(
        sums, same_group(channels), precision=lax.Precision.HIGHEST, preferred_element_type=jnp.float32
    )


def norm_terms(sums, counts_ref):
    totals = over_group(sums[:4], sums.shape[-1])
    terms = []
    for i in range(2):
        average = totals[i : i + 1] / counts_ref[i]
        spread = lax.rsqrt(totals[2 + i : 3 + i] / counts_ref[i] - average * average + EPS)
        terms.append((average, spread))
    return terms


def mask_of(info_ref, i, shape, border):
    rows = lax.broadcasted_iota(jnp.int32, shape, 0) + (info_ref[0] - border)
    cols = lax.broadcasted_iota(jnp.int32, shape, 1)
    valid = (rows >= 0) & (rows < info_ref[1 + i]) & (cols < info_ref[3 + i])
    return valid.astype(jnp.float32)


def extended(low, own, high):
    return jnp.concatenate([low, own, high], axis=0).astype(jnp.float32)


def shifted(values):
    rows, columns, channels = values.shape
    cols = lax.broadcasted_iota(jnp.int32, values.shape, 1).reshape(-1, channels)
    flat = values.reshape(-1, channels)
    before = jnp.where(cols == 0, 0.0, pltpu.roll(flat, 1, 0))
    after = jnp.where(cols == columns - 1, 0.0, pltpu.roll(flat, rows * columns - 1, 0))
    return before, flat, after


def tap_rows(images, a, b, rows, columns=40):
    return jnp.concatenate(
        [image[b][a * columns : (a + rows) * columns] for image in images], axis=0
    ).astype(jnp.bfloat16)


def conv_taps(images, weight_ref, rows):
    patches = jnp.concatenate(
        [tap_rows(images, a, b, rows) for a in range(3) for b in range(3)], axis=1
    )
    return jnp.dot(patches, weight_ref[...], preferred_element_type=jnp.float32)


def put_rows(ref, first, values):
    rows = 9 * values.shape[1] // 16
    width = ref.shape[-1]
    last = first + values.shape[0]
    while first < last:
        place, low = divmod(first, rows)
        count = min(rows - low, last - first)
        for core in range(2):
            part = values[:count, core * width : (core + 1) * width].astype(jnp.bfloat16)
            if len(ref.shape) == 4:
                ref[core, place, low : low + count, :] = part
            else:
                ref[place // 4, core, place % 4, low : low + count, :] = part
        values = values[count:]
        first += count


def conv_grads(images, rows, actives, weight_ref, low, weight_grad_ref):
    total = None
    channels = low.shape[-1]
    for a in range(3):
        for b in range(3):
            span = slice((3 * a + b) * channels, (3 * a + b + 1) * channels)
            put_rows(
                weight_grad_ref,
                span.start,
                lax.dot_general(
                    tap_rows(actives, a, b, 6),
                    low,
                    (((0,), (0,)), ((), ())),
                    preferred_element_type=jnp.float32,
                ),
            )
            part = lax.dot_general(
                tap_rows(images, 2 - a, 2 - b, rows),
                weight_ref[span, :],
                (((1,), (1,)), ((), ())),
                preferred_element_type=jnp.float32,
            )
            total = part if total is None else total + part
    return total


def put_sums(ref, rows):
    for place, row in enumerate(rows):
        ref[place : place + 1, :] = row


def column_sum(values):
    return jnp.sum(values.reshape(-1, values.shape[-1]), axis=0, keepdims=True)


def start_kernel(info_ref, image_ref, cotangent_ref, first_ref, last_ref, out_sums_ref):
    first, second = [], []
    for i in range(2):
        image = image_ref[i]
        first_ref[0, i] = image[:2]
        last_ref[0, i] = image[-2:]
        first_ref[1, i] = cotangent_ref[i, :2]
        last_ref[1, i] = cotangent_ref[i, -2:]
        values = mask_of(info_ref, i, image.shape, 0) * image.astype(jnp.float32)
        first.append(column_sum(values))
        second.append(column_sum(values * values))
    put_sums(out_sums_ref, first + second)


def hidden_kernel(
    info_ref, counts_ref, low_ref, high_ref, sums_ref, gain_ref, bias_ref, conv_bias_ref, own_ref, weight_ref,
    active_ref, hidden_ref, out_sums_ref,
):
    terms = norm_terms(sums_ref[...], counts_ref)
    images = []
    for i in range(2):
        values = extended(low_ref[0, i], own_ref[i], high_ref[0, i])
        mask = mask_of(info_ref, i, values.shape, 2)
        average, spread = terms[i]
        hat = mask * ((mask * values - average) * spread)
        active = jax.nn.silu(mask * (hat * gain_ref[...] + bias_ref[...])).astype(jnp.bfloat16)
        active_ref[i] = active[1:-1]
        images.append(shifted(active.astype(jnp.float32)))
    conv = conv_taps(images, weight_ref, 8)
    first, second = [], []
    for i in range(2):
        shape = hidden_ref.shape[1:]
        mask = mask_of(info_ref, i, shape, 1)
        half = conv.shape[0] // 2
        hidden = mask * (conv[i * half : (i + 1) * half].reshape(shape) + conv_bias_ref[...])
        hidden_ref[i] = hidden
        hidden = hidden[1:-1]
        first.append(column_sum(hidden))
        second.append(column_sum(hidden * hidden))
    put_sums(out_sums_ref, first + second)


def second_norm_of(values, mask, term, gain, bias, shifts_ref, i):
    channels = values.shape[-1]
    average, spread = term
    hat = mask * ((values - average) * spread)
    base = mask * (hat * gain + bias)
    scaling = shifts_ref[i : i + 1, :channels]
    offset = shifts_ref[i : i + 1, channels:]
    return hat, mask * (base * (1.0 + scaling) + offset)


def residual_kernel(
    info_ref, counts_ref, hidden_ref, sums_ref, gain_ref, bias_ref, shifts_ref, conv_bias_ref, image_ref, weight_ref,
    active_ref, residual_ref, out_sums_ref,
):
    terms = norm_terms(sums_ref[...], counts_ref)
    images = []
    for i in range(2):
        values = hidden_ref[i]
        mask = mask_of(info_ref, i, values.shape, 1)
        _, norm = second_norm_of(
            values, mask, terms[i], gain_ref[...], bias_ref[...], shifts_ref, i
        )
        active = jax.nn.silu(norm).astype(jnp.bfloat16)
        active_ref[i] = active
        images.append(shifted(active.astype(jnp.float32)))
    conv = conv_taps(images, weight_ref, 6)
    first, second = [], []
    for i in range(2):
        shape = residual_ref.shape[1:]
        mask = mask_of(info_ref, i, shape, 0)
        half = conv.shape[0] // 2
        residual = mask * image_ref[i].astype(jnp.float32) + mask * (
            conv[i * half : (i + 1) * half].reshape(shape) + conv_bias_ref[...]
        )
        residual_ref[i] = residual
        first.append(column_sum(residual))
        second.append(column_sum(residual * residual))
    put_sums(out_sums_ref, first + second)


def to_parts(values):
    channels = values.shape[-1]
    return jnp.concatenate(
        [values[:, :LEFT].reshape(-1, channels), values[:, LEFT:].reshape(-1, channels)], axis=0
    )


def from_parts(values, shape):
    rows, columns, channels = shape
    edge = rows * LEFT
    return jnp.concatenate(
        [
            values[:edge].reshape(rows, LEFT, channels),
            values[edge:].reshape(rows, columns - LEFT, channels),
        ],
        axis=1,
    )


def mixture_kernel(
    info_ref, counts_ref, residual_ref, sums_ref, gain_ref, bias_ref, key_weight_ref, query_weight_ref,
    key_bias_ref, query_bias_ref, cotangent_ref, third_ref, grad_ref, first_ref, *slot_refs,
):
    terms = norm_terms(sums_ref[...], counts_ref)
    tokens = third_ref.shape[0] // 2
    for i in range(2):
        values = residual_ref[i]
        mask = mask_of(info_ref, i, values.shape, 0)
        average, spread = terms[i]
        hat = mask * ((values - average) * spread)
        span = slice(i * tokens, (i + 1) * tokens)
        third_ref[span, :] = to_parts(mask * (hat * gain_ref[...] + bias_ref[...])).astype(
            jnp.bfloat16
        )
        grad_ref[span, :] = to_parts(mask * cotangent_ref[i].astype(jnp.float32)).astype(
            jnp.bfloat16
        )
    third = third_ref[...]
    both = jnp.concatenate([third, grad_ref[...]], axis=1)
    for head in range(HEAD_COUNT):
        keys = (
            jnp.dot(third[:tokens], key_weight_ref[head], preferred_element_type=jnp.float32)
            + key_bias_ref[head]
        ).astype(jnp.bfloat16)
        for place in range(4):
            first_ref[4 * head + place] = keys
    for slot, ref in enumerate(slot_refs):
        head = lax.rem(info_ref[5] + slot, HEAD_COUNT)
        keys = (
            jnp.dot(third[tokens:], key_weight_ref[head], preferred_element_type=jnp.float32)
            + key_bias_ref[head]
        ).astype(jnp.bfloat16)
        queries = (
            jnp.dot(both, query_weight_ref[head], preferred_element_type=jnp.float32)
            + query_bias_ref[head]
        ).astype(jnp.bfloat16)
        ref[:tokens, :] = keys
        ref[tokens:, :] = queries


def output_kernel(
    info_ref, counts_ref, sums_ref, gain_ref, proj_bias_ref, *refs,
):
    row_refs, first_refs, key_ref, refs = refs[:4], refs[4:8], refs[8], refs[9:]
    third_ref, grad_ref, query_weight_ref, key_weight_ref, proj_weight_ref, residual_ref, *refs = refs
    output_ref, third_grad_ref, first_ref, last_ref, out_sums_ref, early_ref, columns_ref, wait = refs
    tokens, channels = third_ref.shape
    width = channels // 2
    head_width = channels // HEAD_COUNT
    third = third_ref[...]
    proj_grad = grad_ref[...]
    ones = jnp.ones((tokens, width), jnp.bfloat16)
    row_rhs = jnp.concatenate([third, proj_grad, ones], axis=1)
    key_rhs = jnp.concatenate([third, ones], axis=1)
    projected = None
    third_grad = None
    transposed = (((0,), (0,)), ((), ()))
    for slot in range(HEAD_COUNT):
        head = lax.rem(info_ref[5] + slot, HEAD_COUNT)
        rows = row_refs[slot][...].reshape(tokens, width)
        last = key_ref[pl.ds(pl.multiple_of(4 * head, 4), 4)].astype(jnp.float32)
        keys = jnp.concatenate(
            [first_refs[slot][...], jnp.sum(last, axis=0).astype(jnp.bfloat16)], axis=0
        )
        part = jnp.dot(rows, proj_weight_ref[head], preferred_element_type=jnp.float32)
        projected = part if projected is None else projected + part
        part = jnp.dot(
            jnp.concatenate([rows, keys], axis=1),
            jnp.concatenate([query_weight_ref[head], key_weight_ref[head]], axis=0),
            preferred_element_type=jnp.float32,
        )
        third_grad = part if third_grad is None else third_grad + part
        row_grad = lax.dot_general(rows, row_rhs, transposed, preferred_element_type=jnp.float32)
        key_grad = lax.dot_general(keys, key_rhs, transposed, preferred_element_type=jnp.float32)
        start = pl.multiple_of(head * head_width, head_width)
        for place, block in (
            (0, row_grad[:head_width, :channels]),
            (channels, key_grad[:head_width, :channels]),
            (2 * channels, key_grad[head_width:, :channels]),
            (3 * channels, row_grad[head_width:, channels : 2 * channels]),
        ):
            for core in range(2):
                early_ref[place // channels, core, head] = block[
                    :, core * width : (core + 1) * width
                ].astype(jnp.bfloat16)
        columns_ref[pl.ds(start, head_width), :] = row_grad[:head_width, 2 * channels :]
        columns_ref[pl.ds(channels + start, head_width), :] = key_grad[head_width:, channels:]
    terms = norm_terms(sums_ref[...], counts_ref)
    wait()
    first, second = [], []
    for i in range(2):
        shape = residual_ref.shape[1:]
        span = slice(i * (tokens // 2), (i + 1) * (tokens // 2))
        values = residual_ref[i]
        mask = mask_of(info_ref, i, shape, 0)
        output_ref[i] = (
            values + mask * from_parts(projected[span] + proj_bias_ref[...], shape)
        ).astype(jnp.bfloat16)
        average, spread = terms[i]
        hat = mask * ((values - average) * spread)
        grad = mask * from_parts(third_grad[span], shape)
        third_grad_ref[i] = grad
        first_ref[0, i] = grad[:2]
        last_ref[0, i] = grad[-2:]
        first_ref[1, i] = values[:2]
        last_ref[1, i] = values[-2:]
        first.append(column_sum(grad))
        second.append(column_sum(grad * hat))
    query_row = columns_ref[:channels, :].T[:1]
    value_row = columns_ref[channels:, :].T[:1]
    put_sums(
        out_sums_ref,
        first + second + [query_row, value_row, column_sum(proj_grad.astype(jnp.float32))],
    )


def norm_grad_means(grad_sums, counts_ref, factors):
    rows = [grad_sums[i : i + 1] * factors[i] for i in range(2)]
    rows += [grad_sums[2 + i : 3 + i] * factors[i] for i in range(2)]
    totals = over_group(
        jnp.concatenate(rows, axis=0), rows[0].shape[-1]
    )
    return [
        (totals[i : i + 1] / counts_ref[i], totals[2 + i : 3 + i] / counts_ref[i])
        for i in range(2)
    ]


def branch_kernel(
    info_ref, counts_ref, low_ref, high_ref, cot_low_ref, cot_high_ref, sums3_ref, gain3_ref, sums4_ref, sums2_ref,
    gain2_ref, bias2_ref, shifts_ref, grad_ref, residual_ref, cot_ref, hidden_ref, active_ref, weight_ref, rest_ref,
    residual_grad_ref, weight_grad_ref, norm_grad_ref, out_sums_ref, wait,
):
    terms = norm_terms(sums3_ref[...], counts_ref)
    gain = gain3_ref[...]
    means = norm_grad_means(sums4_ref[...], counts_ref, [gain, gain])
    images, actives, lows = [], [], []
    shape = hidden_ref.shape[1:]
    channels = shape[-1]
    for i in range(2):
        grad = extended(low_ref[0, i], grad_ref[i], high_ref[0, i])
        values = extended(low_ref[1, i], residual_ref[i], high_ref[1, i])
        mask = mask_of(info_ref, i, values.shape, 2)
        average, spread = terms[i]
        hat = mask * ((values - average) * spread)
        first_mean, second_mean = means[i]
        residual_grad = extended(cot_low_ref[1, i], cot_ref[i], cot_high_ref[1, i]) + mask * (
            spread * (grad * gain - first_mean - hat * second_mean)
        )
        residual_grad_ref[i] = residual_grad[2:-2]
        low = (mask * residual_grad).astype(jnp.bfloat16).astype(jnp.float32)
        images.append(shifted(low))
        lows.append(low[2:-2].reshape(-1, channels))
    wait()
    for i in range(2):
        actives.append(shifted(active_ref[i].astype(jnp.float32)))
    low = jnp.concatenate(lows, axis=0)
    total = conv_grads(images, 8, actives, weight_ref, low.astype(jnp.bfloat16), weight_grad_ref)
    terms = norm_terms(sums2_ref[...], counts_ref)
    first, second = [], []
    for i in range(2):
        mask = mask_of(info_ref, i, shape, 1)
        hat, norm = second_norm_of(
            hidden_ref[i], mask, terms[i], gain2_ref[...], bias2_ref[...], shifts_ref, i
        )
        half = total.shape[0] // 2
        grad = mask * total[i * half : (i + 1) * half].reshape(shape) * silu_slope(norm)
        norm_grad_ref[i] = grad
        grad, hat = grad[1:-1], hat[1:-1]
        first.append(column_sum(grad))
        second.append(column_sum(grad * hat))
    put_sums(out_sums_ref, first + second + [column_sum(low)])
    weight_grad_ref[:, :, :, -rest_ref.shape[3] :, :] = rest_ref[...]


def hidden_grad_kernel(
    info_ref, counts_ref, sums2_ref, gain2_ref, shifts_ref, sums5_ref, sums1_ref, gain1_ref, bias1_ref,
    grad_ref, hidden_ref, image_ref, active_ref, weight_ref,
    weight_grad_ref, norm_grad_ref, out_sums_ref, wait,
):
    terms = norm_terms(sums2_ref[...], counts_ref)
    shape = image_ref.shape[1:]
    channels = shape[-1]
    factors = [(1.0 + shifts_ref[i : i + 1, :channels]) * gain2_ref[...] for i in range(2)]
    means = norm_grad_means(sums5_ref[...], counts_ref, factors)
    images, actives, lows = [], [], []
    for i in range(2):
        grad = grad_ref[i]
        values = hidden_ref[i]
        mask = mask_of(info_ref, i, values.shape, 1)
        average, spread = terms[i]
        hat = mask * ((values - average) * spread)
        first_mean, second_mean = means[i]
        low = mask * (spread * (grad * factors[i] - first_mean - hat * second_mean))
        low = low.astype(jnp.bfloat16).astype(jnp.float32)
        images.append(shifted(low))
        lows.append(low[1:-1].reshape(-1, channels))
    wait()
    for i in range(2):
        actives.append(shifted(active_ref[i].astype(jnp.float32)))
    low = jnp.concatenate(lows, axis=0)
    total = conv_grads(images, 6, actives, weight_ref, low.astype(jnp.bfloat16), weight_grad_ref)
    terms = norm_terms(sums1_ref[...], counts_ref)
    first, second = [], []
    for i in range(2):
        mask = mask_of(info_ref, i, shape, 0)
        average, spread = terms[i]
        hat = mask * ((mask * image_ref[i].astype(jnp.float32) - average) * spread)
        norm = mask * (hat * gain1_ref[...] + bias1_ref[...])
        half = total.shape[0] // 2
        grad = mask * total[i * half : (i + 1) * half].reshape(shape) * silu_slope(norm)
        norm_grad_ref[i] = grad
        first.append(column_sum(grad))
        second.append(column_sum(grad * hat))
    put_sums(out_sums_ref, first + second + [column_sum(low)])


def image_grad_kernel(
    info_ref, counts_ref, sums1_ref, gain1_ref, sums6_ref, image_ref, grad_ref, residual_grad_ref, out_ref
):
    terms = norm_terms(sums1_ref[...], counts_ref)
    gain = gain1_ref[...]
    means = norm_grad_means(sums6_ref[...], counts_ref, [gain, gain])
    for i in range(2):
        shape = image_ref.shape[1:]
        mask = mask_of(info_ref, i, shape, 0)
        average, spread = terms[i]
        hat = mask * ((mask * image_ref[i].astype(jnp.float32) - average) * spread)
        first_mean, second_mean = means[i]
        result = residual_grad_ref[i] + mask * (
            spread * (grad_ref[i] * gain - first_mean - hat * second_mean)
        )
        out_ref[i] = (mask * result).astype(jnp.bfloat16)


def weights_kernel(info_ref, own_ref, beside_ref, conv1_ref, conv2_ref, qkv_ref, proj_ref, rest_ref):
    channels = proj_ref.shape[0]

    def write(refs):
        taps = conv1_ref.shape[0] // 16
        rest = 4 * channels // 16
        width = channels // 2
        for core, ref in enumerate(refs):
            columns = slice(core * width, (core + 1) * width)
            for place in range(16):
                value = ref[place].astype(jnp.float32)
                conv1_ref[place * taps : (place + 1) * taps, columns] = value[:taps]
                number = place % 4 * 4 + place // 4
                conv2_ref[number * taps : (number + 1) * taps, columns] = value[taps : 2 * taps]
                rest_ref[number * rest : (number + 1) * rest, columns] = value[2 * taps :]

    @pl.when(info_ref[6] == 0)
    def _():
        write((own_ref, beside_ref))

    @pl.when(info_ref[6] != 0)
    def _():
        write((beside_ref, own_ref))

    for part in range(3):
        span = slice(part * channels, (part + 1) * channels)
        qkv_ref[:, span] = rest_ref[span, :].T
    proj_ref[...] = rest_ref[3 * channels :, :]


def fetching(kernel, n_in, early, late, n_out):
    def body(*refs):
        count = early + late
        ins, refs = refs[:n_in], refs[n_in:]
        sources, refs = refs[:count], refs[count:]
        outs, refs = refs[:n_out], refs[n_out:]
        buffers, refs = refs[:count], refs[count:]
        sems, refs = refs[0], refs[1:]
        copies = [
            pltpu.make_async_copy(source, buffer, sems.at[number])
            for number, (source, buffer) in enumerate(zip(sources, buffers))
        ]
        for copy in copies:
            copy.start()
        for copy in copies[:early]:
            copy.wait()

        def wait():
            for copy in copies[early:]:
                copy.wait()

        kernel(*ins, *buffers, *outs, *refs, *((wait,) if late else ()))

    return body


def in_hbm(arrays):
    return [pltpu.with_memory_space_constraint(array, pltpu.HBM) for array in arrays]


def buffers_of(arrays):
    return [pltpu.VMEM(array.shape, array.dtype) for array in arrays] + [
        pltpu.SemaphoreType.DMA((len(arrays),))
    ]


def run_kernel(kernel, scalars, arrays, outs, scratch=(), early=(), late=()):
    vmem = pl.BlockSpec(memory_space=pltpu.VMEM)
    smem = pl.BlockSpec(memory_space=pltpu.SMEM)
    hbm = pl.BlockSpec(memory_space=pltpu.HBM)
    fetched = [*early, *late]
    body, scratch = kernel, list(scratch)
    if fetched:
        body = fetching(kernel, len(scalars) + len(arrays), len(early), len(late), len(outs))
        scratch = buffers_of(fetched) + scratch
    return pl.pallas_call(
        body,
        out_shape=tuple(jax.ShapeDtypeStruct(shape, kind) for shape, kind in outs),
        in_specs=[smem] * len(scalars) + [vmem] * len(arrays) + [hbm] * len(fetched),
        out_specs=(vmem,) * len(outs),
        scratch_shapes=scratch,
        compiler_params=pltpu.CompilerParams(vmem_limit_bytes=VMEM_CONV),
        cost_estimate=pl.CostEstimate(
            flops=2 * 10**9, bytes_accessed=4 * 2**20, transcendentals=0
        ),
        name=kernel.__name__,
    )(*scalars, *arrays, *in_hbm(fetched))


def attention_kernel(which_image, pieces, block, info_ref, *refs):
    mix_refs, refs = refs[:4], refs[4:]
    kv_refs, refs = refs[:pieces], refs[pieces:]
    outs = 1 if pieces == 2 else 2
    rows_refs, dkv_refs, refs = refs[:4], refs[4 : 4 + outs], refs[4 + outs :]
    kv_ref, extra_ref, kvt_ref, qgs_ref, rows_ref, s_ref, p_ref, acc_ref = refs
    tokens, width = rows_refs[0].shape
    half = width // 2
    whole = 8 * tokens
    edge = tokens * LEFT // 40
    left = 8 * edge
    valid_rows = info_ref[1 + which_image]
    landscape = info_ref[3 + which_image] == 40
    place, core = info_ref[5], info_ref[6]
    trips = lax.div(valid_rows + 47, 48)
    sizes = ((whole, jnp.where(landscape, trips, 0)), (left, jnp.where(landscape, 0, trips)))
    scale = half ** (-0.5)
    pair = block // 2

    def slot_of(part):
        return lax.rem(place - part + 4, 4)

    def rows_of(chunk, size):
        return pl.ds(pl.multiple_of(chunk * whole, whole), size)

    def spans(part, which):
        return (
            (0, edge, pl.ds(pl.multiple_of(part * whole + which * edge, 16), edge)),
            (
                edge,
                tokens,
                pl.ds(
                    pl.multiple_of(part * whole + left + which * (tokens - edge), 16),
                    tokens - edge,
                ),
            ),
        )

    if pieces == 2:
        for ref, beside in zip(kv_refs, (core, 1 - core)):
            for number in range(16):
                for low, high, span in spans(number // 4, 2 * (number % 4) + beside):
                    kv_ref[span, :] = ref[number, low:high, :]
    else:
        for which in range(8):
            for slot in range(4):
                for low, high, span in spans(slot_of(slot), which):
                    kv_ref[span, :] = kv_refs[0][which, slot, low:high, :]
    token_ids = lax.broadcasted_iota(jnp.int32, (whole, width), 0)
    key_lane = lax.broadcasted_iota(jnp.int32, (whole, width), 1)
    for slot in range(4):
        span = slice(slot * whole, (slot + 1) * whole)
        kvt_ref[:, span] = kv_ref[span, :].T
        acc_ref[span, :] = jnp.zeros((whole, width), jnp.float32)
        room = valid_rows - slot * (whole // 40)
        bound = jnp.where(token_ids < left, room * LEFT, left + room * (40 - LEFT))
        extra_ref[span, :] = jnp.where(
            key_lane < half,
            jnp.where(token_ids < bound, 0.0, LOWEST),
            pltpu.roll(kv_ref[span, :].astype(jnp.float32), half, 1),
        ).astype(jnp.bfloat16)
    qgs_ref[...] = jnp.zeros(qgs_ref.shape, jnp.bfloat16)
    rows_ref[...] = jnp.zeros(rows_ref.shape, jnp.bfloat16)
    for slot in range(4):
        start = pl.multiple_of(slot_of(slot) * pair, pair)
        span = slice((1 + which_image) * tokens, (2 + which_image) * tokens)
        qgs_ref[pl.ds(start, tokens), :] = mix_refs[slot][span, :]

    lane = lax.broadcasted_iota(jnp.int32, (block, width), 1)
    ones = (lax.broadcasted_iota(jnp.int32, (half, block), 0) == 0).astype(jnp.bfloat16)
    zeros = jnp.zeros((half, block), jnp.bfloat16)

    def query_block(number, _):
        qg = qgs_ref[pl.ds(pl.multiple_of(number * block, block), block), :]
        qgt = qg.T
        scaled = qgt[:half].astype(jnp.float32) * (scale * LOG2E)
        high = scaled.astype(jnp.bfloat16)
        rest = (scaled - high.astype(jnp.float32)).astype(jnp.bfloat16)
        score_rhs = jnp.concatenate([high, zeros, ones, rest], axis=0)

        def score_pass(size, chunk, best):
            rows = rows_of(chunk, size)
            lhs = jnp.concatenate([kv_ref[rows, :], extra_ref[rows, :]], axis=1)
            scores = jnp.dot(lhs, score_rhs, preferred_element_type=jnp.float32)
            s_ref[rows, :] = scores
            return jnp.maximum(best, jnp.max(scores.reshape(size // 8, 8, block), axis=0))

        best = jnp.full((8, block), LOWEST, jnp.float32)
        for size, trips in sizes:
            best = lax.fori_loop(0, trips, functools.partial(score_pass, size), best)
        peak = jnp.max(best, axis=0, keepdims=True)

        def weight_pass(size, chunk, carried):
            total, out_t = carried
            rows = rows_of(chunk, size)
            weights = jnp.exp2(s_ref[rows, :] - peak)
            total = total + jnp.sum(weights.reshape(size // 8, 8, block), axis=0)
            weights = weights.astype(jnp.bfloat16)
            p_ref[rows, :] = weights
            out_t = out_t + jnp.dot(
                kvt_ref[half:, rows], weights, preferred_element_type=jnp.float32
            )
            return total, out_t

        carried = (jnp.zeros((8, block), jnp.float32), jnp.zeros((half, block), jnp.float32))
        for size, trips in sizes:
            carried = lax.fori_loop(0, trips, functools.partial(weight_pass, size), carried)
        total, out_t = carried
        inverse = 1.0 / jnp.sum(total, axis=0, keepdims=True)
        out_t = out_t * inverse
        grad_t = qgt[half:].astype(jnp.float32) * inverse
        delta = jnp.sum(out_t * grad_t, axis=0, keepdims=True) * scale
        grad_rhs = jnp.concatenate([zeros, (grad_t * scale).astype(jnp.bfloat16)], axis=0)
        grad_rows = jnp.concatenate([jnp.zeros_like(grad_t), grad_t], axis=0).T
        out_rhs = jnp.concatenate(
            [jnp.where(lane < half, qg, jnp.zeros_like(qg)), grad_rows.astype(jnp.bfloat16)], axis=0
        )

        def grad_pass(size, chunk, dq_t):
            rows = rows_of(chunk, size)
            prob_grad = jnp.dot(kv_ref[rows, :], grad_rhs, preferred_element_type=jnp.float32)
            weights = p_ref[rows, :]
            score_grad = (weights.astype(jnp.float32) * (prob_grad - delta)).astype(jnp.bfloat16)
            acc_ref[rows, :] += jnp.dot(
                jnp.concatenate([score_grad, weights], axis=1),
                out_rhs,
                preferred_element_type=jnp.float32,
            )
            return dq_t + jnp.dot(
                kvt_ref[:half, rows], score_grad, preferred_element_type=jnp.float32
            )

        dq_t = jnp.zeros((half, block), jnp.float32)
        for size, trips in sizes:
            dq_t = lax.fori_loop(0, trips, functools.partial(grad_pass, size), dq_t)
        result = jnp.concatenate([dq_t, out_t], axis=0).T.astype(jnp.bfloat16)
        rows_ref[pl.ds(pl.multiple_of(number * block, block), block), :] = result
        return 0

    lax.fori_loop(0, jnp.where(trips > 2, 2, 1), query_block, 0)
    for slot in range(4):
        start = pl.multiple_of(slot_of(slot) * pair, pair)
        rows_refs[slot][...] = rows_ref[pl.ds(start, tokens), :]
    if outs == 1:
        for which in range(8):
            for slot in range(4):
                for low, high, span in spans(slot_of(slot), which):
                    dkv_refs[0][which, slot, low:high, :] = acc_ref[span, :].astype(jnp.bfloat16)
    else:
        for ref, beside in zip(dkv_refs, (core, 1 - core)):
            for number in range(16):
                for low, high, span in spans(number // 4, 2 * (number % 4) + beside):
                    ref[number, low:high, :] = acc_ref[span, :].astype(jnp.bfloat16)


def attend(which_image, info, mix, *kvs):
    width = mix[0].shape[-1]
    tokens = mix[0].shape[0] // 3
    keys = 8 * 4 * tokens
    block = 512
    vmem = pl.BlockSpec(memory_space=pltpu.VMEM)
    rows = jax.ShapeDtypeStruct((tokens, width), jnp.bfloat16)
    if len(kvs) == 2:
        grads = (jax.ShapeDtypeStruct((8, 4, tokens, width), jnp.bfloat16),)
    else:
        grads = (jax.ShapeDtypeStruct((16, tokens, width), jnp.bfloat16),) * 2
    arrays = [*mix, *kvs]
    results = pl.pallas_call(
        functools.partial(attention_kernel, which_image, len(kvs), block),
        out_shape=(rows,) * 4 + grads,
        in_specs=[pl.BlockSpec(memory_space=pltpu.SMEM)]
        + [vmem] * len(arrays),
        out_specs=(vmem,) * (4 + len(grads)),
        scratch_shapes=[
            pltpu.VMEM((keys, width), jnp.bfloat16),
            pltpu.VMEM((keys, width), jnp.bfloat16),
            pltpu.VMEM((width, keys), jnp.bfloat16),
            pltpu.VMEM((2 * block, width), jnp.bfloat16),
            pltpu.VMEM((2 * block, width), jnp.bfloat16),
            pltpu.VMEM((keys, block), jnp.float32),
            pltpu.VMEM((keys, block), jnp.bfloat16),
            pltpu.VMEM((keys, width), jnp.float32),
        ],
        compiler_params=pltpu.CompilerParams(vmem_limit_bytes=VMEM_ATTENTION),
        cost_estimate=pl.CostEstimate(
            flops=6 * 2 * 1024 * keys * 256,
            bytes_accessed=8 * 2**20,
            transcendentals=1024 * keys,
        ),
        name="attention",
    )(info, *arrays)
    return results[:4], *results[4:]


def per_device(
    image,
    embedding,
    cotangent,
    valid_rows,
    orientation,
    gn1_gain,
    gn1_bias,
    conv1_weight,
    conv1_bias,
    time_weight,
    time_bias,
    gn2_gain,
    gn2_bias,
    conv2_weight,
    conv2_bias,
    gn3_gain,
    gn3_bias,
    qkv_weight,
    qv_bias,
    proj_weight,
    proj_bias,
):
    images, shard_rows, columns, channels = image.shape
    tokens = shard_rows * columns
    head_width = channels // HEAD_COUNT
    seq_index = lax.axis_index("seq")
    dp_index = lax.axis_index("dp")
    places = {"x": seq_index // 8, "y": seq_index // 2 % 4, "c": seq_index % 2, "z": dp_index}
    place_x, place_y, place_c = places["x"], places["y"], places["c"]
    col_valid = columns - 2 * columns // 5 * orientation
    info = jnp.stack(
        [
            jnp.asarray(number, jnp.int32)
            for number in (
                seq_index * shard_rows,
                valid_rows[0],
                valid_rows[1],
                col_valid[0],
                col_valid[1],
                place_x,
                place_c,
                0,
            )
        ]
    )
    counts = (valid_rows * col_valid).astype(jnp.float32) * (channels // GROUPS)
    scalars = (info, counts)
    gain1, bias1, gain2, bias2, gain3, bias3, conv1_bias, conv2_bias, proj_bias = (
        value[None]
        for value in (
            gn1_gain, gn1_bias, gn2_gain, gn2_bias, gn3_gain, gn3_bias, conv1_bias, conv2_bias, proj_bias,
        )
    )
    taps = conv1_weight.shape
    conv1_weight = conv1_weight.reshape(-1, channels)
    conv2_weight = conv2_weight.reshape(-1, channels)
    wide, low_kind = jnp.float32, jnp.bfloat16
    field = (images, shard_rows, columns, channels)
    edges = (2, images, 2, columns, channels)
    extended_field = (images, shard_rows + 2, columns, channels)

    by_head = jnp.transpose(
        qkv_weight.reshape(channels, 3, HEAD_COUNT, head_width), (2, 1, 0, 3)
    )
    proj_heads = proj_weight.reshape(HEAD_COUNT, head_width, channels)
    blank = jnp.zeros((HEAD_COUNT, channels, head_width), low_kind)
    key_weight = jnp.concatenate([by_head[:, 1], by_head[:, 2]], axis=2)
    query_weight = jnp.concatenate(
        [
            jnp.concatenate([by_head[:, 0], blank], axis=2),
            jnp.concatenate([blank, jnp.swapaxes(proj_heads, 1, 2)], axis=2),
        ],
        axis=1,
    )
    blank_rows = jnp.swapaxes(blank, 1, 2)
    turned = jnp.swapaxes(by_head, 2, 3)
    key_weight_t = jnp.concatenate([turned[:, 1], turned[:, 2]], axis=1)
    query_weight_t = jnp.concatenate([turned[:, 0], blank_rows], axis=1)
    proj_weight_t = jnp.concatenate([blank_rows, proj_heads], axis=1)
    head_bias = qv_bias.reshape(2, HEAD_COUNT, 1, head_width)
    blank_bias = jnp.zeros((HEAD_COUNT, 1, head_width), wide)
    query_bias = jnp.concatenate([head_bias[0], blank_bias], axis=2)
    key_bias = jnp.concatenate([blank_bias, head_bias[1]], axis=2)

    time_input = jax.nn.silu(embedding.astype(wide)).astype(low_kind)
    shifts = jnp.dot(time_input, time_weight, preferred_element_type=wide) + time_bias

    first_edges, last_edges, sums1 = run_kernel(
        start_kernel,
        (info,),
        (),
        ((edges, low_kind), (edges, low_kind), ((4, channels), wide)),
        early=(image, cotangent),
    )
    low_edges, high_edges = row_shift(last_edges, 1), row_shift(first_edges, -1)
    sums1 = seq_total(sums1)
    active1, hidden, sums2 = run_kernel(
        hidden_kernel,
        scalars,
        (low_edges, high_edges, sums1, gain1, bias1, conv1_bias, image, conv1_weight),
        ((extended_field, low_kind), (extended_field, wide), ((4, channels), wide)),
    )
    sums2 = seq_total(sums2)
    active2, residual, sums3 = run_kernel(
        residual_kernel,
        scalars,
        (hidden, sums2, gain2, bias2, shifts, conv2_bias, image, conv2_weight),
        ((extended_field, low_kind), (field, wide), ((4, channels), wide)),
    )
    sums3 = seq_total(sums3)

    third, proj_grad, placed_a, *slots = run_kernel(
        mixture_kernel,
        scalars,
        (residual, sums3, gain3, bias3, key_weight, query_weight, key_bias, query_bias),
        (((images * tokens, channels), low_kind),) * 2
        + (((16, tokens, 2 * head_width), low_kind),)
        + (((3 * tokens, 2 * head_width), low_kind),) * HEAD_COUNT,
        early=(cotangent,),
    )
    column = swap_places(placed_a)
    mix = [slots[0]] + [seq_shift(slots[d], d, 0, 0) for d in range(1, 4)]
    groups = [[x * 8 + place for place in range(8)] for x in range(4)]
    beside = seq_shift(column, 0, 0, 1)
    own_b = jnp.stack([part[:tokens] for part in mix])
    gathered_b = lax.all_gather(own_b, "seq", axis_index_groups=groups)
    rows_a, keys_a = attend(0, info, mix, column, beside)
    keys_a = lax.psum_scatter(keys_a, "seq", scatter_dimension=0, axis_index_groups=groups)
    rows_b, own_b, beside_b = attend(1, info, mix, gathered_b)
    keys_b = swap_places(low_sum(own_b, seq_shift(beside_b, 0, 0, 1)))

    rows = [jnp.stack(pair) for pair in zip(rows_a, rows_b)]
    rows = [rows[0]] + [seq_shift(rows[d], 4 - d, 0, 0) for d in range(1, 4)]
    keys_a = [keys_a[0]] + [seq_shift(keys_a[d], 4 - d, 0, 0) for d in range(1, 4)]
    output, third_grad, third_first, third_last, sums4, early_rest = run_kernel(
        output_kernel,
        scalars,
        (
            sums3, gain3, proj_bias, *rows, *keys_a, keys_b,
        ),
        (
            (field, low_kind), (field, wide), (edges, wide), (edges, wide), ((7, channels), wide),
            ((4, 2, HEAD_COUNT, head_width, channels // 2), low_kind),
        ),
        scratch=(pltpu.VMEM((2 * channels, 2 * head_width), wide),),
        early=(third, proj_grad, query_weight_t, key_weight_t, proj_weight_t),
        late=(residual,),
    )
    low_third, high_third = row_shift(third_last, 1), row_shift(third_first, -1)
    sums4 = seq_total(sums4)
    residual_grad, early, norm2_grad, sums5 = run_kernel(
        branch_kernel,
        scalars,
        (
            low_third, high_third, low_edges, high_edges, sums3, gain3, sums4, sums2, gain2, bias2, shifts,
        ),
        (
            (field, wide), ((4, 2, 4, 208, channels // 2), low_kind), (extended_field, wide), ((5, channels), wide),
        ),
        early=(third_grad, residual, cotangent),
        late=(hidden, active2, conv2_weight, early_rest),
    )
    early = lax.psum_scatter(
        early.reshape((8,) + early.shape[2:]), "seq", scatter_dimension=0, axis_index_groups=groups
    )
    sums5 = seq_total(sums5)
    conv1_grad, norm1_grad, sums6 = run_kernel(
        hidden_grad_kernel,
        scalars,
        (
            sums2, gain2, shifts, sums5, sums1, gain1, bias1,
        ),
        (((2, 16, 144, channels // 2), low_kind), (field, wide), ((5, channels), wide)),
        early=(norm2_grad, hidden),
        late=(image, active1, conv1_weight),
    )
    late, sums6 = sums_over_seq(conv1_grad, sums6, places)
    early = scatter_ring(early, "x", place_x)
    both = jnp.concatenate([late, early])
    (image_grad,) = run_kernel(
        image_grad_kernel,
        scalars,
        (sums1, gain1, sums6),
        ((field, low_kind),),
        early=(image, norm1_grad, residual_grad),
    )

    scaling = shifts[:, :channels]
    scale_total = gain2 * sums5[2:4] + bias2 * sums5[:2]
    shift_low = jnp.concatenate([scale_total, sums5[:2]], axis=-1).astype(low_kind)
    embedding_grad = jnp.einsum(
        "ik,ek->ie", shift_low, time_weight, preferred_element_type=wide
    ) * silu_slope(embedding.astype(wide))
    rows = [
        sums6[2] + sums6[3],
        sums6[0] + sums6[1],
        sums6[4],
        jnp.sum((1.0 + scaling) * sums5[2:4], axis=0),
        jnp.sum((1.0 + scaling) * sums5[:2], axis=0),
        sums5[4],
        sums4[2] + sums4[3],
        sums4[0] + sums4[1],
        sums4[4],
        sums4[5],
        sums4[6],
    ]
    time_pair = jnp.concatenate([time_input, shift_low], axis=-1)
    both, totals, every_pair = sums_over_dp(
        both, jnp.stack(rows), time_pair.reshape(-1, channels // 2), places
    )
    every_input, every_shift = jnp.split(
        every_pair.reshape(-1, time_pair.shape[-1]), (time_input.shape[-1],), axis=-1
    )
    time_weight_grad = jnp.einsum(
        "ie,ik->ek", every_input, every_shift, preferred_element_type=wide
    )
    time_bias_grad = jnp.sum(every_shift, axis=0, dtype=wide)
    parts = gathered_over_seq(both, places)
    conv1_total, conv2_total, qkv_total, proj_total = run_kernel(
        weights_kernel,
        (info,),
        parts,
        (
            (conv1_weight.shape, wide), (conv2_weight.shape, wide), ((channels, 3 * channels), wide),
            ((channels, channels), wide),
        ),
        scratch=(pltpu.VMEM((4 * channels, channels), wide),),
    )
    return (
        output,
        image_grad,
        embedding_grad,
        totals[0],
        totals[1],
        conv1_total.reshape(taps),
        totals[2],
        time_weight_grad,
        time_bias_grad,
        totals[3],
        totals[4],
        conv2_total.reshape(taps),
        totals[5],
        totals[6],
        totals[7],
        qkv_total,
        jnp.concatenate([totals[8], totals[9]]),
        proj_total,
        totals[10],
    )


def solution(mesh):
    return jax.shard_map(
        per_device,
        mesh=mesh,
        in_specs=(
            P("dp", "seq", None, None),
            P("dp", None),
            P("dp", "seq", None, None),
            P("dp"),
            P("dp"),
            P(),
            P(),
            P(),
            P(),
            P(),
            P(),
            P(),
            P(),
            P(),
            P(),
            P(),
            P(),
            P(),
            P(),
            P(),
            P(),
        ),
        out_specs=(
            P("dp", "seq", None, None),
            P("dp", "seq", None, None),
            P("dp", None),
            P(),
            P(),
            P(),
            P(),
            P(),
            P(),
            P(),
            P(),
            P(),
            P(),
            P(),
            P(),
            P(),
            P(),
            P(),
            P(),
        ),
        check_vma=False,
    )
```

```python
import functools

import jax
import jax.numpy as jnp
from jax import lax
from jax.experimental import pallas as pl
from jax.experimental.pallas import tpu as pltpu
from jax.sharding import PartitionSpec as P

GROUPS = 32
HEAD_COUNT = 4


EPS = 1e-05
LOWEST = -1e30
LOG2E = 1.4426950408889634

LEFT = 24

VMEM_CONV = 24 * 2**20
VMEM_ATTENTION = 44 * 2**20


def seq_shift(value, dx, dy, dc):
    pairs = []
    for place in range(32):
        x, y, c = place // 8, place // 2 % 4, place % 2
        pairs.append((place, (x + dx) % 4 * 8 + (y + dy) % 4 * 2 + (c + dc) % 2))
    return lax.ppermute(value, "seq", pairs)


def axis_shift(value, axis, step):
    if axis == "x":
        return seq_shift(value, step, 0, 0)
    if axis == "y":
        return seq_shift(value, 0, step, 0)
    return lax.ppermute(value, "dp", [(i, (i + step) % 4) for i in range(4)])


def swap_edges(core_edges, next_edges):
    pairs = [(i, (i + 1) % 32 if i % 2 else (i - 1) % 32) for i in range(32)]
    return seq_shift(core_edges, 0, 0, 1), lax.ppermute(next_edges, "seq", pairs)


def swap_places(value):
    groups = [[place * 2 + core for place in range(16)] for core in range(2)]
    return lax.all_to_all(value, "seq", 0, 0, axis_index_groups=groups)


def seq_total(value, beside=None):
    value = value + seq_shift(value, 0, 0, 1)
    swapped = swap_places(jnp.broadcast_to(value[None], (16,) + value.shape))
    if beside is None:
        return jnp.sum(swapped, axis=0)
    swapped, beside = lax.optimization_barrier((swapped, beside))
    return jnp.sum(swapped, axis=0), beside


def core_total(value, c):
    return low_sum(take_slot(value, c), seq_shift(take_slot(value, 1 - c), 0, 0, 1))


def take_slot(value, slot):
    return lax.dynamic_index_in_dim(value, slot, 0, keepdims=False)


def low_sum(*parts):
    total = parts[0].astype(jnp.float32)
    for part in parts[1:]:
        total = total + part.astype(jnp.float32)
    return total.astype(jnp.bfloat16)


def scatter_ring(value, axis, place):
    return low_sum(
        take_slot(value, place),
        *(axis_shift(take_slot(value, (place + step) % 4), axis, step) for step in (1, 3, 2)),
    )


def gather_ring(value, axis, place):
    result = jnp.zeros((4,) + value.shape, value.dtype)
    result = lax.dynamic_update_index_in_dim(result, value, place, 0)
    for step in (1, 3, 2):
        result = lax.dynamic_update_index_in_dim(
            result, axis_shift(value, axis, step), (place - step) % 4, 0
        )
    return result


def split_low(value):
    high = value.astype(jnp.bfloat16)
    both = jnp.concatenate([high, (value - high.astype(jnp.float32)).astype(jnp.bfloat16)])
    both = both.reshape(-1, 128)
    return jnp.pad(both, ((0, -both.shape[0] % 16), (0, 0)))


def join_low(value, rows):
    value = value[: 4 * rows].astype(jnp.float32).reshape(2, rows, 256)
    return value[0] + value[1]


def paired(parts):
    return (parts[0] + parts[2]) + (parts[1] + parts[3])


def sums_over_seq(late, vector, early, places):
    late = core_total(late, places["c"])
    low = split_low(vector + seq_shift(vector, 0, 0, 1))
    swapped = swap_places(
        jnp.concatenate([late, jnp.broadcast_to(low[None], (16,) + low.shape)], axis=1)
    )
    early = scatter_ring(early, "x", places["x"])
    swapped, early = lax.optimization_barrier((swapped, early))
    total = jnp.sum(swapped.astype(jnp.float32), axis=0)
    count = late.shape[1]
    return total[:count].astype(jnp.bfloat16), early, join_low(total[count:], vector.shape[0])


def sums_over_dp(both, vector, extra, places):
    low = split_low(vector)
    sent = jnp.concatenate([both, low, extra])
    got = [sent] + [axis_shift(sent, "z", step) for step in (1, 2, 3)]
    count = both.shape[0]
    both = paired([part[:count].astype(jnp.float32) for part in got]).astype(jnp.bfloat16)
    count += low.shape[0]
    vector = paired(
        [join_low(part[count - low.shape[0] : count], vector.shape[0]) for part in got]
    )
    extras = jnp.zeros((4,) + extra.shape, extra.dtype)
    for step in range(4):
        extras = lax.dynamic_update_index_in_dim(
            extras, got[step][count:], (places["z"] - step) % 4, 0
        )
    return both, vector, extras


def gathered_over_seq(both, places):
    both = gather_ring(both, "y", places["y"])
    both = gather_ring(both, "x", places["x"]).reshape((16, -1) + both.shape[2:])
    return both, seq_shift(both, 0, 0, 1)


def silu_slope(values):
    sigmoid = jax.nn.sigmoid(values)
    return sigmoid * (1.0 + values * (1.0 - sigmoid))


def same_group(channels):
    size = channels // GROUPS
    rows = lax.broadcasted_iota(jnp.int32, (channels, channels), 0) // size
    cols = lax.broadcasted_iota(jnp.int32, (channels, channels), 1) // size
    return (rows == cols).astype(jnp.float32)


def over_group(sums, channels):
    return jnp.dot(
        sums, same_group(channels), precision=lax.Precision.HIGHEST, preferred_element_type=jnp.float32
    )


def norm_terms(sums, counts_ref):
    totals = over_group(sums[:4], sums.shape[-1])
    terms = []
    for i in range(2):
        average = totals[i : i + 1] / counts_ref[i]
        spread = lax.rsqrt(totals[2 + i : 3 + i] / counts_ref[i] - average * average + EPS)
        terms.append((average, spread))
    return terms


def mask_of(info_ref, i, shape, border):
    rows = lax.broadcasted_iota(jnp.int32, shape, 0) + (info_ref[0] - border)
    cols = lax.broadcasted_iota(jnp.int32, shape, 1)
    valid = (rows >= 0) & (rows < info_ref[1 + i]) & (cols < info_ref[3 + i])
    return valid.astype(jnp.float32)


def extended(edges, own):
    low, high = edges
    return jnp.concatenate([low, own.astype(jnp.float32), high], axis=0)


def shifted(values):
    rows, columns, channels = values.shape
    cols = lax.broadcasted_iota(jnp.int32, values.shape, 1).reshape(-1, channels)
    flat = values.reshape(-1, channels)
    before = jnp.where(cols == 0, 0.0, pltpu.roll(flat, 1, 0))
    after = jnp.where(cols == columns - 1, 0.0, pltpu.roll(flat, rows * columns - 1, 0))
    return before, flat, after


def tap_rows(images, a, b, rows, columns=40):
    return jnp.concatenate(
        [image[b][a * columns : (a + rows) * columns] for image in images], axis=0
    ).astype(jnp.bfloat16)


def conv_taps(images, weight_ref, rows):
    patches = jnp.concatenate(
        [tap_rows(images, a, b, rows) for a in range(3) for b in range(3)], axis=1
    )
    return jnp.dot(patches, weight_ref[...], preferred_element_type=jnp.float32)


def put_rows(ref, first, values):
    rows = 9 * values.shape[1] // 16
    width = ref.shape[-1]
    last = first + values.shape[0]
    while first < last:
        place, low = divmod(first, rows)
        count = min(rows - low, last - first)
        for core in range(2):
            part = values[:count, core * width : (core + 1) * width].astype(jnp.bfloat16)
            if len(ref.shape) == 4:
                ref[core, place, low : low + count, :] = part
            else:
                ref[place // 4, core, place % 4, low : low + count, :] = part
        values = values[count:]
        first += count


def conv_grads(images, rows, actives, weight_ref, low, weight_grad_ref):
    total = None
    channels = low.shape[-1]
    for a in range(3):
        for b in range(3):
            span = slice((3 * a + b) * channels, (3 * a + b + 1) * channels)
            put_rows(
                weight_grad_ref,
                span.start,
                lax.dot_general(
                    tap_rows(actives, a, b, 6),
                    low,
                    (((0,), (0,)), ((), ())),
                    preferred_element_type=jnp.float32,
                ),
            )
            part = lax.dot_general(
                tap_rows(images, 2 - a, 2 - b, rows),
                weight_ref[span, :],
                (((1,), (1,)), ((), ())),
                preferred_element_type=jnp.float32,
            )
            total = part if total is None else total + part
    return total


def put_sums(ref, rows):
    for place, row in enumerate(rows):
        ref[place : place + 1, :] = row


def column_sum(values):
    return jnp.sum(values.reshape(-1, values.shape[-1]), axis=0, keepdims=True)


def put_edges(info_ref, core_ref, next_ref, which, i, first, last):
    first, last = first.astype(jnp.float32), last.astype(jnp.float32)
    low_core = info_ref[6] == 0
    core_ref[which, i] = jnp.where(low_core, last, first).astype(core_ref.dtype)
    next_ref[which, i] = jnp.where(low_core, first, last).astype(core_ref.dtype)


def edges_of(info_ref, core_ref, next_ref, which, i):
    low_core = info_ref[6] == 0
    core = core_ref[which, i].astype(jnp.float32)
    beyond = next_ref[which, i].astype(jnp.float32)
    return jnp.where(low_core, beyond, core), jnp.where(low_core, core, beyond)


def start_kernel(info_ref, image_ref, cotangent_ref, core_ref, next_ref, out_sums_ref):
    first, second = [], []
    for i in range(2):
        image = image_ref[i]
        cotangent = cotangent_ref[i]
        put_edges(info_ref, core_ref, next_ref, 0, i, image[:2], image[-2:])
        put_edges(info_ref, core_ref, next_ref, 1, i, cotangent[:2], cotangent[-2:])
        values = mask_of(info_ref, i, image.shape, 0) * image.astype(jnp.float32)
        first.append(column_sum(values))
        second.append(column_sum(values * values))
    put_sums(out_sums_ref, first + second)


def hidden_kernel(
    info_ref, counts_ref, core_ref, next_ref, sums_ref, gain_ref, bias_ref, conv_bias_ref, own_ref, weight_ref,
    active_ref, hidden_ref, out_sums_ref,
):
    terms = norm_terms(sums_ref[...], counts_ref)
    images = []
    for i in range(2):
        values = extended(edges_of(info_ref, core_ref, next_ref, 0, i), own_ref[i])
        mask = mask_of(info_ref, i, values.shape, 2)
        average, spread = terms[i]
        hat = mask * ((mask * values - average) * spread)
        active = jax.nn.silu(mask * (hat * gain_ref[...] + bias_ref[...])).astype(jnp.bfloat16)
        active_ref[i] = active[1:-1]
        images.append(shifted(active.astype(jnp.float32)))
    conv = conv_taps(images, weight_ref, 8)
    first, second = [], []
    for i in range(2):
        shape = hidden_ref.shape[1:]
        mask = mask_of(info_ref, i, shape, 1)
        half = conv.shape[0] // 2
        hidden = mask * (conv[i * half : (i + 1) * half].reshape(shape) + conv_bias_ref[...])
        hidden_ref[i] = hidden
        hidden = hidden[1:-1]
        first.append(column_sum(hidden))
        second.append(column_sum(hidden * hidden))
    put_sums(out_sums_ref, first + second)


def second_norm_of(values, mask, term, gain, bias, shifts_ref, i):
    channels = values.shape[-1]
    average, spread = term
    hat = mask * ((values - average) * spread)
    base = mask * (hat * gain + bias)
    scaling = shifts_ref[i : i + 1, :channels]
    offset = shifts_ref[i : i + 1, channels:]
    return hat, mask * (base * (1.0 + scaling) + offset)


def residual_kernel(
    info_ref, counts_ref, hidden_ref, sums_ref, gain_ref, bias_ref, shifts_ref, conv_bias_ref, image_ref, weight_ref,
    active_ref, residual_ref, out_sums_ref,
):
    terms = norm_terms(sums_ref[...], counts_ref)
    images = []
    for i in range(2):
        values = hidden_ref[i]
        mask = mask_of(info_ref, i, values.shape, 1)
        _, norm = second_norm_of(
            values, mask, terms[i], gain_ref[...], bias_ref[...], shifts_ref, i
        )
        active = jax.nn.silu(norm).astype(jnp.bfloat16)
        active_ref[i] = active
        images.append(shifted(active.astype(jnp.float32)))
    conv = conv_taps(images, weight_ref, 6)
    first, second = [], []
    for i in range(2):
        shape = residual_ref.shape[1:]
        mask = mask_of(info_ref, i, shape, 0)
        half = conv.shape[0] // 2
        residual = mask * image_ref[i].astype(jnp.float32) + mask * (
            conv[i * half : (i + 1) * half].reshape(shape) + conv_bias_ref[...]
        )
        residual_ref[i] = residual
        first.append(column_sum(residual))
        second.append(column_sum(residual * residual))
    put_sums(out_sums_ref, first + second)


def to_parts(values):
    channels = values.shape[-1]
    return jnp.concatenate(
        [values[:, :LEFT].reshape(-1, channels), values[:, LEFT:].reshape(-1, channels)], axis=0
    )


def from_parts(values, shape):
    rows, columns, channels = shape
    edge = rows * LEFT
    return jnp.concatenate(
        [
            values[:edge].reshape(rows, LEFT, channels),
            values[edge:].reshape(rows, columns - LEFT, channels),
        ],
        axis=1,
    )


def mixture_kernel(
    info_ref, counts_ref, residual_ref, sums_ref, gain_ref, bias_ref, key_weight_ref, query_weight_ref,
    key_bias_ref, query_bias_ref, cotangent_ref, third_ref, grad_ref, first_ref, *slot_refs,
):
    terms = norm_terms(sums_ref[...], counts_ref)
    tokens = third_ref.shape[0] // 2
    for i in range(2):
        values = residual_ref[i]
        mask = mask_of(info_ref, i, values.shape, 0)
        average, spread = terms[i]
        hat = mask * ((values - average) * spread)
        span = slice(i * tokens, (i + 1) * tokens)
        third_ref[span, :] = to_parts(mask * (hat * gain_ref[...] + bias_ref[...])).astype(
            jnp.bfloat16
        )
        grad_ref[span, :] = to_parts(mask * cotangent_ref[i].astype(jnp.float32)).astype(
            jnp.bfloat16
        )
    third = third_ref[...]
    both = jnp.concatenate([third, grad_ref[...]], axis=1)
    for head in range(HEAD_COUNT):
        keys = (
            jnp.dot(third[:tokens], key_weight_ref[head], preferred_element_type=jnp.float32)
            + key_bias_ref[head]
        ).astype(jnp.bfloat16)
        for place in range(4):
            first_ref[4 * head + place] = keys
    for slot, ref in enumerate(slot_refs):
        head = lax.rem(info_ref[5] + slot, HEAD_COUNT)
        keys = (
            jnp.dot(third[tokens:], key_weight_ref[head], preferred_element_type=jnp.float32)
            + key_bias_ref[head]
        ).astype(jnp.bfloat16)
        queries = (
            jnp.dot(both, query_weight_ref[head], preferred_element_type=jnp.float32)
            + query_bias_ref[head]
        ).astype(jnp.bfloat16)
        ref[:tokens, :] = keys
        ref[tokens:, :] = queries


def output_kernel(
    info_ref, counts_ref, sums_ref, gain_ref, proj_bias_ref, *refs,
):
    row_refs, first_refs, key_ref, refs = refs[:4], refs[4:8], refs[8], refs[9:]
    third_ref, grad_ref, query_weight_ref, key_weight_ref, proj_weight_ref, residual_ref, *refs = refs
    output_ref, third_grad_ref, core_ref, next_ref, out_sums_ref, early_ref, columns_ref, wait = refs
    tokens, channels = third_ref.shape
    width = channels // 2
    head_width = channels // HEAD_COUNT
    third = third_ref[...]
    proj_grad = grad_ref[...]
    ones = jnp.ones((tokens, width), jnp.bfloat16)
    row_rhs = jnp.concatenate([third, proj_grad, ones], axis=1)
    key_rhs = jnp.concatenate([third, ones], axis=1)
    projected = None
    third_grad = None
    transposed = (((0,), (0,)), ((), ()))
    for slot in range(HEAD_COUNT):
        head = lax.rem(info_ref[5] + slot, HEAD_COUNT)
        rows = row_refs[slot][...].reshape(tokens, width)
        last = key_ref[pl.ds(pl.multiple_of(4 * head, 4), 4)].astype(jnp.float32)
        keys = jnp.concatenate(
            [first_refs[slot][...], jnp.sum(last, axis=0).astype(jnp.bfloat16)], axis=0
        )
        part = jnp.dot(rows, proj_weight_ref[head], preferred_element_type=jnp.float32)
        projected = part if projected is None else projected + part
        part = jnp.dot(
            jnp.concatenate([rows, keys], axis=1),
            jnp.concatenate([query_weight_ref[head], key_weight_ref[head]], axis=0),
            preferred_element_type=jnp.float32,
        )
        third_grad = part if third_grad is None else third_grad + part
        row_grad = lax.dot_general(rows, row_rhs, transposed, preferred_element_type=jnp.float32)
        key_grad = lax.dot_general(keys, key_rhs, transposed, preferred_element_type=jnp.float32)
        start = pl.multiple_of(head * head_width, head_width)
        for place, block in (
            (0, row_grad[:head_width, :channels]),
            (channels, key_grad[:head_width, :channels]),
            (2 * channels, key_grad[head_width:, :channels]),
            (3 * channels, row_grad[head_width:, channels : 2 * channels]),
        ):
            for core in range(2):
                early_ref[place // channels, core, head] = block[
                    :, core * width : (core + 1) * width
                ].astype(jnp.bfloat16)
        columns_ref[pl.ds(start, head_width), :] = row_grad[:head_width, 2 * channels :]
        columns_ref[pl.ds(channels + start, head_width), :] = key_grad[head_width:, channels:]
    terms = norm_terms(sums_ref[...], counts_ref)
    wait()
    first, second = [], []
    for i in range(2):
        shape = residual_ref.shape[1:]
        span = slice(i * (tokens // 2), (i + 1) * (tokens // 2))
        values = residual_ref[i]
        mask = mask_of(info_ref, i, shape, 0)
        output_ref[i] = (
            values + mask * from_parts(projected[span] + proj_bias_ref[...], shape)
        ).astype(jnp.bfloat16)
        average, spread = terms[i]
        hat = mask * ((values - average) * spread)
        grad = mask * from_parts(third_grad[span], shape)
        third_grad_ref[i] = grad
        put_edges(info_ref, core_ref, next_ref, 0, i, grad[:2], grad[-2:])
        put_edges(info_ref, core_ref, next_ref, 1, i, values[:2], values[-2:])
        first.append(column_sum(grad))
        second.append(column_sum(grad * hat))
    query_row = columns_ref[:channels, :].T[:1]
    value_row = columns_ref[channels:, :].T[:1]
    put_sums(
        out_sums_ref,
        first + second + [query_row, value_row, column_sum(proj_grad.astype(jnp.float32))],
    )


def norm_grad_means(grad_sums, counts_ref, factors):
    rows = [grad_sums[i : i + 1] * factors[i] for i in range(2)]
    rows += [grad_sums[2 + i : 3 + i] * factors[i] for i in range(2)]
    totals = over_group(
        jnp.concatenate(rows, axis=0), rows[0].shape[-1]
    )
    return [
        (totals[i : i + 1] / counts_ref[i], totals[2 + i : 3 + i] / counts_ref[i])
        for i in range(2)
    ]


def branch_kernel(
    info_ref, counts_ref, core_ref, next_ref, cot_core_ref, cot_next_ref, sums3_ref, gain3_ref, sums4_ref, sums2_ref,
    gain2_ref, bias2_ref, shifts_ref, grad_ref, residual_ref, cot_ref, hidden_ref, active_ref, weight_ref, rest_ref,
    residual_grad_ref, weight_grad_ref, norm_grad_ref, out_sums_ref, wait,
):
    terms = norm_terms(sums3_ref[...], counts_ref)
    gain = gain3_ref[...]
    means = norm_grad_means(sums4_ref[...], counts_ref, [gain, gain])
    images, actives, lows = [], [], []
    shape = hidden_ref.shape[1:]
    channels = shape[-1]
    for i in range(2):
        grad = extended(edges_of(info_ref, core_ref, next_ref, 0, i), grad_ref[i])
        values = extended(edges_of(info_ref, core_ref, next_ref, 1, i), residual_ref[i])
        mask = mask_of(info_ref, i, values.shape, 2)
        average, spread = terms[i]
        hat = mask * ((values - average) * spread)
        first_mean, second_mean = means[i]
        residual_grad = extended(
            edges_of(info_ref, cot_core_ref, cot_next_ref, 1, i), cot_ref[i]
        ) + mask * (spread * (grad * gain - first_mean - hat * second_mean))
        residual_grad_ref[i] = residual_grad[2:-2]
        low = (mask * residual_grad).astype(jnp.bfloat16).astype(jnp.float32)
        images.append(shifted(low))
        lows.append(low[2:-2].reshape(-1, channels))
    wait()
    for i in range(2):
        actives.append(shifted(active_ref[i].astype(jnp.float32)))
    low = jnp.concatenate(lows, axis=0)
    total = conv_grads(images, 8, actives, weight_ref, low.astype(jnp.bfloat16), weight_grad_ref)
    terms = norm_terms(sums2_ref[...], counts_ref)
    first, second = [], []
    for i in range(2):
        mask = mask_of(info_ref, i, shape, 1)
        hat, norm = second_norm_of(
            hidden_ref[i], mask, terms[i], gain2_ref[...], bias2_ref[...], shifts_ref, i
        )
        half = total.shape[0] // 2
        grad = mask * total[i * half : (i + 1) * half].reshape(shape) * silu_slope(norm)
        norm_grad_ref[i] = grad
        grad, hat = grad[1:-1], hat[1:-1]
        first.append(column_sum(grad))
        second.append(column_sum(grad * hat))
    put_sums(out_sums_ref, first + second + [column_sum(low)])
    weight_grad_ref[:, :, :, -rest_ref.shape[3] :, :] = rest_ref[...]


def hidden_grad_kernel(
    info_ref, counts_ref, sums2_ref, gain2_ref, shifts_ref, sums5_ref, sums1_ref, gain1_ref, bias1_ref,
    grad_ref, hidden_ref, image_ref, active_ref, weight_ref,
    weight_grad_ref, norm_grad_ref, out_sums_ref, wait,
):
    terms = norm_terms(sums2_ref[...], counts_ref)
    shape = image_ref.shape[1:]
    channels = shape[-1]
    factors = [(1.0 + shifts_ref[i : i + 1, :channels]) * gain2_ref[...] for i in range(2)]
    means = norm_grad_means(sums5_ref[...], counts_ref, factors)
    images, actives, lows = [], [], []
    for i in range(2):
        grad = grad_ref[i]
        values = hidden_ref[i]
        mask = mask_of(info_ref, i, values.shape, 1)
        average, spread = terms[i]
        hat = mask * ((values - average) * spread)
        first_mean, second_mean = means[i]
        low = mask * (spread * (grad * factors[i] - first_mean - hat * second_mean))
        low = low.astype(jnp.bfloat16).astype(jnp.float32)
        images.append(shifted(low))
        lows.append(low[1:-1].reshape(-1, channels))
    wait()
    for i in range(2):
        actives.append(shifted(active_ref[i].astype(jnp.float32)))
    low = jnp.concatenate(lows, axis=0)
    total = conv_grads(images, 6, actives, weight_ref, low.astype(jnp.bfloat16), weight_grad_ref)
    terms = norm_terms(sums1_ref[...], counts_ref)
    first, second = [], []
    for i in range(2):
        mask = mask_of(info_ref, i, shape, 0)
        average, spread = terms[i]
        hat = mask * ((mask * image_ref[i].astype(jnp.float32) - average) * spread)
        norm = mask * (hat * gain1_ref[...] + bias1_ref[...])
        half = total.shape[0] // 2
        grad = mask * total[i * half : (i + 1) * half].reshape(shape) * silu_slope(norm)
        norm_grad_ref[i] = grad
        first.append(column_sum(grad))
        second.append(column_sum(grad * hat))
    put_sums(out_sums_ref, first + second + [column_sum(low)])


def image_grad_kernel(
    info_ref, counts_ref, sums1_ref, gain1_ref, sums6_ref, image_ref, grad_ref, residual_grad_ref, out_ref
):
    terms = norm_terms(sums1_ref[...], counts_ref)
    gain = gain1_ref[...]
    means = norm_grad_means(sums6_ref[...], counts_ref, [gain, gain])
    for i in range(2):
        shape = image_ref.shape[1:]
        mask = mask_of(info_ref, i, shape, 0)
        average, spread = terms[i]
        hat = mask * ((mask * image_ref[i].astype(jnp.float32) - average) * spread)
        first_mean, second_mean = means[i]
        result = residual_grad_ref[i] + mask * (
            spread * (grad_ref[i] * gain - first_mean - hat * second_mean)
        )
        out_ref[i] = (mask * result).astype(jnp.bfloat16)


def weights_kernel(
    info_ref, own_ref, beside_ref, conv1_out, conv2_out, qkv_out, proj_out, conv1_ref, conv2_ref, qkv_ref, proj_ref,
    rest_ref, sems,
):
    channels = proj_ref.shape[0]
    width = channels // 2
    taps = conv1_ref.shape[0] // 16
    rest = 4 * channels // 16
    low_core = info_ref[6] == 0

    def write(first, count, target, in_order):
        def fill(refs):
            for core, ref in enumerate(refs):
                columns = slice(core * width, (core + 1) * width)
                for place in range(16):
                    number = place if in_order else place % 4 * 4 + place // 4
                    target[number * count : (number + 1) * count, columns] = ref[
                        place, first : first + count, :
                    ].astype(jnp.float32)

        @pl.when(low_core)
        def _():
            fill((own_ref, beside_ref))

        @pl.when(jnp.logical_not(low_core))
        def _():
            fill((beside_ref, own_ref))

    write(0, taps, conv1_ref, True)
    copies = [pltpu.make_async_copy(conv1_ref, conv1_out, sems.at[0])]
    copies[0].start()
    write(taps, taps, conv2_ref, False)
    copies.append(pltpu.make_async_copy(conv2_ref, conv2_out, sems.at[1]))
    copies[1].start()
    write(2 * taps, rest, rest_ref, False)
    for part in range(3):
        span = slice(part * channels, (part + 1) * channels)
        qkv_ref[:, span] = rest_ref[span, :].T
    proj_ref[...] = rest_ref[3 * channels :, :]
    copies.append(pltpu.make_async_copy(qkv_ref, qkv_out, sems.at[2]))
    copies.append(pltpu.make_async_copy(proj_ref, proj_out, sems.at[3]))
    copies[2].start()
    copies[3].start()
    for copy in copies:
        copy.wait()


def fetching(kernel, n_in, early, late, n_out):
    def body(*refs):
        count = early + late
        ins, refs = refs[:n_in], refs[n_in:]
        sources, refs = refs[:count], refs[count:]
        outs, refs = refs[:n_out], refs[n_out:]
        buffers, refs = refs[:count], refs[count:]
        sems, refs = refs[0], refs[1:]
        copies = [
            pltpu.make_async_copy(source, buffer, sems.at[number])
            for number, (source, buffer) in enumerate(zip(sources, buffers))
        ]
        for copy in copies:
            copy.start()
        for copy in copies[:early]:
            copy.wait()

        def wait():
            for copy in copies[early:]:
                copy.wait()

        kernel(*ins, *buffers, *outs, *refs, *((wait,) if late else ()))

    return body


def in_hbm(arrays):
    return [pltpu.with_memory_space_constraint(array, pltpu.HBM) for array in arrays]


def buffers_of(arrays):
    return [pltpu.VMEM(array.shape, array.dtype) for array in arrays] + [
        pltpu.SemaphoreType.DMA((len(arrays),))
    ]


def run_kernel(kernel, scalars, arrays, outs, scratch=(), early=(), late=()):
    vmem = pl.BlockSpec(memory_space=pltpu.VMEM)
    smem = pl.BlockSpec(memory_space=pltpu.SMEM)
    hbm = pl.BlockSpec(memory_space=pltpu.HBM)
    fetched = [*early, *late]
    body, scratch = kernel, list(scratch)
    if fetched:
        body = fetching(kernel, len(scalars) + len(arrays), len(early), len(late), len(outs))
        scratch = buffers_of(fetched) + scratch
    return pl.pallas_call(
        body,
        out_shape=tuple(jax.ShapeDtypeStruct(shape, kind) for shape, kind in outs),
        in_specs=[smem] * len(scalars) + [vmem] * len(arrays) + [hbm] * len(fetched),
        out_specs=(vmem,) * len(outs),
        scratch_shapes=scratch,
        compiler_params=pltpu.CompilerParams(vmem_limit_bytes=VMEM_CONV),
        cost_estimate=pl.CostEstimate(
            flops=2 * 10**9, bytes_accessed=4 * 2**20, transcendentals=0
        ),
        name=kernel.__name__,
    )(*scalars, *arrays, *in_hbm(fetched))


def attention_kernel(which_image, pieces, block, info_ref, *refs):
    mix_refs, refs = refs[:4], refs[4:]
    kv_refs, refs = refs[:pieces], refs[pieces:]
    outs = 1 if pieces == 2 else 2
    rows_refs, dkv_refs, refs = refs[:4], refs[4 : 4 + outs], refs[4 + outs :]
    kv_ref, extra_ref, kvt_ref, qgs_ref, rows_ref, s_ref, p_ref, acc_ref = refs
    tokens, width = rows_refs[0].shape
    half = width // 2
    whole = 8 * tokens
    edge = tokens * LEFT // 40
    left = 8 * edge
    valid_rows = info_ref[1 + which_image]
    landscape = info_ref[3 + which_image] == 40
    place, core = info_ref[5], info_ref[6]
    trips = lax.div(valid_rows + 47, 48)
    sizes = ((whole, jnp.where(landscape, trips, 0)), (left, jnp.where(landscape, 0, trips)))
    scale = half ** (-0.5)
    pair = block // 2

    def slot_of(part):
        return lax.rem(place - part + 4, 4)

    def rows_of(chunk, size):
        return pl.ds(pl.multiple_of(chunk * whole, whole), size)

    def spans(part, which):
        return (
            (0, edge, pl.ds(pl.multiple_of(part * whole + which * edge, 16), edge)),
            (
                edge,
                tokens,
                pl.ds(
                    pl.multiple_of(part * whole + left + which * (tokens - edge), 16),
                    tokens - edge,
                ),
            ),
        )

    if pieces == 2:
        for ref, beside in zip(kv_refs, (core, 1 - core)):
            for number in range(16):
                for low, high, span in spans(number // 4, 2 * (number % 4) + beside):
                    kv_ref[span, :] = ref[number, low:high, :]
    else:
        for which in range(8):
            for slot in range(4):
                for low, high, span in spans(slot_of(slot), which):
                    kv_ref[span, :] = kv_refs[0][which, slot, low:high, :]
    token_ids = lax.broadcasted_iota(jnp.int32, (whole, width), 0)
    key_lane = lax.broadcasted_iota(jnp.int32, (whole, width), 1)
    for slot in range(4):
        span = slice(slot * whole, (slot + 1) * whole)
        kvt_ref[:, span] = kv_ref[span, :].T
        acc_ref[span, :] = jnp.zeros((whole, width), jnp.float32)
        room = valid_rows - slot * (whole // 40)
        bound = jnp.where(token_ids < left, room * LEFT, left + room * (40 - LEFT))
        extra_ref[span, :] = jnp.where(
            key_lane < half,
            jnp.where(token_ids < bound, 0.0, LOWEST),
            pltpu.roll(kv_ref[span, :].astype(jnp.float32), half, 1),
        ).astype(jnp.bfloat16)
    qgs_ref[...] = jnp.zeros(qgs_ref.shape, jnp.bfloat16)
    rows_ref[...] = jnp.zeros(rows_ref.shape, jnp.bfloat16)
    for slot in range(4):
        start = pl.multiple_of(slot_of(slot) * pair, pair)
        span = slice((1 + which_image) * tokens, (2 + which_image) * tokens)
        qgs_ref[pl.ds(start, tokens), :] = mix_refs[slot][span, :]

    lane = lax.broadcasted_iota(jnp.int32, (block, width), 1)
    ones = (lax.broadcasted_iota(jnp.int32, (half, block), 0) == 0).astype(jnp.bfloat16)
    zeros = jnp.zeros((half, block), jnp.bfloat16)

    def query_block(number, _):
        qg = qgs_ref[pl.ds(pl.multiple_of(number * block, block), block), :]
        qgt = qg.T
        scaled = qgt[:half].astype(jnp.float32) * (scale * LOG2E)
        high = scaled.astype(jnp.bfloat16)
        rest = (scaled - high.astype(jnp.float32)).astype(jnp.bfloat16)
        score_rhs = jnp.concatenate([high, zeros, ones, rest], axis=0)

        def score_pass(size, chunk, best):
            rows = rows_of(chunk, size)
            lhs = jnp.concatenate([kv_ref[rows, :], extra_ref[rows, :]], axis=1)
            scores = jnp.dot(lhs, score_rhs, preferred_element_type=jnp.float32)
            s_ref[rows, :] = scores
            return jnp.maximum(best, jnp.max(scores.reshape(size // 8, 8, block), axis=0))

        best = jnp.full((8, block), LOWEST, jnp.float32)
        for size, trips in sizes:
            best = lax.fori_loop(0, trips, functools.partial(score_pass, size), best)
        peak = jnp.max(best, axis=0, keepdims=True)

        def weight_pass(size, chunk, carried):
            total, out_t = carried
            rows = rows_of(chunk, size)
            weights = jnp.exp2(s_ref[rows, :] - peak)
            total = total + jnp.sum(weights.reshape(size // 8, 8, block), axis=0)
            weights = weights.astype(jnp.bfloat16)
            p_ref[rows, :] = weights
            out_t = out_t + jnp.dot(
                kvt_ref[half:, rows], weights, preferred_element_type=jnp.float32
            )
            return total, out_t

        carried = (jnp.zeros((8, block), jnp.float32), jnp.zeros((half, block), jnp.float32))
        for size, trips in sizes:
            carried = lax.fori_loop(0, trips, functools.partial(weight_pass, size), carried)
        total, out_t = carried
        inverse = 1.0 / jnp.sum(total, axis=0, keepdims=True)
        out_t = out_t * inverse
        grad_t = qgt[half:].astype(jnp.float32) * inverse
        delta = jnp.sum(out_t * grad_t, axis=0, keepdims=True) * scale
        grad_rhs = jnp.concatenate([zeros, (grad_t * scale).astype(jnp.bfloat16)], axis=0)
        grad_rows = jnp.concatenate([jnp.zeros_like(grad_t), grad_t], axis=0).T
        out_rhs = jnp.concatenate(
            [jnp.where(lane < half, qg, jnp.zeros_like(qg)), grad_rows.astype(jnp.bfloat16)], axis=0
        )

        def grad_pass(size, chunk, dq_t):
            rows = rows_of(chunk, size)
            prob_grad = jnp.dot(kv_ref[rows, :], grad_rhs, preferred_element_type=jnp.float32)
            weights = p_ref[rows, :]
            score_grad = (weights.astype(jnp.float32) * (prob_grad - delta)).astype(jnp.bfloat16)
            acc_ref[rows, :] += jnp.dot(
                jnp.concatenate([score_grad, weights], axis=1),
                out_rhs,
                preferred_element_type=jnp.float32,
            )
            return dq_t + jnp.dot(
                kvt_ref[:half, rows], score_grad, preferred_element_type=jnp.float32
            )

        dq_t = jnp.zeros((half, block), jnp.float32)
        for size, trips in sizes:
            dq_t = lax.fori_loop(0, trips, functools.partial(grad_pass, size), dq_t)
        result = jnp.concatenate([dq_t, out_t], axis=0).T.astype(jnp.bfloat16)
        rows_ref[pl.ds(pl.multiple_of(number * block, block), block), :] = result
        return 0

    lax.fori_loop(0, jnp.where(trips > 2, 2, 1), query_block, 0)
    for slot in range(4):
        start = pl.multiple_of(slot_of(slot) * pair, pair)
        rows_refs[slot][...] = rows_ref[pl.ds(start, tokens), :]
    if outs == 1:
        for which in range(8):
            for slot in range(4):
                for low, high, span in spans(slot_of(slot), which):
                    dkv_refs[0][which, slot, low:high, :] = acc_ref[span, :].astype(jnp.bfloat16)
    else:
        for ref, beside in zip(dkv_refs, (core, 1 - core)):
            for number in range(16):
                for low, high, span in spans(number // 4, 2 * (number % 4) + beside):
                    ref[number, low:high, :] = acc_ref[span, :].astype(jnp.bfloat16)


def attend(which_image, info, mix, *kvs):
    width = mix[0].shape[-1]
    tokens = mix[0].shape[0] // 3
    keys = 8 * 4 * tokens
    block = 512
    vmem = pl.BlockSpec(memory_space=pltpu.VMEM)
    rows = jax.ShapeDtypeStruct((tokens, width), jnp.bfloat16)
    if len(kvs) == 2:
        grads = (jax.ShapeDtypeStruct((8, 4, tokens, width), jnp.bfloat16),)
    else:
        grads = (jax.ShapeDtypeStruct((16, tokens, width), jnp.bfloat16),) * 2
    arrays = [*mix, *kvs]
    results = pl.pallas_call(
        functools.partial(attention_kernel, which_image, len(kvs), block),
        out_shape=(rows,) * 4 + grads,
        in_specs=[pl.BlockSpec(memory_space=pltpu.SMEM)]
        + [vmem] * len(arrays),
        out_specs=(vmem,) * (4 + len(grads)),
        scratch_shapes=[
            pltpu.VMEM((keys, width), jnp.bfloat16),
            pltpu.VMEM((keys, width), jnp.bfloat16),
            pltpu.VMEM((width, keys), jnp.bfloat16),
            pltpu.VMEM((2 * block, width), jnp.bfloat16),
            pltpu.VMEM((2 * block, width), jnp.bfloat16),
            pltpu.VMEM((keys, block), jnp.float32),
            pltpu.VMEM((keys, block), jnp.bfloat16),
            pltpu.VMEM((keys, width), jnp.float32),
        ],
        compiler_params=pltpu.CompilerParams(vmem_limit_bytes=VMEM_ATTENTION),
        cost_estimate=pl.CostEstimate(
            flops=6 * 2 * 1024 * keys * 256,
            bytes_accessed=8 * 2**20,
            transcendentals=1024 * keys,
        ),
        name="attention",
    )(info, *arrays)
    return results[:4], *results[4:]


def per_device(
    image,
    embedding,
    cotangent,
    valid_rows,
    orientation,
    gn1_gain,
    gn1_bias,
    conv1_weight,
    conv1_bias,
    time_weight,
    time_bias,
    gn2_gain,
    gn2_bias,
    conv2_weight,
    conv2_bias,
    gn3_gain,
    gn3_bias,
    qkv_weight,
    qv_bias,
    proj_weight,
    proj_bias,
):
    images, shard_rows, columns, channels = image.shape
    tokens = shard_rows * columns
    head_width = channels // HEAD_COUNT
    seq_index = lax.axis_index("seq")
    dp_index = lax.axis_index("dp")
    places = {"x": seq_index // 8, "y": seq_index // 2 % 4, "c": seq_index % 2, "z": dp_index}
    place_x, place_y, place_c = places["x"], places["y"], places["c"]
    col_valid = columns - 2 * columns // 5 * orientation
    info = jnp.stack(
        [
            jnp.asarray(number, jnp.int32)
            for number in (
                seq_index * shard_rows,
                valid_rows[0],
                valid_rows[1],
                col_valid[0],
                col_valid[1],
                place_x,
                place_c,
                0,
            )
        ]
    )
    counts = (valid_rows * col_valid).astype(jnp.float32) * (channels // GROUPS)
    scalars = (info, counts)
    gain1, bias1, gain2, bias2, gain3, bias3, conv1_bias, conv2_bias, proj_bias = (
        value[None]
        for value in (
            gn1_gain, gn1_bias, gn2_gain, gn2_bias, gn3_gain, gn3_bias, conv1_bias, conv2_bias, proj_bias,
        )
    )
    taps = conv1_weight.shape
    conv1_weight = conv1_weight.reshape(-1, channels)
    conv2_weight = conv2_weight.reshape(-1, channels)
    wide, low_kind = jnp.float32, jnp.bfloat16
    field = (images, shard_rows, columns, channels)
    edges = (2, images, 2, columns, channels)
    extended_field = (images, shard_rows + 2, columns, channels)

    by_head = jnp.transpose(
        qkv_weight.reshape(channels, 3, HEAD_COUNT, head_width), (2, 1, 0, 3)
    )
    proj_heads = proj_weight.reshape(HEAD_COUNT, head_width, channels)
    blank = jnp.zeros((HEAD_COUNT, channels, head_width), low_kind)
    key_weight = jnp.concatenate([by_head[:, 1], by_head[:, 2]], axis=2)
    query_weight = jnp.concatenate(
        [
            jnp.concatenate([by_head[:, 0], blank], axis=2),
            jnp.concatenate([blank, jnp.swapaxes(proj_heads, 1, 2)], axis=2),
        ],
        axis=1,
    )
    blank_rows = jnp.swapaxes(blank, 1, 2)
    turned = jnp.swapaxes(by_head, 2, 3)
    key_weight_t = jnp.concatenate([turned[:, 1], turned[:, 2]], axis=1)
    query_weight_t = jnp.concatenate([turned[:, 0], blank_rows], axis=1)
    proj_weight_t = jnp.concatenate([blank_rows, proj_heads], axis=1)
    head_bias = qv_bias.reshape(2, HEAD_COUNT, 1, head_width)
    blank_bias = jnp.zeros((HEAD_COUNT, 1, head_width), wide)
    query_bias = jnp.concatenate([head_bias[0], blank_bias], axis=2)
    key_bias = jnp.concatenate([blank_bias, head_bias[1]], axis=2)

    time_input = jax.nn.silu(embedding.astype(wide)).astype(low_kind)
    shifts = jnp.dot(time_input, time_weight, preferred_element_type=wide) + time_bias

    core_edges, next_edges, sums1 = run_kernel(
        start_kernel,
        (info,),
        (),
        ((edges, low_kind), (edges, low_kind), ((4, channels), wide)),
        early=(image, cotangent),
    )
    core_edges, next_edges = swap_edges(core_edges, next_edges)
    sums1, next_edges = seq_total(sums1, next_edges)
    active1, hidden, sums2 = run_kernel(
        hidden_kernel,
        scalars,
        (core_edges, next_edges, sums1, gain1, bias1, conv1_bias, image, conv1_weight),
        ((extended_field, low_kind), (extended_field, wide), ((4, channels), wide)),
    )
    sums2 = seq_total(sums2)
    active2, residual, sums3 = run_kernel(
        residual_kernel,
        scalars,
        (hidden, sums2, gain2, bias2, shifts, conv2_bias, image, conv2_weight),
        ((extended_field, low_kind), (field, wide), ((4, channels), wide)),
    )
    sums3 = seq_total(sums3)

    third, proj_grad, placed_a, *slots = run_kernel(
        mixture_kernel,
        scalars,
        (residual, sums3, gain3, bias3, key_weight, query_weight, key_bias, query_bias),
        (((images * tokens, channels), low_kind),) * 2
        + (((16, tokens, 2 * head_width), low_kind),)
        + (((3 * tokens, 2 * head_width), low_kind),) * HEAD_COUNT,
        early=(cotangent,),
    )
    column = swap_places(placed_a)
    mix = [slots[0]] + [seq_shift(slots[d], d, 0, 0) for d in range(1, 4)]
    groups = [[x * 8 + place for place in range(8)] for x in range(4)]
    beside = seq_shift(column, 0, 0, 1)
    own_b = jnp.stack([part[:tokens] for part in mix])
    gathered_b = lax.all_gather(own_b, "seq", axis_index_groups=groups)
    rows_a, keys_a = attend(0, info, mix, column, beside)
    keys_a = lax.psum_scatter(keys_a, "seq", scatter_dimension=0, axis_index_groups=groups)
    rows_b, own_b, beside_b = attend(1, info, mix, gathered_b)
    keys_b = swap_places(low_sum(own_b, seq_shift(beside_b, 0, 0, 1)))

    rows = [jnp.stack(pair) for pair in zip(rows_a, rows_b)]
    rows = [rows[0]] + [seq_shift(rows[d], 4 - d, 0, 0) for d in range(1, 4)]
    keys_a = [keys_a[0]] + [seq_shift(keys_a[d], 4 - d, 0, 0) for d in range(1, 4)]
    output, third_grad, core_third, next_third, sums4, early_rest = run_kernel(
        output_kernel,
        scalars,
        (
            sums3, gain3, proj_bias, *rows, *keys_a, keys_b,
        ),
        (
            (field, low_kind), (field, wide), (edges, wide), (edges, wide), ((7, channels), wide),
            ((4, 2, HEAD_COUNT, head_width, channels // 2), low_kind),
        ),
        scratch=(pltpu.VMEM((2 * channels, 2 * head_width), wide),),
        early=(third, proj_grad, query_weight_t, key_weight_t, proj_weight_t),
        late=(residual,),
    )
    core_third, next_third = swap_edges(core_third, next_third)
    sums4, next_third = seq_total(sums4, next_third)
    residual_grad, early, norm2_grad, sums5 = run_kernel(
        branch_kernel,
        scalars,
        (
            core_third, next_third, core_edges, next_edges, sums3, gain3, sums4, sums2, gain2, bias2, shifts,
        ),
        (
            (field, wide), ((4, 2, 4, 208, channels // 2), low_kind), (extended_field, wide), ((5, channels), wide),
        ),
        early=(third_grad, residual, cotangent),
        late=(hidden, active2, conv2_weight, early_rest),
    )
    early = lax.psum_scatter(
        early.reshape((8,) + early.shape[2:]), "seq", scatter_dimension=0, axis_index_groups=groups
    )
    sums5 = seq_total(sums5)
    conv1_grad, norm1_grad, sums6 = run_kernel(
        hidden_grad_kernel,
        scalars,
        (
            sums2, gain2, shifts, sums5, sums1, gain1, bias1,
        ),
        (((2, 16, 144, channels // 2), low_kind), (field, wide), ((5, channels), wide)),
        early=(norm2_grad, hidden),
        late=(image, active1, conv1_weight),
    )
    late, early, sums6 = sums_over_seq(conv1_grad, sums6, early, places)
    both = jnp.concatenate([late, early])
    (image_grad,) = run_kernel(
        image_grad_kernel,
        scalars,
        (sums1, gain1, sums6),
        ((field, low_kind),),
        early=(image, norm1_grad, residual_grad),
    )

    scaling = shifts[:, :channels]
    scale_total = gain2 * sums5[2:4] + bias2 * sums5[:2]
    shift_low = jnp.concatenate([scale_total, sums5[:2]], axis=-1).astype(low_kind)
    embedding_grad = jnp.einsum(
        "ik,ek->ie", shift_low, time_weight, preferred_element_type=wide
    ) * silu_slope(embedding.astype(wide))
    rows = [
        sums6[2] + sums6[3],
        sums6[0] + sums6[1],
        sums6[4],
        jnp.sum((1.0 + scaling) * sums5[2:4], axis=0),
        jnp.sum((1.0 + scaling) * sums5[:2], axis=0),
        sums5[4],
        sums4[2] + sums4[3],
        sums4[0] + sums4[1],
        sums4[4],
        sums4[5],
        sums4[6],
    ]
    time_pair = jnp.concatenate([time_input, shift_low], axis=-1)
    both, totals, every_pair = sums_over_dp(
        both, jnp.stack(rows), time_pair.reshape(-1, channels // 2), places
    )
    every_input, every_shift = jnp.split(
        every_pair.reshape(-1, time_pair.shape[-1]), (time_input.shape[-1],), axis=-1
    )
    time_weight_grad = jnp.einsum(
        "ie,ik->ek", every_input, every_shift, preferred_element_type=wide
    )
    time_bias_grad = jnp.sum(every_shift, axis=0, dtype=wide)
    parts = gathered_over_seq(both, places)
    shapes = [conv1_weight.shape, conv2_weight.shape, (channels, 3 * channels), (channels, channels)]
    vmem = pl.BlockSpec(memory_space=pltpu.VMEM)
    conv1_total, conv2_total, qkv_total, proj_total = pl.pallas_call(
        weights_kernel,
        out_shape=tuple(jax.ShapeDtypeStruct(shape, wide) for shape in shapes),
        in_specs=[pl.BlockSpec(memory_space=pltpu.SMEM), vmem, vmem],
        out_specs=(pl.BlockSpec(memory_space=pltpu.HBM),) * 4,
        scratch_shapes=[pltpu.VMEM(shape, wide) for shape in shapes]
        + [pltpu.VMEM((4 * channels, channels), wide), pltpu.SemaphoreType.DMA((4,))],
        compiler_params=pltpu.CompilerParams(vmem_limit_bytes=VMEM_CONV),
        name="weights_kernel",
    )(info, *parts)
    return (
        output,
        image_grad,
        embedding_grad,
        totals[0],
        totals[1],
        conv1_total.reshape(taps),
        totals[2],
        time_weight_grad,
        time_bias_grad,
        totals[3],
        totals[4],
        conv2_total.reshape(taps),
        totals[5],
        totals[6],
        totals[7],
        qkv_total,
        jnp.concatenate([totals[8], totals[9]]),
        proj_total,
        totals[10],
    )


def solution(mesh):
    return jax.shard_map(
        per_device,
        mesh=mesh,
        in_specs=(
            P("dp", "seq", None, None),
            P("dp", None),
            P("dp", "seq", None, None),
            P("dp"),
            P("dp"),
            P(),
            P(),
            P(),
            P(),
            P(),
            P(),
            P(),
            P(),
            P(),
            P(),
            P(),
            P(),
            P(),
            P(),
            P(),
            P(),
        ),
        out_specs=(
            P("dp", "seq", None, None),
            P("dp", "seq", None, None),
            P("dp", None),
            P(),
            P(),
            P(),
            P(),
            P(),
            P(),
            P(),
            P(),
            P(),
            P(),
            P(),
            P(),
            P(),
            P(),
            P(),
            P(),
        ),
        check_vma=False,
    )
```

```python
import functools

import jax
import jax.numpy as jnp
from jax import lax
from jax.experimental import pallas as pl
from jax.experimental.pallas import tpu as pltpu
from jax.sharding import PartitionSpec as P

GROUPS = 32
HEAD_COUNT = 4


EPS = 1e-05
LOWEST = -1e30
LOG2E = 1.4426950408889634

LEFT = 24

VMEM_CONV = 24 * 2**20
VMEM_ATTENTION = 44 * 2**20


def seq_shift(value, dx, dy, dc):
    pairs = []
    for place in range(32):
        x, y, c = place // 8, place // 2 % 4, place % 2
        pairs.append((place, (x + dx) % 4 * 8 + (y + dy) % 4 * 2 + (c + dc) % 2))
    return lax.ppermute(value, "seq", pairs)


def axis_shift(value, axis, step):
    if axis == "x":
        return seq_shift(value, step, 0, 0)
    if axis == "y":
        return seq_shift(value, 0, step, 0)
    return lax.ppermute(value, "dp", [(i, (i + step) % 4) for i in range(4)])


def swap_edges(core_edges, next_edges):
    pairs = [(i, (i + 1) % 32 if i % 2 else (i - 1) % 32) for i in range(32)]
    return seq_shift(core_edges, 0, 0, 1), lax.ppermute(next_edges, "seq", pairs)


def swap_places(value):
    groups = [[place * 2 + core for place in range(16)] for core in range(2)]
    return lax.all_to_all(value, "seq", 0, 0, axis_index_groups=groups)


def seq_total(value, beside=None):
    value = value + seq_shift(value, 0, 0, 1)
    swapped = swap_places(jnp.broadcast_to(value[None], (16,) + value.shape))
    if beside is None:
        return jnp.sum(swapped, axis=0)
    swapped, beside = lax.optimization_barrier((swapped, beside))
    return jnp.sum(swapped, axis=0), beside


def core_total(value, c):
    return low_sum(take_slot(value, c), seq_shift(take_slot(value, 1 - c), 0, 0, 1))


def take_slot(value, slot):
    return lax.dynamic_index_in_dim(value, slot, 0, keepdims=False)


def low_sum(*parts):
    total = parts[0].astype(jnp.float32)
    for part in parts[1:]:
        total = total + part.astype(jnp.float32)
    return total.astype(jnp.bfloat16)


def scatter_ring(value, axis, place):
    return low_sum(
        take_slot(value, place),
        *(axis_shift(take_slot(value, (place + step) % 4), axis, step) for step in (1, 3, 2)),
    )


def gather_ring(value, axis, place):
    result = jnp.zeros((4,) + value.shape, value.dtype)
    result = lax.dynamic_update_index_in_dim(result, value, place, 0)
    for step in (1, 3, 2):
        result = lax.dynamic_update_index_in_dim(
            result, axis_shift(value, axis, step), (place - step) % 4, 0
        )
    return result


def split_low(value):
    high = value.astype(jnp.bfloat16)
    both = jnp.concatenate([high, (value - high.astype(jnp.float32)).astype(jnp.bfloat16)])
    both = both.reshape(-1, 128)
    return jnp.pad(both, ((0, -both.shape[0] % 16), (0, 0)))


def join_low(value, rows):
    value = value[: 4 * rows].astype(jnp.float32).reshape(2, rows, 256)
    return value[0] + value[1]


def paired(parts):
    return (parts[0] + parts[2]) + (parts[1] + parts[3])


def sums_over_seq(late, vector, early, places):
    late = core_total(late, places["c"])
    low = split_low(vector + seq_shift(vector, 0, 0, 1))
    swapped = swap_places(
        jnp.concatenate([late, jnp.broadcast_to(low[None], (16,) + low.shape)], axis=1)
    )
    early = scatter_ring(early, "x", places["x"])
    swapped, early = lax.optimization_barrier((swapped, early))
    total = jnp.sum(swapped.astype(jnp.float32), axis=0)
    count = late.shape[1]
    return total[:count].astype(jnp.bfloat16), early, join_low(total[count:], vector.shape[0])


def sums_over_dp(both, vector, extra, places):
    low = split_low(vector)
    sent = jnp.concatenate([both, low, extra])
    got = [sent] + [axis_shift(sent, "z", step) for step in (1, 2, 3)]
    count = both.shape[0]
    both = paired([part[:count].astype(jnp.float32) for part in got]).astype(jnp.bfloat16)
    count += low.shape[0]
    vector = paired(
        [join_low(part[count - low.shape[0] : count], vector.shape[0]) for part in got]
    )
    extras = jnp.zeros((4,) + extra.shape, extra.dtype)
    for step in range(4):
        extras = lax.dynamic_update_index_in_dim(
            extras, got[step][count:], (places["z"] - step) % 4, 0
        )
    return both, vector, extras


def gathered_over_seq(both, places):
    both = gather_ring(both, "y", places["y"])
    both = gather_ring(both, "x", places["x"]).reshape((16, -1) + both.shape[2:])
    return both, seq_shift(both, 0, 0, 1)


def silu_slope(values):
    sigmoid = jax.nn.sigmoid(values)
    return sigmoid * (1.0 + values * (1.0 - sigmoid))


def same_group(channels):
    size = channels // GROUPS
    rows = lax.broadcasted_iota(jnp.int32, (channels, channels), 0) // size
    cols = lax.broadcasted_iota(jnp.int32, (channels, channels), 1) // size
    return (rows == cols).astype(jnp.float32)


def over_group(sums, channels):
    return jnp.dot(
        sums, same_group(channels), precision=lax.Precision.HIGHEST, preferred_element_type=jnp.float32
    )


def norm_terms(sums, counts_ref):
    totals = over_group(sums[:4], sums.shape[-1])
    terms = []
    for i in range(2):
        average = totals[i : i + 1] / counts_ref[i]
        spread = lax.rsqrt(totals[2 + i : 3 + i] / counts_ref[i] - average * average + EPS)
        terms.append((average, spread))
    return terms


def mask_of(info_ref, i, shape, border):
    rows = lax.broadcasted_iota(jnp.int32, shape, 0) + (info_ref[0] - border)
    cols = lax.broadcasted_iota(jnp.int32, shape, 1)
    valid = (rows >= 0) & (rows < info_ref[1 + i]) & (cols < info_ref[3 + i])
    return valid.astype(jnp.float32)


def extended(edges, own):
    low, high = edges
    return jnp.concatenate([low, own.astype(jnp.float32), high], axis=0)


def shifted(values):
    rows, columns, channels = values.shape
    cols = lax.broadcasted_iota(jnp.int32, values.shape, 1).reshape(-1, channels)
    flat = values.reshape(-1, channels)
    before = jnp.where(cols == 0, 0.0, pltpu.roll(flat, 1, 0))
    after = jnp.where(cols == columns - 1, 0.0, pltpu.roll(flat, rows * columns - 1, 0))
    return before, flat, after


def tap_rows(images, a, b, rows, columns=40):
    return jnp.concatenate(
        [image[b][a * columns : (a + rows) * columns] for image in images], axis=0
    ).astype(jnp.bfloat16)


def conv_taps(images, weight_ref, rows):
    patches = jnp.concatenate(
        [tap_rows(images, a, b, rows) for a in range(3) for b in range(3)], axis=1
    )
    return jnp.dot(patches, weight_ref[...], preferred_element_type=jnp.float32)


def put_rows(ref, first, values):
    rows = 9 * values.shape[1] // 16
    width = ref.shape[-1]
    last = first + values.shape[0]
    while first < last:
        place, low = divmod(first, rows)
        count = min(rows - low, last - first)
        for core in range(2):
            part = values[:count, core * width : (core + 1) * width].astype(jnp.bfloat16)
            if len(ref.shape) == 4:
                ref[core, place, low : low + count, :] = part
            else:
                ref[place // 4, core, place % 4, low : low + count, :] = part
        values = values[count:]
        first += count


def conv_grads(images, rows, actives, weight_ref, low, weight_grad_ref):
    total = None
    channels = low.shape[-1]
    for a in range(3):
        for b in range(3):
            span = slice((3 * a + b) * channels, (3 * a + b + 1) * channels)
            put_rows(
                weight_grad_ref,
                span.start,
                lax.dot_general(
                    tap_rows(actives, a, b, 6),
                    low,
                    (((0,), (0,)), ((), ())),
                    preferred_element_type=jnp.float32,
                ),
            )
            part = lax.dot_general(
                tap_rows(images, 2 - a, 2 - b, rows),
                weight_ref[span, :],
                (((1,), (1,)), ((), ())),
                preferred_element_type=jnp.float32,
            )
            total = part if total is None else total + part
    return total


def put_sums(ref, rows):
    for place, row in enumerate(rows):
        ref[place : place + 1, :] = row


def column_sum(values):
    return jnp.sum(values.reshape(-1, values.shape[-1]), axis=0, keepdims=True)


def put_edges(info_ref, core_ref, next_ref, which, i, first, last):
    first, last = first.astype(jnp.float32), last.astype(jnp.float32)
    low_core = info_ref[6] == 0
    core_ref[which, i] = jnp.where(low_core, last, first).astype(core_ref.dtype)
    next_ref[which, i] = jnp.where(low_core, first, last).astype(core_ref.dtype)


def edges_of(info_ref, core_ref, next_ref, which, i):
    low_core = info_ref[6] == 0
    core = core_ref[which, i].astype(jnp.float32)
    beyond = next_ref[which, i].astype(jnp.float32)
    return jnp.where(low_core, beyond, core), jnp.where(low_core, core, beyond)


def start_kernel(
    valid_rows_ref, orientation_ref, image_ref, cotangent_ref, core_ref, next_ref, out_sums_ref, info_ref
):
    place = lax.axis_index("seq")
    info_ref[0] = place * 6
    for i in range(2):
        info_ref[1 + i] = valid_rows_ref[i]
        info_ref[3 + i] = 40 - 16 * orientation_ref[i]
    info_ref[5] = lax.div(place, 8)
    info_ref[6] = lax.rem(place, 2)
    info_ref[7] = 0
    first, second = [], []
    for i in range(2):
        image = image_ref[i]
        cotangent = cotangent_ref[i]
        put_edges(info_ref, core_ref, next_ref, 0, i, image[:2], image[-2:])
        put_edges(info_ref, core_ref, next_ref, 1, i, cotangent[:2], cotangent[-2:])
        values = mask_of(info_ref, i, image.shape, 0) * image.astype(jnp.float32)
        first.append(column_sum(values))
        second.append(column_sum(values * values))
    put_sums(out_sums_ref, first + second)


def hidden_kernel(
    info_ref, counts_ref, core_ref, next_ref, sums_ref, gain_ref, bias_ref, conv_bias_ref, own_ref, weight_ref,
    active_ref, hidden_ref, out_sums_ref,
):
    terms = norm_terms(sums_ref[...], counts_ref)
    images = []
    for i in range(2):
        values = extended(edges_of(info_ref, core_ref, next_ref, 0, i), own_ref[i])
        mask = mask_of(info_ref, i, values.shape, 2)
        average, spread = terms[i]
        hat = mask * ((mask * values - average) * spread)
        active = jax.nn.silu(mask * (hat * gain_ref[...] + bias_ref[...])).astype(jnp.bfloat16)
        active_ref[i] = active[1:-1]
        images.append(shifted(active.astype(jnp.float32)))
    conv = conv_taps(images, weight_ref, 8)
    first, second = [], []
    for i in range(2):
        shape = hidden_ref.shape[1:]
        mask = mask_of(info_ref, i, shape, 1)
        half = conv.shape[0] // 2
        hidden = mask * (conv[i * half : (i + 1) * half].reshape(shape) + conv_bias_ref[...])
        hidden_ref[i] = hidden
        hidden = hidden[1:-1]
        first.append(column_sum(hidden))
        second.append(column_sum(hidden * hidden))
    put_sums(out_sums_ref, first + second)


def second_norm_of(values, mask, term, gain, bias, shifts_ref, i):
    channels = values.shape[-1]
    average, spread = term
    hat = mask * ((values - average) * spread)
    base = mask * (hat * gain + bias)
    scaling = shifts_ref[i : i + 1, :channels]
    offset = shifts_ref[i : i + 1, channels:]
    return hat, mask * (base * (1.0 + scaling) + offset)


def residual_kernel(
    info_ref, counts_ref, hidden_ref, sums_ref, gain_ref, bias_ref, shifts_ref, conv_bias_ref, image_ref, weight_ref,
    active_ref, residual_ref, out_sums_ref,
):
    terms = norm_terms(sums_ref[...], counts_ref)
    images = []
    for i in range(2):
        values = hidden_ref[i]
        mask = mask_of(info_ref, i, values.shape, 1)
        _, norm = second_norm_of(
            values, mask, terms[i], gain_ref[...], bias_ref[...], shifts_ref, i
        )
        active = jax.nn.silu(norm).astype(jnp.bfloat16)
        active_ref[i] = active
        images.append(shifted(active.astype(jnp.float32)))
    conv = conv_taps(images, weight_ref, 6)
    first, second = [], []
    for i in range(2):
        shape = residual_ref.shape[1:]
        mask = mask_of(info_ref, i, shape, 0)
        half = conv.shape[0] // 2
        residual = mask * image_ref[i].astype(jnp.float32) + mask * (
            conv[i * half : (i + 1) * half].reshape(shape) + conv_bias_ref[...]
        )
        residual_ref[i] = residual
        first.append(column_sum(residual))
        second.append(column_sum(residual * residual))
    put_sums(out_sums_ref, first + second)


def to_parts(values):
    channels = values.shape[-1]
    return jnp.concatenate(
        [values[:, :LEFT].reshape(-1, channels), values[:, LEFT:].reshape(-1, channels)], axis=0
    )


def from_parts(values, shape):
    rows, columns, channels = shape
    edge = rows * LEFT
    return jnp.concatenate(
        [
            values[:edge].reshape(rows, LEFT, channels),
            values[edge:].reshape(rows, columns - LEFT, channels),
        ],
        axis=1,
    )


def mixture_kernel(
    info_ref, counts_ref, residual_ref, sums_ref, gain_ref, bias_ref, key_weight_ref, query_weight_ref,
    key_bias_ref, query_bias_ref, cotangent_ref, third_ref, grad_ref, first_ref, *slot_refs,
):
    terms = norm_terms(sums_ref[...], counts_ref)
    tokens = third_ref.shape[0] // 2
    for i in range(2):
        values = residual_ref[i]
        mask = mask_of(info_ref, i, values.shape, 0)
        average, spread = terms[i]
        hat = mask * ((values - average) * spread)
        span = slice(i * tokens, (i + 1) * tokens)
        third_ref[span, :] = to_parts(mask * (hat * gain_ref[...] + bias_ref[...])).astype(
            jnp.bfloat16
        )
        grad_ref[span, :] = to_parts(mask * cotangent_ref[i].astype(jnp.float32)).astype(
            jnp.bfloat16
        )
    third = third_ref[...]
    both = jnp.concatenate([third, grad_ref[...]], axis=1)
    first = first_image(info_ref)
    third_first = third_ref[pl.ds(pl.multiple_of(first * tokens, 16), tokens), :]
    third_second = third_ref[pl.ds(pl.multiple_of((1 - first) * tokens, 16), tokens), :]
    for head in range(HEAD_COUNT):
        keys = (
            jnp.dot(third_first, key_weight_ref[head], preferred_element_type=jnp.float32)
            + key_bias_ref[head]
        ).astype(jnp.bfloat16)
        for place in range(4):
            first_ref[4 * head + place] = keys
    for slot, ref in enumerate(slot_refs):
        head = lax.rem(info_ref[5] + slot, HEAD_COUNT)
        keys = (
            jnp.dot(third_second, key_weight_ref[head], preferred_element_type=jnp.float32)
            + key_bias_ref[head]
        ).astype(jnp.bfloat16)
        queries = (
            jnp.dot(both, query_weight_ref[head], preferred_element_type=jnp.float32)
            + query_bias_ref[head]
        ).astype(jnp.bfloat16)
        ref[:tokens, :] = keys
        ref[tokens:, :] = queries


def output_kernel(
    info_ref, counts_ref, sums_ref, gain_ref, proj_bias_ref, *refs,
):
    row_refs, first_refs, key_ref, refs = refs[:4], refs[4:8], refs[8], refs[9:]
    third_ref, grad_ref, query_weight_ref, key_weight_ref, proj_weight_ref, residual_ref, *refs = refs
    output_ref, third_grad_ref, core_ref, next_ref, out_sums_ref, early_ref, columns_ref, wait = refs
    tokens, channels = third_ref.shape
    width = channels // 2
    head_width = channels // HEAD_COUNT
    third = third_ref[...]
    proj_grad = grad_ref[...]
    ones = jnp.ones((tokens, width), jnp.bfloat16)
    row_rhs = jnp.concatenate([third, proj_grad, ones], axis=1)
    key_rhs = jnp.concatenate([third, ones], axis=1)
    projected = None
    third_grad = None
    transposed = (((0,), (0,)), ((), ()))
    for slot in range(HEAD_COUNT):
        head = lax.rem(info_ref[5] + slot, HEAD_COUNT)
        turn = first_image(info_ref)
        rows = jnp.concatenate([row_refs[slot][turn], row_refs[slot][1 - turn]], axis=0)
        first_keys = first_refs[slot][...].astype(jnp.float32)
        last_keys = key_ref[pl.ds(pl.multiple_of(4 * head, 4), 4)].astype(jnp.float32)
        last_keys = jnp.sum(last_keys, axis=0)
        keys = jnp.concatenate(
            [
                jnp.where(turn == 0, first_keys, last_keys),
                jnp.where(turn == 0, last_keys, first_keys),
            ],
            axis=0,
        ).astype(jnp.bfloat16)
        part = jnp.dot(rows, proj_weight_ref[head], preferred_element_type=jnp.float32)
        projected = part if projected is None else projected + part
        part = jnp.dot(
            jnp.concatenate([rows, keys], axis=1),
            jnp.concatenate([query_weight_ref[head], key_weight_ref[head]], axis=0),
            preferred_element_type=jnp.float32,
        )
        third_grad = part if third_grad is None else third_grad + part
        row_grad = lax.dot_general(rows, row_rhs, transposed, preferred_element_type=jnp.float32)
        key_grad = lax.dot_general(keys, key_rhs, transposed, preferred_element_type=jnp.float32)
        start = pl.multiple_of(head * head_width, head_width)
        for place, block in (
            (0, row_grad[:head_width, :channels]),
            (channels, key_grad[:head_width, :channels]),
            (2 * channels, key_grad[head_width:, :channels]),
            (3 * channels, row_grad[head_width:, channels : 2 * channels]),
        ):
            for core in range(2):
                early_ref[place // channels, core, head] = block[
                    :, core * width : (core + 1) * width
                ].astype(jnp.bfloat16)
        columns_ref[pl.ds(start, head_width), :] = row_grad[:head_width, 2 * channels :]
        columns_ref[pl.ds(channels + start, head_width), :] = key_grad[head_width:, channels:]
    terms = norm_terms(sums_ref[...], counts_ref)
    wait()
    first, second = [], []
    for i in range(2):
        shape = residual_ref.shape[1:]
        span = slice(i * (tokens // 2), (i + 1) * (tokens // 2))
        values = residual_ref[i]
        mask = mask_of(info_ref, i, shape, 0)
        output_ref[i] = (
            values + mask * from_parts(projected[span] + proj_bias_ref[...], shape)
        ).astype(jnp.bfloat16)
        average, spread = terms[i]
        hat = mask * ((values - average) * spread)
        grad = mask * from_parts(third_grad[span], shape)
        third_grad_ref[i] = grad
        put_edges(info_ref, core_ref, next_ref, 0, i, grad[:2], grad[-2:])
        put_edges(info_ref, core_ref, next_ref, 1, i, values[:2], values[-2:])
        first.append(column_sum(grad))
        second.append(column_sum(grad * hat))
    query_row = columns_ref[:channels, :].T[:1]
    value_row = columns_ref[channels:, :].T[:1]
    put_sums(
        out_sums_ref,
        first + second + [query_row, value_row, column_sum(proj_grad.astype(jnp.float32))],
    )


def norm_grad_means(grad_sums, counts_ref, factors):
    rows = [grad_sums[i : i + 1] * factors[i] for i in range(2)]
    rows += [grad_sums[2 + i : 3 + i] * factors[i] for i in range(2)]
    totals = over_group(
        jnp.concatenate(rows, axis=0), rows[0].shape[-1]
    )
    return [
        (totals[i : i + 1] / counts_ref[i], totals[2 + i : 3 + i] / counts_ref[i])
        for i in range(2)
    ]


def branch_kernel(
    info_ref, counts_ref, core_ref, next_ref, cot_core_ref, cot_next_ref, sums3_ref, gain3_ref, sums4_ref, sums2_ref,
    gain2_ref, bias2_ref, shifts_ref, grad_ref, residual_ref, cot_ref, hidden_ref, active_ref, weight_ref, rest_ref,
    residual_grad_ref, weight_grad_ref, norm_grad_ref, out_sums_ref, wait,
):
    terms = norm_terms(sums3_ref[...], counts_ref)
    gain = gain3_ref[...]
    means = norm_grad_means(sums4_ref[...], counts_ref, [gain, gain])
    images, actives, lows = [], [], []
    shape = hidden_ref.shape[1:]
    channels = shape[-1]
    for i in range(2):
        grad = extended(edges_of(info_ref, core_ref, next_ref, 0, i), grad_ref[i])
        values = extended(edges_of(info_ref, core_ref, next_ref, 1, i), residual_ref[i])
        mask = mask_of(info_ref, i, values.shape, 2)
        average, spread = terms[i]
        hat = mask * ((values - average) * spread)
        first_mean, second_mean = means[i]
        residual_grad = extended(
            edges_of(info_ref, cot_core_ref, cot_next_ref, 1, i), cot_ref[i]
        ) + mask * (spread * (grad * gain - first_mean - hat * second_mean))
        residual_grad_ref[i] = residual_grad[2:-2]
        low = (mask * residual_grad).astype(jnp.bfloat16).astype(jnp.float32)
        images.append(shifted(low))
        lows.append(low[2:-2].reshape(-1, channels))
    wait()
    for i in range(2):
        actives.append(shifted(active_ref[i].astype(jnp.float32)))
    low = jnp.concatenate(lows, axis=0)
    total = conv_grads(images, 8, actives, weight_ref, low.astype(jnp.bfloat16), weight_grad_ref)
    terms = norm_terms(sums2_ref[...], counts_ref)
    first, second = [], []
    for i in range(2):
        mask = mask_of(info_ref, i, shape, 1)
        hat, norm = second_norm_of(
            hidden_ref[i], mask, terms[i], gain2_ref[...], bias2_ref[...], shifts_ref, i
        )
        half = total.shape[0] // 2
        grad = mask * total[i * half : (i + 1) * half].reshape(shape) * silu_slope(norm)
        norm_grad_ref[i] = grad
        grad, hat = grad[1:-1], hat[1:-1]
        first.append(column_sum(grad))
        second.append(column_sum(grad * hat))
    put_sums(out_sums_ref, first + second + [column_sum(low)])
    weight_grad_ref[:, :, :, -rest_ref.shape[3] :, :] = rest_ref[...]


def hidden_grad_kernel(
    info_ref, counts_ref, sums2_ref, gain2_ref, shifts_ref, sums5_ref, sums1_ref, gain1_ref, bias1_ref,
    grad_ref, hidden_ref, image_ref, active_ref, weight_ref,
    weight_grad_ref, norm_grad_ref, out_sums_ref, wait,
):
    terms = norm_terms(sums2_ref[...], counts_ref)
    shape = image_ref.shape[1:]
    channels = shape[-1]
    factors = [(1.0 + shifts_ref[i : i + 1, :channels]) * gain2_ref[...] for i in range(2)]
    means = norm_grad_means(sums5_ref[...], counts_ref, factors)
    images, actives, lows = [], [], []
    for i in range(2):
        grad = grad_ref[i]
        values = hidden_ref[i]
        mask = mask_of(info_ref, i, values.shape, 1)
        average, spread = terms[i]
        hat = mask * ((values - average) * spread)
        first_mean, second_mean = means[i]
        low = mask * (spread * (grad * factors[i] - first_mean - hat * second_mean))
        low = low.astype(jnp.bfloat16).astype(jnp.float32)
        images.append(shifted(low))
        lows.append(low[1:-1].reshape(-1, channels))
    wait()
    for i in range(2):
        actives.append(shifted(active_ref[i].astype(jnp.float32)))
    low = jnp.concatenate(lows, axis=0)
    total = conv_grads(images, 6, actives, weight_ref, low.astype(jnp.bfloat16), weight_grad_ref)
    terms = norm_terms(sums1_ref[...], counts_ref)
    first, second = [], []
    for i in range(2):
        mask = mask_of(info_ref, i, shape, 0)
        average, spread = terms[i]
        hat = mask * ((mask * image_ref[i].astype(jnp.float32) - average) * spread)
        norm = mask * (hat * gain1_ref[...] + bias1_ref[...])
        half = total.shape[0] // 2
        grad = mask * total[i * half : (i + 1) * half].reshape(shape) * silu_slope(norm)
        norm_grad_ref[i] = grad
        first.append(column_sum(grad))
        second.append(column_sum(grad * hat))
    put_sums(out_sums_ref, first + second + [column_sum(low)])


def image_grad_kernel(
    info_ref, counts_ref, sums1_ref, gain1_ref, sums6_ref, image_ref, grad_ref, residual_grad_ref, out_ref
):
    terms = norm_terms(sums1_ref[...], counts_ref)
    gain = gain1_ref[...]
    means = norm_grad_means(sums6_ref[...], counts_ref, [gain, gain])
    for i in range(2):
        shape = image_ref.shape[1:]
        mask = mask_of(info_ref, i, shape, 0)
        average, spread = terms[i]
        hat = mask * ((mask * image_ref[i].astype(jnp.float32) - average) * spread)
        first_mean, second_mean = means[i]
        result = residual_grad_ref[i] + mask * (
            spread * (grad_ref[i] * gain - first_mean - hat * second_mean)
        )
        out_ref[i] = (mask * result).astype(jnp.bfloat16)


def weights_kernel(
    info_ref, own_ref, beside_ref, conv1_out, conv2_out, qkv_out, proj_out, conv1_ref, conv2_ref, qkv_ref, proj_ref,
    rest_ref, sems,
):
    channels = proj_ref.shape[0]
    width = channels // 2
    taps = conv1_ref.shape[0] // 16
    rest = 4 * channels // 16
    low_core = info_ref[6] == 0

    def write(first, count, target, in_order):
        def fill(refs):
            for core, ref in enumerate(refs):
                columns = slice(core * width, (core + 1) * width)
                for place in range(16):
                    number = place if in_order else place % 4 * 4 + place // 4
                    target[number * count : (number + 1) * count, columns] = ref[
                        place, first : first + count, :
                    ].astype(jnp.float32)

        @pl.when(low_core)
        def _():
            fill((own_ref, beside_ref))

        @pl.when(jnp.logical_not(low_core))
        def _():
            fill((beside_ref, own_ref))

    write(0, taps, conv1_ref, True)
    copies = [pltpu.make_async_copy(conv1_ref, conv1_out, sems.at[0])]
    copies[0].start()
    write(taps, taps, conv2_ref, False)
    copies.append(pltpu.make_async_copy(conv2_ref, conv2_out, sems.at[1]))
    copies[1].start()
    write(2 * taps, rest, rest_ref, False)
    for part in range(3):
        span = slice(part * channels, (part + 1) * channels)
        qkv_ref[:, span] = rest_ref[span, :].T
    proj_ref[...] = rest_ref[3 * channels :, :]
    copies.append(pltpu.make_async_copy(qkv_ref, qkv_out, sems.at[2]))
    copies.append(pltpu.make_async_copy(proj_ref, proj_out, sems.at[3]))
    copies[2].start()
    copies[3].start()
    for copy in copies:
        copy.wait()


def fetching(kernel, n_in, early, late, n_out):
    def body(*refs):
        count = early + late
        ins, refs = refs[:n_in], refs[n_in:]
        sources, refs = refs[:count], refs[count:]
        outs, refs = refs[:n_out], refs[n_out:]
        buffers, refs = refs[:count], refs[count:]
        sems, refs = refs[0], refs[1:]
        copies = [
            pltpu.make_async_copy(source, buffer, sems.at[number])
            for number, (source, buffer) in enumerate(zip(sources, buffers))
        ]
        for copy in copies:
            copy.start()
        for copy in copies[:early]:
            copy.wait()

        def wait():
            for copy in copies[early:]:
                copy.wait()

        kernel(*ins, *buffers, *outs, *refs, *((wait,) if late else ()))

    return body


def in_hbm(arrays):
    return [pltpu.with_memory_space_constraint(array, pltpu.HBM) for array in arrays]


def buffers_of(arrays):
    return [pltpu.VMEM(array.shape, array.dtype) for array in arrays] + [
        pltpu.SemaphoreType.DMA((len(arrays),))
    ]


def run_kernel(kernel, scalars, arrays, outs, scratch=(), early=(), late=()):
    vmem = pl.BlockSpec(memory_space=pltpu.VMEM)
    smem = pl.BlockSpec(memory_space=pltpu.SMEM)
    hbm = pl.BlockSpec(memory_space=pltpu.HBM)
    fetched = [*early, *late]
    body, scratch = kernel, list(scratch)
    if fetched:
        body = fetching(kernel, len(scalars) + len(arrays), len(early), len(late), len(outs))
        scratch = buffers_of(fetched) + scratch
    return pl.pallas_call(
        body,
        out_shape=tuple(jax.ShapeDtypeStruct(shape, kind) for shape, kind in outs),
        in_specs=[smem] * len(scalars) + [vmem] * len(arrays) + [hbm] * len(fetched),
        out_specs=(vmem,) * len(outs),
        scratch_shapes=scratch,
        compiler_params=pltpu.CompilerParams(vmem_limit_bytes=VMEM_CONV),
        cost_estimate=pl.CostEstimate(
            flops=2 * 10**9, bytes_accessed=4 * 2**20, transcendentals=0
        ),
        name=kernel.__name__,
    )(*scalars, *arrays, *in_hbm(fetched))


def first_image(info_ref):
    work = [lax.div(info_ref[1 + i] + 47, 48) * info_ref[3 + i] for i in range(2)]
    return jnp.where(work[1] < work[0], 1, 0)


def attention_kernel(turn, pieces, block, info_ref, *refs):
    mix_refs, refs = refs[:4], refs[4:]
    kv_refs, refs = refs[:pieces], refs[pieces:]
    outs = 1 if pieces == 2 else 2
    rows_refs, dkv_refs, refs = refs[:4], refs[4 : 4 + outs], refs[4 + outs :]
    kv_ref, extra_ref, kvt_ref, qgs_ref, rows_ref, s_ref, p_ref, acc_ref = refs
    tokens, width = rows_refs[0].shape
    half = width // 2
    whole = 8 * tokens
    edge = tokens * LEFT // 40
    left = 8 * edge
    which_image = first_image(info_ref) if turn == 0 else 1 - first_image(info_ref)
    valid_rows = info_ref[1 + which_image]
    landscape = info_ref[3 + which_image] == 40
    place, core = info_ref[5], info_ref[6]
    trips = lax.div(valid_rows + 47, 48)
    sizes = ((whole, jnp.where(landscape, trips, 0)), (left, jnp.where(landscape, 0, trips)))
    scale = half ** (-0.5)
    pair = block // 2

    def slot_of(part):
        return lax.rem(place - part + 4, 4)

    def rows_of(chunk, size):
        return pl.ds(pl.multiple_of(chunk * whole, whole), size)

    def spans(part, which):
        return (
            (0, edge, pl.ds(pl.multiple_of(part * whole + which * edge, 16), edge)),
            (
                edge,
                tokens,
                pl.ds(
                    pl.multiple_of(part * whole + left + which * (tokens - edge), 16),
                    tokens - edge,
                ),
            ),
        )

    if pieces == 2:
        for ref, beside in zip(kv_refs, (core, 1 - core)):
            for number in range(16):
                for low, high, span in spans(number // 4, 2 * (number % 4) + beside):
                    kv_ref[span, :] = ref[number, low:high, :]
    else:
        for which in range(8):
            for slot in range(4):
                for low, high, span in spans(slot_of(slot), which):
                    kv_ref[span, :] = kv_refs[0][which, slot, low:high, :]
    token_ids = lax.broadcasted_iota(jnp.int32, (whole, width), 0)
    key_lane = lax.broadcasted_iota(jnp.int32, (whole, width), 1)
    for slot in range(4):
        span = slice(slot * whole, (slot + 1) * whole)
        kvt_ref[:, span] = kv_ref[span, :].T
        acc_ref[span, :] = jnp.zeros((whole, width), jnp.float32)
        room = valid_rows - slot * (whole // 40)
        bound = jnp.where(token_ids < left, room * LEFT, left + room * (40 - LEFT))
        extra_ref[span, :] = jnp.where(
            key_lane < half,
            jnp.where(token_ids < bound, 0.0, LOWEST),
            pltpu.roll(kv_ref[span, :].astype(jnp.float32), half, 1),
        ).astype(jnp.bfloat16)
    qgs_ref[...] = jnp.zeros(qgs_ref.shape, jnp.bfloat16)
    rows_ref[...] = jnp.zeros(rows_ref.shape, jnp.bfloat16)
    for slot in range(4):
        start = pl.multiple_of(slot_of(slot) * pair, pair)
        span = pl.ds(pl.multiple_of((1 + which_image) * tokens, 16), tokens)
        qgs_ref[pl.ds(start, tokens), :] = mix_refs[slot][span, :]

    lane = lax.broadcasted_iota(jnp.int32, (block, width), 1)
    ones = (lax.broadcasted_iota(jnp.int32, (half, block), 0) == 0).astype(jnp.bfloat16)
    zeros = jnp.zeros((half, block), jnp.bfloat16)

    def query_block(number, _):
        qg = qgs_ref[pl.ds(pl.multiple_of(number * block, block), block), :]
        qgt = qg.T
        scaled = qgt[:half].astype(jnp.float32) * (scale * LOG2E)
        high = scaled.astype(jnp.bfloat16)
        rest = (scaled - high.astype(jnp.float32)).astype(jnp.bfloat16)
        score_rhs = jnp.concatenate([high, zeros, ones, rest], axis=0)

        def score_pass(size, chunk, best):
            rows = rows_of(chunk, size)
            lhs = jnp.concatenate([kv_ref[rows, :], extra_ref[rows, :]], axis=1)
            scores = jnp.dot(lhs, score_rhs, preferred_element_type=jnp.float32)
            s_ref[rows, :] = scores
            return jnp.maximum(best, jnp.max(scores.reshape(size // 8, 8, block), axis=0))

        best = jnp.full((8, block), LOWEST, jnp.float32)
        for size, trips in sizes:
            best = lax.fori_loop(0, trips, functools.partial(score_pass, size), best)
        peak = jnp.max(best, axis=0, keepdims=True)

        def weight_pass(size, chunk, carried):
            total, out_t = carried
            rows = rows_of(chunk, size)
            weights = jnp.exp2(s_ref[rows, :] - peak)
            total = total + jnp.sum(weights.reshape(size // 8, 8, block), axis=0)
            weights = weights.astype(jnp.bfloat16)
            p_ref[rows, :] = weights
            out_t = out_t + jnp.dot(
                kvt_ref[half:, rows], weights, preferred_element_type=jnp.float32
            )
            return total, out_t

        carried = (jnp.zeros((8, block), jnp.float32), jnp.zeros((half, block), jnp.float32))
        for size, trips in sizes:
            carried = lax.fori_loop(0, trips, functools.partial(weight_pass, size), carried)
        total, out_t = carried
        inverse = 1.0 / jnp.sum(total, axis=0, keepdims=True)
        out_t = out_t * inverse
        grad_t = qgt[half:].astype(jnp.float32) * inverse
        delta = jnp.sum(out_t * grad_t, axis=0, keepdims=True) * scale
        grad_rhs = jnp.concatenate([zeros, (grad_t * scale).astype(jnp.bfloat16)], axis=0)
        grad_rows = jnp.concatenate([jnp.zeros_like(grad_t), grad_t], axis=0).T
        out_rhs = jnp.concatenate(
            [jnp.where(lane < half, qg, jnp.zeros_like(qg)), grad_rows.astype(jnp.bfloat16)], axis=0
        )

        def grad_pass(size, chunk, dq_t):
            rows = rows_of(chunk, size)
            prob_grad = jnp.dot(kv_ref[rows, :], grad_rhs, preferred_element_type=jnp.float32)
            weights = p_ref[rows, :]
            score_grad = (weights.astype(jnp.float32) * (prob_grad - delta)).astype(jnp.bfloat16)
            acc_ref[rows, :] += jnp.dot(
                jnp.concatenate([score_grad, weights], axis=1),
                out_rhs,
                preferred_element_type=jnp.float32,
            )
            return dq_t + jnp.dot(
                kvt_ref[:half, rows], score_grad, preferred_element_type=jnp.float32
            )

        dq_t = jnp.zeros((half, block), jnp.float32)
        for size, trips in sizes:
            dq_t = lax.fori_loop(0, trips, functools.partial(grad_pass, size), dq_t)
        result = jnp.concatenate([dq_t, out_t], axis=0).T.astype(jnp.bfloat16)
        rows_ref[pl.ds(pl.multiple_of(number * block, block), block), :] = result
        return 0

    lax.fori_loop(0, jnp.where(trips > 2, 2, 1), query_block, 0)
    for slot in range(4):
        start = pl.multiple_of(slot_of(slot) * pair, pair)
        rows_refs[slot][...] = rows_ref[pl.ds(start, tokens), :]
    if outs == 1:
        for which in range(8):
            for slot in range(4):
                for low, high, span in spans(slot_of(slot), which):
                    dkv_refs[0][which, slot, low:high, :] = acc_ref[span, :].astype(jnp.bfloat16)
    else:
        for ref, beside in zip(dkv_refs, (core, 1 - core)):
            for number in range(16):
                for low, high, span in spans(number // 4, 2 * (number % 4) + beside):
                    ref[number, low:high, :] = acc_ref[span, :].astype(jnp.bfloat16)


def attend(turn, info, mix, *kvs):
    width = mix[0].shape[-1]
    tokens = mix[0].shape[0] // 3
    keys = 8 * 4 * tokens
    block = 512
    vmem = pl.BlockSpec(memory_space=pltpu.VMEM)
    rows = jax.ShapeDtypeStruct((tokens, width), jnp.bfloat16)
    if len(kvs) == 2:
        grads = (jax.ShapeDtypeStruct((8, 4, tokens, width), jnp.bfloat16),)
    else:
        grads = (jax.ShapeDtypeStruct((16, tokens, width), jnp.bfloat16),) * 2
    arrays = [*mix, *kvs]
    results = pl.pallas_call(
        functools.partial(attention_kernel, turn, len(kvs), block),
        out_shape=(rows,) * 4 + grads,
        in_specs=[pl.BlockSpec(memory_space=pltpu.SMEM)]
        + [vmem] * len(arrays),
        out_specs=(vmem,) * (4 + len(grads)),
        scratch_shapes=[
            pltpu.VMEM((keys, width), jnp.bfloat16),
            pltpu.VMEM((keys, width), jnp.bfloat16),
            pltpu.VMEM((width, keys), jnp.bfloat16),
            pltpu.VMEM((2 * block, width), jnp.bfloat16),
            pltpu.VMEM((2 * block, width), jnp.bfloat16),
            pltpu.VMEM((keys, block), jnp.float32),
            pltpu.VMEM((keys, block), jnp.bfloat16),
            pltpu.VMEM((keys, width), jnp.float32),
        ],
        compiler_params=pltpu.CompilerParams(vmem_limit_bytes=VMEM_ATTENTION),
        cost_estimate=pl.CostEstimate(
            flops=6 * 2 * 1024 * keys * 256,
            bytes_accessed=8 * 2**20,
            transcendentals=1024 * keys,
        ),
        name="attention",
    )(info, *arrays)
    return results[:4], *results[4:]


def per_device(
    image,
    embedding,
    cotangent,
    valid_rows,
    orientation,
    gn1_gain,
    gn1_bias,
    conv1_weight,
    conv1_bias,
    time_weight,
    time_bias,
    gn2_gain,
    gn2_bias,
    conv2_weight,
    conv2_bias,
    gn3_gain,
    gn3_bias,
    qkv_weight,
    qv_bias,
    proj_weight,
    proj_bias,
):
    images, shard_rows, columns, channels = image.shape
    tokens = shard_rows * columns
    head_width = channels // HEAD_COUNT
    seq_index = lax.axis_index("seq")
    dp_index = lax.axis_index("dp")
    places = {"x": seq_index // 8, "y": seq_index // 2 % 4, "c": seq_index % 2, "z": dp_index}
    place_x, place_y, place_c = places["x"], places["y"], places["c"]
    col_valid = columns - 2 * columns // 5 * orientation
    info = jnp.stack(
        [
            jnp.asarray(number, jnp.int32)
            for number in (
                seq_index * shard_rows,
                valid_rows[0],
                valid_rows[1],
                col_valid[0],
                col_valid[1],
                place_x,
                place_c,
                0,
            )
        ]
    )
    counts = (valid_rows * col_valid).astype(jnp.float32) * (channels // GROUPS)
    scalars = (info, counts)
    gain1, bias1, gain2, bias2, gain3, bias3, conv1_bias, conv2_bias, proj_bias = (
        value[None]
        for value in (
            gn1_gain, gn1_bias, gn2_gain, gn2_bias, gn3_gain, gn3_bias, conv1_bias, conv2_bias, proj_bias,
        )
    )
    taps = conv1_weight.shape
    conv1_weight = conv1_weight.reshape(-1, channels)
    conv2_weight = conv2_weight.reshape(-1, channels)
    wide, low_kind = jnp.float32, jnp.bfloat16
    field = (images, shard_rows, columns, channels)
    edges = (2, images, 2, columns, channels)
    extended_field = (images, shard_rows + 2, columns, channels)

    by_head = jnp.transpose(
        qkv_weight.reshape(channels, 3, HEAD_COUNT, head_width), (2, 1, 0, 3)
    )
    proj_heads = proj_weight.reshape(HEAD_COUNT, head_width, channels)
    blank = jnp.zeros((HEAD_COUNT, channels, head_width), low_kind)
    key_weight = jnp.concatenate([by_head[:, 1], by_head[:, 2]], axis=2)
    query_weight = jnp.concatenate(
        [
            jnp.concatenate([by_head[:, 0], blank], axis=2),
            jnp.concatenate([blank, jnp.swapaxes(proj_heads, 1, 2)], axis=2),
        ],
        axis=1,
    )
    blank_rows = jnp.swapaxes(blank, 1, 2)
    turned = jnp.swapaxes(by_head, 2, 3)
    key_weight_t = jnp.concatenate([turned[:, 1], turned[:, 2]], axis=1)
    query_weight_t = jnp.concatenate([turned[:, 0], blank_rows], axis=1)
    proj_weight_t = jnp.concatenate([blank_rows, proj_heads], axis=1)
    head_bias = qv_bias.reshape(2, HEAD_COUNT, 1, head_width)
    blank_bias = jnp.zeros((HEAD_COUNT, 1, head_width), wide)
    query_bias = jnp.concatenate([head_bias[0], blank_bias], axis=2)
    key_bias = jnp.concatenate([blank_bias, head_bias[1]], axis=2)

    time_input = jax.nn.silu(embedding.astype(wide)).astype(low_kind)
    shifts = jnp.dot(time_input, time_weight, preferred_element_type=wide) + time_bias

    core_edges, next_edges, sums1 = run_kernel(
        start_kernel,
        (valid_rows, orientation),
        (),
        ((edges, low_kind), (edges, low_kind), ((4, channels), wide)),
        scratch=(pltpu.SMEM((8,), jnp.int32),),
        early=(image, cotangent),
    )
    core_edges, next_edges = swap_edges(core_edges, next_edges)
    sums1, next_edges = seq_total(sums1, next_edges)
    active1, hidden, sums2 = run_kernel(
        hidden_kernel,
        scalars,
        (core_edges, next_edges, sums1, gain1, bias1, conv1_bias, image, conv1_weight),
        ((extended_field, low_kind), (extended_field, wide), ((4, channels), wide)),
    )
    sums2 = seq_total(sums2)
    active2, residual, sums3 = run_kernel(
        residual_kernel,
        scalars,
        (hidden, sums2, gain2, bias2, shifts, conv2_bias, image, conv2_weight),
        ((extended_field, low_kind), (field, wide), ((4, channels), wide)),
    )
    sums3 = seq_total(sums3)

    third, proj_grad, placed_a, *slots = run_kernel(
        mixture_kernel,
        scalars,
        (residual, sums3, gain3, bias3, key_weight, query_weight, key_bias, query_bias),
        (((images * tokens, channels), low_kind),) * 2
        + (((16, tokens, 2 * head_width), low_kind),)
        + (((3 * tokens, 2 * head_width), low_kind),) * HEAD_COUNT,
        early=(cotangent,),
    )
    column = swap_places(placed_a)
    mix = [slots[0]] + [seq_shift(slots[d], d, 0, 0) for d in range(1, 4)]
    groups = [[x * 8 + place for place in range(8)] for x in range(4)]
    beside = seq_shift(column, 0, 0, 1)
    own_b = jnp.stack([part[:tokens] for part in mix])
    gathered_b = lax.all_gather(own_b, "seq", axis_index_groups=groups)
    rows_a, keys_a = attend(0, info, mix, column, beside)
    keys_a = lax.psum_scatter(keys_a, "seq", scatter_dimension=0, axis_index_groups=groups)
    rows_b, own_b, beside_b = attend(1, info, mix, gathered_b)
    keys_b = swap_places(low_sum(own_b, seq_shift(beside_b, 0, 0, 1)))

    rows = [jnp.stack(pair) for pair in zip(rows_a, rows_b)]
    rows = [rows[0]] + [seq_shift(rows[d], 4 - d, 0, 0) for d in range(1, 4)]
    keys_a = [keys_a[0]] + [seq_shift(keys_a[d], 4 - d, 0, 0) for d in range(1, 4)]
    output, third_grad, core_third, next_third, sums4, early_rest = run_kernel(
        output_kernel,
        scalars,
        (
            sums3, gain3, proj_bias, *rows, *keys_a, keys_b,
        ),
        (
            (field, low_kind), (field, wide), (edges, wide), (edges, wide), ((7, channels), wide),
            ((4, 2, HEAD_COUNT, head_width, channels // 2), low_kind),
        ),
        scratch=(pltpu.VMEM((2 * channels, 2 * head_width), wide),),
        early=(third, proj_grad, query_weight_t, key_weight_t, proj_weight_t),
        late=(residual,),
    )
    core_third, next_third = swap_edges(core_third, next_third)
    sums4, next_third = seq_total(sums4, next_third)
    residual_grad, early, norm2_grad, sums5 = run_kernel(
        branch_kernel,
        scalars,
        (
            core_third, next_third, core_edges, next_edges, sums3, gain3, sums4, sums2, gain2, bias2, shifts,
        ),
        (
            (field, wide), ((4, 2, 4, 208, channels // 2), low_kind), (extended_field, wide), ((5, channels), wide),
        ),
        early=(third_grad, residual, cotangent),
        late=(hidden, active2, conv2_weight, early_rest),
    )
    early = lax.psum_scatter(
        early.reshape((8,) + early.shape[2:]), "seq", scatter_dimension=0, axis_index_groups=groups
    )
    sums5 = seq_total(sums5)
    conv1_grad, norm1_grad, sums6 = run_kernel(
        hidden_grad_kernel,
        scalars,
        (
            sums2, gain2, shifts, sums5, sums1, gain1, bias1,
        ),
        (((2, 16, 144, channels // 2), low_kind), (field, wide), ((5, channels), wide)),
        early=(norm2_grad, hidden),
        late=(image, active1, conv1_weight),
    )
    late, early, sums6 = sums_over_seq(conv1_grad, sums6, early, places)
    both = jnp.concatenate([late, early])
    (image_grad,) = run_kernel(
        image_grad_kernel,
        scalars,
        (sums1, gain1, sums6),
        ((field, low_kind),),
        early=(image, norm1_grad, residual_grad),
    )

    scaling = shifts[:, :channels]
    scale_total = gain2 * sums5[2:4] + bias2 * sums5[:2]
    shift_low = jnp.concatenate([scale_total, sums5[:2]], axis=-1).astype(low_kind)
    embedding_grad = jnp.einsum(
        "ik,ek->ie", shift_low, time_weight, preferred_element_type=wide
    ) * silu_slope(embedding.astype(wide))
    rows = [
        sums6[2] + sums6[3],
        sums6[0] + sums6[1],
        sums6[4],
        jnp.sum((1.0 + scaling) * sums5[2:4], axis=0),
        jnp.sum((1.0 + scaling) * sums5[:2], axis=0),
        sums5[4],
        sums4[2] + sums4[3],
        sums4[0] + sums4[1],
        sums4[4],
        sums4[5],
        sums4[6],
    ]
    time_pair = jnp.concatenate([time_input, shift_low], axis=-1)
    both, totals, every_pair = sums_over_dp(
        both, jnp.stack(rows), time_pair.reshape(-1, channels // 2), places
    )
    every_input, every_shift = jnp.split(
        every_pair.reshape(-1, time_pair.shape[-1]), (time_input.shape[-1],), axis=-1
    )
    time_weight_grad = jnp.einsum(
        "ie,ik->ek", every_input, every_shift, preferred_element_type=wide
    )
    time_bias_grad = jnp.sum(every_shift, axis=0, dtype=wide)
    parts = gathered_over_seq(both, places)
    shapes = [conv1_weight.shape, conv2_weight.shape, (channels, 3 * channels), (channels, channels)]
    vmem = pl.BlockSpec(memory_space=pltpu.VMEM)
    conv1_total, conv2_total, qkv_total, proj_total = pl.pallas_call(
        weights_kernel,
        out_shape=tuple(jax.ShapeDtypeStruct(shape, wide) for shape in shapes),
        in_specs=[pl.BlockSpec(memory_space=pltpu.SMEM), vmem, vmem],
        out_specs=(pl.BlockSpec(memory_space=pltpu.HBM),) * 4,
        scratch_shapes=[pltpu.VMEM(shape, wide) for shape in shapes]
        + [pltpu.VMEM((4 * channels, channels), wide), pltpu.SemaphoreType.DMA((4,))],
        compiler_params=pltpu.CompilerParams(vmem_limit_bytes=VMEM_CONV),
        name="weights_kernel",
    )(info, *parts)
    return (
        output,
        image_grad,
        embedding_grad,
        totals[0],
        totals[1],
        conv1_total.reshape(taps),
        totals[2],
        time_weight_grad,
        time_bias_grad,
        totals[3],
        totals[4],
        conv2_total.reshape(taps),
        totals[5],
        totals[6],
        totals[7],
        qkv_total,
        jnp.concatenate([totals[8], totals[9]]),
        proj_total,
        totals[10],
    )


def solution(mesh):
    return jax.shard_map(
        per_device,
        mesh=mesh,
        in_specs=(
            P("dp", "seq", None, None),
            P("dp", None),
            P("dp", "seq", None, None),
            P("dp"),
            P("dp"),
            P(),
            P(),
            P(),
            P(),
            P(),
            P(),
            P(),
            P(),
            P(),
            P(),
            P(),
            P(),
            P(),
            P(),
            P(),
            P(),
        ),
        out_specs=(
            P("dp", "seq", None, None),
            P("dp", "seq", None, None),
            P("dp", None),
            P(),
            P(),
            P(),
            P(),
            P(),
            P(),
            P(),
            P(),
            P(),
            P(),
            P(),
            P(),
            P(),
            P(),
            P(),
            P(),
        ),
        check_vma=False,
    )
```

```python
import functools

import jax
import jax.numpy as jnp
from jax import lax
from jax.experimental import pallas as pl
from jax.experimental.pallas import tpu as pltpu
from jax.sharding import PartitionSpec as P

GROUPS = 32
HEAD_COUNT = 4


EPS = 1e-05
LOWEST = -1e30
LOG2E = 1.4426950408889634

LEFT = 24

VMEM_CONV = 24 * 2**20
VMEM_ATTENTION = 44 * 2**20


def seq_shift(value, dx, dy, dc):
    pairs = []
    for place in range(32):
        x, y, c = place // 8, place // 2 % 4, place % 2
        pairs.append((place, (x + dx) % 4 * 8 + (y + dy) % 4 * 2 + (c + dc) % 2))
    return lax.ppermute(value, "seq", pairs)


def axis_shift(value, axis, step):
    if axis == "x":
        return seq_shift(value, step, 0, 0)
    if axis == "y":
        return seq_shift(value, 0, step, 0)
    return lax.ppermute(value, "dp", [(i, (i + step) % 4) for i in range(4)])


def swap_edges(core_edges, next_edges):
    pairs = [(i, (i + 1) % 32 if i % 2 else (i - 1) % 32) for i in range(32)]
    return seq_shift(core_edges, 0, 0, 1), lax.ppermute(next_edges, "seq", pairs)


def swap_places(value):
    groups = [[place * 2 + core for place in range(16)] for core in range(2)]
    return lax.all_to_all(value, "seq", 0, 0, axis_index_groups=groups)


def seq_total(value, beside=None):
    value = value + seq_shift(value, 0, 0, 1)
    swapped = swap_places(jnp.broadcast_to(value[None], (16,) + value.shape))
    if beside is None:
        return jnp.sum(swapped, axis=0)
    swapped, beside = lax.optimization_barrier((swapped, beside))
    return jnp.sum(swapped, axis=0), beside


def core_total(value, c):
    return low_sum(take_slot(value, c), seq_shift(take_slot(value, 1 - c), 0, 0, 1))


def take_slot(value, slot):
    return lax.dynamic_index_in_dim(value, slot, 0, keepdims=False)


def low_sum(*parts):
    total = parts[0].astype(jnp.float32)
    for part in parts[1:]:
        total = total + part.astype(jnp.float32)
    return total.astype(jnp.bfloat16)


def scatter_ring(value, axis, place):
    return low_sum(
        take_slot(value, place),
        *(axis_shift(take_slot(value, (place + step) % 4), axis, step) for step in (1, 3, 2)),
    )


def gather_ring(value, axis, place):
    result = jnp.zeros((4,) + value.shape, value.dtype)
    result = lax.dynamic_update_index_in_dim(result, value, place, 0)
    for step in (1, 3, 2):
        result = lax.dynamic_update_index_in_dim(
            result, axis_shift(value, axis, step), (place - step) % 4, 0
        )
    return result


def split_low(value):
    high = value.astype(jnp.bfloat16)
    both = jnp.concatenate([high, (value - high.astype(jnp.float32)).astype(jnp.bfloat16)])
    both = both.reshape(-1, 128)
    return jnp.pad(both, ((0, -both.shape[0] % 16), (0, 0)))


def join_low(value, rows):
    value = value[: 4 * rows].astype(jnp.float32).reshape(2, rows, 256)
    return value[0] + value[1]


def paired(parts):
    return (parts[0] + parts[2]) + (parts[1] + parts[3])


def sums_over_seq(late, vector, early, places):
    late = core_total(late, places["c"])
    low = split_low(vector + seq_shift(vector, 0, 0, 1))
    swapped = swap_places(
        jnp.concatenate([late, jnp.broadcast_to(low[None], (16,) + low.shape)], axis=1)
    )
    early = scatter_ring(early, "x", places["x"])
    swapped, early = lax.optimization_barrier((swapped, early))
    total = jnp.sum(swapped.astype(jnp.float32), axis=0)
    count = late.shape[1]
    return total[:count].astype(jnp.bfloat16), early, join_low(total[count:], vector.shape[0])


def sums_over_dp(both, vector, extra, places):
    low = split_low(vector)
    sent = jnp.concatenate([both, low, extra])
    got = [sent] + [axis_shift(sent, "z", step) for step in (1, 2, 3)]
    count = both.shape[0]
    both = paired([part[:count].astype(jnp.float32) for part in got]).astype(jnp.bfloat16)
    count += low.shape[0]
    vector = paired(
        [join_low(part[count - low.shape[0] : count], vector.shape[0]) for part in got]
    )
    extras = jnp.zeros((4,) + extra.shape, extra.dtype)
    for step in range(4):
        extras = lax.dynamic_update_index_in_dim(
            extras, got[step][count:], (places["z"] - step) % 4, 0
        )
    return both, vector, extras


def gathered_over_seq(both, places):
    both = gather_ring(both, "y", places["y"])
    both = gather_ring(both, "x", places["x"]).reshape((16, -1) + both.shape[2:])
    return both, seq_shift(both, 0, 0, 1)


def silu_slope(values):
    sigmoid = jax.nn.sigmoid(values)
    return sigmoid * (1.0 + values * (1.0 - sigmoid))


def same_group(channels):
    size = channels // GROUPS
    rows = lax.broadcasted_iota(jnp.int32, (channels, channels), 0) // size
    cols = lax.broadcasted_iota(jnp.int32, (channels, channels), 1) // size
    return (rows == cols).astype(jnp.float32)


def over_group(sums, channels):
    return jnp.dot(
        sums, same_group(channels), precision=lax.Precision.HIGHEST, preferred_element_type=jnp.float32
    )


def norm_terms(sums, counts_ref):
    totals = over_group(sums[:4], sums.shape[-1])
    terms = []
    for i in range(2):
        average = totals[i : i + 1] / counts_ref[i]
        spread = lax.rsqrt(totals[2 + i : 3 + i] / counts_ref[i] - average * average + EPS)
        terms.append((average, spread))
    return terms


def mask_of(info_ref, i, shape, border):
    rows = lax.broadcasted_iota(jnp.int32, shape, 0) + (info_ref[0] - border)
    cols = lax.broadcasted_iota(jnp.int32, shape, 1)
    valid = (rows >= 0) & (rows < info_ref[1 + i]) & (cols < info_ref[3 + i])
    return valid.astype(jnp.float32)


def extended(edges, own):
    low, high = edges
    return jnp.concatenate([low, own.astype(jnp.float32), high], axis=0)


def shifted(values):
    rows, columns, channels = values.shape
    cols = lax.broadcasted_iota(jnp.int32, values.shape, 1).reshape(-1, channels)
    flat = values.reshape(-1, channels)
    before = jnp.where(cols == 0, 0.0, pltpu.roll(flat, 1, 0))
    after = jnp.where(cols == columns - 1, 0.0, pltpu.roll(flat, rows * columns - 1, 0))
    return before, flat, after


def tap_rows(images, a, b, rows, columns=40):
    return jnp.concatenate(
        [image[b][a * columns : (a + rows) * columns] for image in images], axis=0
    ).astype(jnp.bfloat16)


def conv_taps(images, weight_ref, rows):
    patches = jnp.concatenate(
        [tap_rows(images, a, b, rows) for a in range(3) for b in range(3)], axis=1
    )
    return jnp.dot(patches, weight_ref[...], preferred_element_type=jnp.float32)


def put_rows(ref, first, values):
    rows = 9 * values.shape[1] // 16
    width = ref.shape[-1]
    last = first + values.shape[0]
    while first < last:
        place, low = divmod(first, rows)
        count = min(rows - low, last - first)
        for core in range(2):
            part = values[:count, core * width : (core + 1) * width].astype(jnp.bfloat16)
            if len(ref.shape) == 4:
                ref[core, place, low : low + count, :] = part
            else:
                ref[place // 4, core, place % 4, low : low + count, :] = part
        values = values[count:]
        first += count


def conv_grads(images, rows, actives, weight_ref, low, weight_grad_ref):
    total = None
    channels = low.shape[-1]
    for a in range(3):
        for b in range(3):
            span = slice((3 * a + b) * channels, (3 * a + b + 1) * channels)
            put_rows(
                weight_grad_ref,
                span.start,
                lax.dot_general(
                    tap_rows(actives, a, b, 6),
                    low,
                    (((0,), (0,)), ((), ())),
                    preferred_element_type=jnp.float32,
                ),
            )
            part = lax.dot_general(
                tap_rows(images, 2 - a, 2 - b, rows),
                weight_ref[span, :],
                (((1,), (1,)), ((), ())),
                preferred_element_type=jnp.float32,
            )
            total = part if total is None else total + part
    return total


def put_sums(ref, rows):
    for place, row in enumerate(rows):
        ref[place : place + 1, :] = row


def column_sum(values):
    return jnp.sum(values.reshape(-1, values.shape[-1]), axis=0, keepdims=True)


def put_edges(info_ref, core_ref, next_ref, which, i, first, last):
    first, last = first.astype(jnp.float32), last.astype(jnp.float32)
    low_core = info_ref[6] == 0
    core_ref[which, i] = jnp.where(low_core, last, first).astype(core_ref.dtype)
    next_ref[which, i] = jnp.where(low_core, first, last).astype(core_ref.dtype)


def edges_of(info_ref, core_ref, next_ref, which, i):
    low_core = info_ref[6] == 0
    core = core_ref[which, i].astype(jnp.float32)
    beyond = next_ref[which, i].astype(jnp.float32)
    return jnp.where(low_core, beyond, core), jnp.where(low_core, core, beyond)


def start_kernel(
    valid_rows_ref, orientation_ref, image_ref, cotangent_ref, core_ref, next_ref, out_sums_ref, info_ref
):
    place = lax.axis_index("seq")
    info_ref[0] = place * 6
    for i in range(2):
        info_ref[1 + i] = valid_rows_ref[i]
        info_ref[3 + i] = 40 - 16 * orientation_ref[i]
    info_ref[5] = lax.div(place, 8)
    info_ref[6] = lax.rem(place, 2)
    info_ref[7] = 0
    first, second = [], []
    for i in range(2):
        image = image_ref[i]
        cotangent = cotangent_ref[i]
        put_edges(info_ref, core_ref, next_ref, 0, i, image[:2], image[-2:])
        put_edges(info_ref, core_ref, next_ref, 1, i, cotangent[:2], cotangent[-2:])
        values = mask_of(info_ref, i, image.shape, 0) * image.astype(jnp.float32)
        first.append(column_sum(values))
        second.append(column_sum(values * values))
    put_sums(out_sums_ref, first + second)


def hidden_kernel(
    info_ref, counts_ref, core_ref, next_ref, sums_ref, gain_ref, bias_ref, conv_bias_ref, own_ref, weight_ref,
    active_ref, hidden_ref, out_sums_ref,
):
    terms = norm_terms(sums_ref[...], counts_ref)
    images = []
    for i in range(2):
        values = extended(edges_of(info_ref, core_ref, next_ref, 0, i), own_ref[i])
        mask = mask_of(info_ref, i, values.shape, 2)
        average, spread = terms[i]
        hat = mask * ((mask * values - average) * spread)
        active = jax.nn.silu(mask * (hat * gain_ref[...] + bias_ref[...])).astype(jnp.bfloat16)
        active_ref[i] = active[1:-1]
        images.append(shifted(active.astype(jnp.float32)))
    conv = conv_taps(images, weight_ref, 8)
    first, second = [], []
    for i in range(2):
        shape = hidden_ref.shape[1:]
        mask = mask_of(info_ref, i, shape, 1)
        half = conv.shape[0] // 2
        hidden = mask * (conv[i * half : (i + 1) * half].reshape(shape) + conv_bias_ref[...])
        hidden_ref[i] = hidden
        hidden = hidden[1:-1]
        first.append(column_sum(hidden))
        second.append(column_sum(hidden * hidden))
    put_sums(out_sums_ref, first + second)


def second_norm_of(values, mask, term, gain, bias, shifts_ref, i):
    channels = values.shape[-1]
    average, spread = term
    hat = mask * ((values - average) * spread)
    base = mask * (hat * gain + bias)
    scaling = shifts_ref[i : i + 1, :channels]
    offset = shifts_ref[i : i + 1, channels:]
    return hat, mask * (base * (1.0 + scaling) + offset)


def residual_kernel(
    info_ref, counts_ref, hidden_ref, sums_ref, gain_ref, bias_ref, shifts_ref, conv_bias_ref, image_ref, weight_ref,
    active_ref, residual_ref, out_sums_ref,
):
    terms = norm_terms(sums_ref[...], counts_ref)
    images = []
    for i in range(2):
        values = hidden_ref[i]
        mask = mask_of(info_ref, i, values.shape, 1)
        _, norm = second_norm_of(
            values, mask, terms[i], gain_ref[...], bias_ref[...], shifts_ref, i
        )
        active = jax.nn.silu(norm).astype(jnp.bfloat16)
        active_ref[i] = active
        images.append(shifted(active.astype(jnp.float32)))
    conv = conv_taps(images, weight_ref, 6)
    first, second = [], []
    for i in range(2):
        shape = residual_ref.shape[1:]
        mask = mask_of(info_ref, i, shape, 0)
        half = conv.shape[0] // 2
        residual = mask * image_ref[i].astype(jnp.float32) + mask * (
            conv[i * half : (i + 1) * half].reshape(shape) + conv_bias_ref[...]
        )
        residual_ref[i] = residual
        first.append(column_sum(residual))
        second.append(column_sum(residual * residual))
    put_sums(out_sums_ref, first + second)


def to_parts(values):
    channels = values.shape[-1]
    return jnp.concatenate(
        [values[:, :LEFT].reshape(-1, channels), values[:, LEFT:].reshape(-1, channels)], axis=0
    )


def from_parts(values, shape):
    rows, columns, channels = shape
    edge = rows * LEFT
    return jnp.concatenate(
        [
            values[:edge].reshape(rows, LEFT, channels),
            values[edge:].reshape(rows, columns - LEFT, channels),
        ],
        axis=1,
    )


def mixture_kernel(
    info_ref, counts_ref, residual_ref, sums_ref, gain_ref, bias_ref, key_weight_ref, query_weight_ref,
    key_bias_ref, query_bias_ref, cotangent_ref, third_ref, grad_ref, first_ref, *slot_refs,
):
    terms = norm_terms(sums_ref[...], counts_ref)
    tokens = third_ref.shape[0] // 2
    for i in range(2):
        values = residual_ref[i]
        mask = mask_of(info_ref, i, values.shape, 0)
        average, spread = terms[i]
        hat = mask * ((values - average) * spread)
        span = slice(i * tokens, (i + 1) * tokens)
        third_ref[span, :] = to_parts(mask * (hat * gain_ref[...] + bias_ref[...])).astype(
            jnp.bfloat16
        )
        grad_ref[span, :] = to_parts(mask * cotangent_ref[i].astype(jnp.float32)).astype(
            jnp.bfloat16
        )
    third = third_ref[...]
    both = jnp.concatenate([third, grad_ref[...]], axis=1)
    first = first_image(info_ref)
    third_first = third_ref[pl.ds(pl.multiple_of(first * tokens, 16), tokens), :]
    third_second = third_ref[pl.ds(pl.multiple_of((1 - first) * tokens, 16), tokens), :]
    for head in range(HEAD_COUNT):
        keys = (
            jnp.dot(third_first, key_weight_ref[head], preferred_element_type=jnp.float32)
            + key_bias_ref[head]
        ).astype(jnp.bfloat16)
        for place in range(4):
            first_ref[4 * head + place] = keys
    for slot, ref in enumerate(slot_refs):
        head = lax.rem(info_ref[5] + slot, HEAD_COUNT)
        keys = (
            jnp.dot(third_second, key_weight_ref[head], preferred_element_type=jnp.float32)
            + key_bias_ref[head]
        ).astype(jnp.bfloat16)
        queries = (
            jnp.dot(both, query_weight_ref[head], preferred_element_type=jnp.float32)
            + query_bias_ref[head]
        ).astype(jnp.bfloat16)
        ref[:tokens, :] = keys
        ref[tokens:, :] = queries


def output_kernel(
    info_ref, counts_ref, sums_ref, gain_ref, proj_bias_ref, *refs,
):
    row_refs, first_refs, key_ref, refs = refs[:4], refs[4:8], refs[8], refs[9:]
    third_ref, grad_ref, query_weight_ref, key_weight_ref, proj_weight_ref, residual_ref, *refs = refs
    output_ref, third_grad_ref, core_ref, next_ref, out_sums_ref, early_ref, columns_ref, wait = refs
    tokens, channels = third_ref.shape
    width = channels // 2
    head_width = channels // HEAD_COUNT
    third = third_ref[...]
    proj_grad = grad_ref[...]
    ones = jnp.ones((tokens, width), jnp.bfloat16)
    row_rhs = jnp.concatenate([third, proj_grad, ones], axis=1)
    key_rhs = jnp.concatenate([third, ones], axis=1)
    projected = None
    third_grad = None
    transposed = (((0,), (0,)), ((), ()))
    for slot in range(HEAD_COUNT):
        head = lax.rem(info_ref[5] + slot, HEAD_COUNT)
        turn = first_image(info_ref)
        rows = jnp.concatenate([row_refs[slot][turn], row_refs[slot][1 - turn]], axis=0)
        first_keys = first_refs[slot][...].astype(jnp.float32)
        last_keys = key_ref[pl.ds(pl.multiple_of(4 * head, 4), 4)].astype(jnp.float32)
        last_keys = jnp.sum(last_keys, axis=0)
        keys = jnp.concatenate(
            [
                jnp.where(turn == 0, first_keys, last_keys),
                jnp.where(turn == 0, last_keys, first_keys),
            ],
            axis=0,
        ).astype(jnp.bfloat16)
        part = jnp.dot(rows, proj_weight_ref[head], preferred_element_type=jnp.float32)
        projected = part if projected is None else projected + part
        part = jnp.dot(
            jnp.concatenate([rows, keys], axis=1),
            jnp.concatenate([query_weight_ref[head], key_weight_ref[head]], axis=0),
            preferred_element_type=jnp.float32,
        )
        third_grad = part if third_grad is None else third_grad + part
        row_grad = lax.dot_general(rows, row_rhs, transposed, preferred_element_type=jnp.float32)
        key_grad = lax.dot_general(keys, key_rhs, transposed, preferred_element_type=jnp.float32)
        start = pl.multiple_of(head * head_width, head_width)
        for place, block in (
            (0, row_grad[:head_width, :channels]),
            (channels, key_grad[:head_width, :channels]),
            (2 * channels, key_grad[head_width:, :channels]),
            (3 * channels, row_grad[head_width:, channels : 2 * channels]),
        ):
            for core in range(2):
                early_ref[place // channels, core, head] = block[
                    :, core * width : (core + 1) * width
                ].astype(jnp.bfloat16)
        columns_ref[pl.ds(start, head_width), :] = row_grad[:head_width, 2 * channels :]
        columns_ref[pl.ds(channels + start, head_width), :] = key_grad[head_width:, channels:]
    terms = norm_terms(sums_ref[...], counts_ref)
    wait()
    first, second = [], []
    for i in range(2):
        shape = residual_ref.shape[1:]
        span = slice(i * (tokens // 2), (i + 1) * (tokens // 2))
        values = residual_ref[i]
        mask = mask_of(info_ref, i, shape, 0)
        output_ref[i] = (
            values + mask * from_parts(projected[span] + proj_bias_ref[...], shape)
        ).astype(jnp.bfloat16)
        average, spread = terms[i]
        hat = mask * ((values - average) * spread)
        grad = mask * from_parts(third_grad[span], shape)
        third_grad_ref[i] = grad
        put_edges(info_ref, core_ref, next_ref, 0, i, grad[:2], grad[-2:])
        put_edges(info_ref, core_ref, next_ref, 1, i, values[:2], values[-2:])
        first.append(column_sum(grad))
        second.append(column_sum(grad * hat))
    query_row = columns_ref[:channels, :].T[:1]
    value_row = columns_ref[channels:, :].T[:1]
    put_sums(
        out_sums_ref,
        first + second + [query_row, value_row, column_sum(proj_grad.astype(jnp.float32))],
    )


def norm_grad_means(grad_sums, counts_ref, factors):
    rows = [grad_sums[i : i + 1] * factors[i] for i in range(2)]
    rows += [grad_sums[2 + i : 3 + i] * factors[i] for i in range(2)]
    totals = over_group(
        jnp.concatenate(rows, axis=0), rows[0].shape[-1]
    )
    return [
        (totals[i : i + 1] / counts_ref[i], totals[2 + i : 3 + i] / counts_ref[i])
        for i in range(2)
    ]


def branch_kernel(
    info_ref, counts_ref, core_ref, next_ref, cot_core_ref, cot_next_ref, sums3_ref, gain3_ref, sums4_ref, sums2_ref,
    gain2_ref, bias2_ref, shifts_ref, grad_ref, residual_ref, cot_ref, hidden_ref, active_ref, weight_ref, rest_ref,
    residual_grad_ref, weight_grad_ref, norm_grad_ref, out_sums_ref, wait,
):
    terms = norm_terms(sums3_ref[...], counts_ref)
    gain = gain3_ref[...]
    means = norm_grad_means(sums4_ref[...], counts_ref, [gain, gain])
    images, actives, lows = [], [], []
    shape = hidden_ref.shape[1:]
    channels = shape[-1]
    for i in range(2):
        grad = extended(edges_of(info_ref, core_ref, next_ref, 0, i), grad_ref[i])
        values = extended(edges_of(info_ref, core_ref, next_ref, 1, i), residual_ref[i])
        mask = mask_of(info_ref, i, values.shape, 2)
        average, spread = terms[i]
        hat = mask * ((values - average) * spread)
        first_mean, second_mean = means[i]
        residual_grad = extended(
            edges_of(info_ref, cot_core_ref, cot_next_ref, 1, i), cot_ref[i]
        ) + mask * (spread * (grad * gain - first_mean - hat * second_mean))
        residual_grad_ref[i] = residual_grad[2:-2]
        low = (mask * residual_grad).astype(jnp.bfloat16).astype(jnp.float32)
        images.append(shifted(low))
        lows.append(low[2:-2].reshape(-1, channels))
    wait()
    for i in range(2):
        actives.append(shifted(active_ref[i].astype(jnp.float32)))
    low = jnp.concatenate(lows, axis=0)
    total = conv_grads(images, 8, actives, weight_ref, low.astype(jnp.bfloat16), weight_grad_ref)
    terms = norm_terms(sums2_ref[...], counts_ref)
    first, second = [], []
    for i in range(2):
        mask = mask_of(info_ref, i, shape, 1)
        hat, norm = second_norm_of(
            hidden_ref[i], mask, terms[i], gain2_ref[...], bias2_ref[...], shifts_ref, i
        )
        half = total.shape[0] // 2
        grad = mask * total[i * half : (i + 1) * half].reshape(shape) * silu_slope(norm)
        norm_grad_ref[i] = grad
        grad, hat = grad[1:-1], hat[1:-1]
        first.append(column_sum(grad))
        second.append(column_sum(grad * hat))
    put_sums(out_sums_ref, first + second + [column_sum(low)])
    weight_grad_ref[:, :, :, -rest_ref.shape[3] :, :] = rest_ref[...]


def hidden_grad_kernel(
    info_ref, counts_ref, sums2_ref, gain2_ref, shifts_ref, sums5_ref, sums1_ref, gain1_ref, bias1_ref,
    grad_ref, hidden_ref, image_ref, active_ref, weight_ref,
    weight_grad_ref, norm_grad_ref, out_sums_ref, wait,
):
    terms = norm_terms(sums2_ref[...], counts_ref)
    shape = image_ref.shape[1:]
    channels = shape[-1]
    factors = [(1.0 + shifts_ref[i : i + 1, :channels]) * gain2_ref[...] for i in range(2)]
    means = norm_grad_means(sums5_ref[...], counts_ref, factors)
    images, actives, lows = [], [], []
    for i in range(2):
        grad = grad_ref[i]
        values = hidden_ref[i]
        mask = mask_of(info_ref, i, values.shape, 1)
        average, spread = terms[i]
        hat = mask * ((values - average) * spread)
        first_mean, second_mean = means[i]
        low = mask * (spread * (grad * factors[i] - first_mean - hat * second_mean))
        low = low.astype(jnp.bfloat16).astype(jnp.float32)
        images.append(shifted(low))
        lows.append(low[1:-1].reshape(-1, channels))
    wait()
    for i in range(2):
        actives.append(shifted(active_ref[i].astype(jnp.float32)))
    low = jnp.concatenate(lows, axis=0)
    total = conv_grads(images, 6, actives, weight_ref, low.astype(jnp.bfloat16), weight_grad_ref)
    terms = norm_terms(sums1_ref[...], counts_ref)
    first, second = [], []
    for i in range(2):
        mask = mask_of(info_ref, i, shape, 0)
        average, spread = terms[i]
        hat = mask * ((mask * image_ref[i].astype(jnp.float32) - average) * spread)
        norm = mask * (hat * gain1_ref[...] + bias1_ref[...])
        half = total.shape[0] // 2
        grad = mask * total[i * half : (i + 1) * half].reshape(shape) * silu_slope(norm)
        norm_grad_ref[i] = grad
        first.append(column_sum(grad))
        second.append(column_sum(grad * hat))
    put_sums(out_sums_ref, first + second + [column_sum(low)])


def image_grad_kernel(
    info_ref, counts_ref, sums1_ref, gain1_ref, sums6_ref, image_ref, grad_ref, residual_grad_ref, out_ref
):
    terms = norm_terms(sums1_ref[...], counts_ref)
    gain = gain1_ref[...]
    means = norm_grad_means(sums6_ref[...], counts_ref, [gain, gain])
    for i in range(2):
        shape = image_ref.shape[1:]
        mask = mask_of(info_ref, i, shape, 0)
        average, spread = terms[i]
        hat = mask * ((mask * image_ref[i].astype(jnp.float32) - average) * spread)
        first_mean, second_mean = means[i]
        result = residual_grad_ref[i] + mask * (
            spread * (grad_ref[i] * gain - first_mean - hat * second_mean)
        )
        out_ref[i] = (mask * result).astype(jnp.bfloat16)


def weights_kernel(
    info_ref, own_ref, beside_ref, conv1_out, conv2_out, qkv_out, proj_out, conv1_ref, conv2_ref, qkv_ref, proj_ref,
    rest_ref, sems,
):
    channels = proj_ref.shape[0]
    width = channels // 2
    taps = conv1_ref.shape[0] // 16
    rest = 4 * channels // 16
    low_core = info_ref[6] == 0

    def write(first, count, target, in_order):
        def fill(refs):
            for core, ref in enumerate(refs):
                columns = slice(core * width, (core + 1) * width)
                for place in range(16):
                    number = place if in_order else place % 4 * 4 + place // 4
                    target[number * count : (number + 1) * count, columns] = ref[
                        place, first : first + count, :
                    ].astype(jnp.float32)

        @pl.when(low_core)
        def _():
            fill((own_ref, beside_ref))

        @pl.when(jnp.logical_not(low_core))
        def _():
            fill((beside_ref, own_ref))

    write(0, taps, conv1_ref, True)
    copies = [pltpu.make_async_copy(conv1_ref, conv1_out, sems.at[0])]
    copies[0].start()
    write(taps, taps, conv2_ref, False)
    copies.append(pltpu.make_async_copy(conv2_ref, conv2_out, sems.at[1]))
    copies[1].start()
    write(2 * taps, rest, rest_ref, False)
    for part in range(3):
        span = slice(part * channels, (part + 1) * channels)
        qkv_ref[:, span] = rest_ref[span, :].T
    proj_ref[...] = rest_ref[3 * channels :, :]
    copies.append(pltpu.make_async_copy(qkv_ref, qkv_out, sems.at[2]))
    copies.append(pltpu.make_async_copy(proj_ref, proj_out, sems.at[3]))
    copies[2].start()
    copies[3].start()
    for copy in copies:
        copy.wait()


def fetching(kernel, n_in, early, late, n_out):
    def body(*refs):
        count = early + late
        ins, refs = refs[:n_in], refs[n_in:]
        sources, refs = refs[:count], refs[count:]
        outs, refs = refs[:n_out], refs[n_out:]
        buffers, refs = refs[:count], refs[count:]
        sems, refs = refs[0], refs[1:]
        copies = [
            pltpu.make_async_copy(source, buffer, sems.at[number])
            for number, (source, buffer) in enumerate(zip(sources, buffers))
        ]
        for copy in copies:
            copy.start()
        for copy in copies[:early]:
            copy.wait()

        def wait():
            for copy in copies[early:]:
                copy.wait()

        kernel(*ins, *buffers, *outs, *refs, *((wait,) if late else ()))

    return body


def in_hbm(arrays):
    return [pltpu.with_memory_space_constraint(array, pltpu.HBM) for array in arrays]


def buffers_of(arrays):
    return [pltpu.VMEM(array.shape, array.dtype) for array in arrays] + [
        pltpu.SemaphoreType.DMA((len(arrays),))
    ]


def run_kernel(kernel, scalars, arrays, outs, scratch=(), early=(), late=()):
    vmem = pl.BlockSpec(memory_space=pltpu.VMEM)
    smem = pl.BlockSpec(memory_space=pltpu.SMEM)
    hbm = pl.BlockSpec(memory_space=pltpu.HBM)
    fetched = [*early, *late]
    body, scratch = kernel, list(scratch)
    if fetched:
        body = fetching(kernel, len(scalars) + len(arrays), len(early), len(late), len(outs))
        scratch = buffers_of(fetched) + scratch
    return pl.pallas_call(
        body,
        out_shape=tuple(jax.ShapeDtypeStruct(shape, kind) for shape, kind in outs),
        in_specs=[smem] * len(scalars) + [vmem] * len(arrays) + [hbm] * len(fetched),
        out_specs=(vmem,) * len(outs),
        scratch_shapes=scratch,
        compiler_params=pltpu.CompilerParams(vmem_limit_bytes=VMEM_CONV),
        cost_estimate=pl.CostEstimate(
            flops=2 * 10**9, bytes_accessed=4 * 2**20, transcendentals=0
        ),
        name=kernel.__name__,
    )(*scalars, *arrays, *in_hbm(fetched))


def first_image(info_ref):
    work = [lax.div(info_ref[1 + i] + 47, 48) * info_ref[3 + i] for i in range(2)]
    return jnp.where(work[1] < work[0], 1, 0)


def attention_kernel(turn, pieces, block, info_ref, *refs):
    mix_refs, refs = refs[:4], refs[4:]
    kv_refs, refs = refs[:pieces], refs[pieces:]
    outs = 1 if pieces == 2 else 2
    rows_refs, dkv_refs, refs = refs[:4], refs[4 : 4 + outs], refs[4 + outs :]
    kv_ref, extra_ref, kvt_ref, qgs_ref, rows_ref, s_ref, p_ref, acc_ref, *wait = refs
    tokens, width = rows_refs[0].shape
    half = width // 2
    whole = 8 * tokens
    edge = tokens * LEFT // 40
    left = 8 * edge
    which_image = first_image(info_ref) if turn == 0 else 1 - first_image(info_ref)
    valid_rows = info_ref[1 + which_image]
    landscape = info_ref[3 + which_image] == 40
    place, core = info_ref[5], info_ref[6]
    trips = lax.div(valid_rows + 47, 48)
    sizes = ((whole, jnp.where(landscape, trips, 0)), (left, jnp.where(landscape, 0, trips)))
    scale = half ** (-0.5)
    pair = block // 2

    def slot_of(part):
        return lax.rem(place - part + 4, 4)

    def rows_of(chunk, size):
        return pl.ds(pl.multiple_of(chunk * whole, whole), size)

    def spans(part, which):
        return (
            (0, edge, pl.ds(pl.multiple_of(part * whole + which * edge, 16), edge)),
            (
                edge,
                tokens,
                pl.ds(
                    pl.multiple_of(part * whole + left + which * (tokens - edge), 16),
                    tokens - edge,
                ),
            ),
        )

    qgs_ref[...] = jnp.zeros(qgs_ref.shape, jnp.bfloat16)
    rows_ref[...] = jnp.zeros(rows_ref.shape, jnp.bfloat16)
    for slot in range(4):
        start = pl.multiple_of(slot_of(slot) * pair, pair)
        span = pl.ds(pl.multiple_of((1 + which_image) * tokens, 16), tokens)
        qgs_ref[pl.ds(start, tokens), :] = mix_refs[slot][span, :]
    for ready in wait:
        ready()
    if pieces == 2:
        for ref, beside in zip(kv_refs, (core, 1 - core)):
            for number in range(16):
                for low, high, span in spans(number // 4, 2 * (number % 4) + beside):
                    kv_ref[span, :] = ref[number, low:high, :]
    else:
        for which in range(8):
            for slot in range(4):
                for low, high, span in spans(slot_of(slot), which):
                    kv_ref[span, :] = kv_refs[0][which, slot, low:high, :]
    token_ids = lax.broadcasted_iota(jnp.int32, (whole, width), 0)
    key_lane = lax.broadcasted_iota(jnp.int32, (whole, width), 1)
    for slot in range(4):
        span = slice(slot * whole, (slot + 1) * whole)
        kvt_ref[:, span] = kv_ref[span, :].T
        acc_ref[span, :] = jnp.zeros((whole, width), jnp.float32)
        room = valid_rows - slot * (whole // 40)
        bound = jnp.where(token_ids < left, room * LEFT, left + room * (40 - LEFT))
        extra_ref[span, :] = jnp.where(
            key_lane < half,
            jnp.where(token_ids < bound, 0.0, LOWEST),
            pltpu.roll(kv_ref[span, :].astype(jnp.float32), half, 1),
        ).astype(jnp.bfloat16)
    lane = lax.broadcasted_iota(jnp.int32, (block, width), 1)
    ones = (lax.broadcasted_iota(jnp.int32, (half, block), 0) == 0).astype(jnp.bfloat16)
    zeros = jnp.zeros((half, block), jnp.bfloat16)

    def query_block(number, _):
        qg = qgs_ref[pl.ds(pl.multiple_of(number * block, block), block), :]
        qgt = qg.T
        scaled = qgt[:half].astype(jnp.float32) * (scale * LOG2E)
        high = scaled.astype(jnp.bfloat16)
        rest = (scaled - high.astype(jnp.float32)).astype(jnp.bfloat16)
        score_rhs = jnp.concatenate([high, zeros, ones, rest], axis=0)

        def score_pass(size, chunk, best):
            rows = rows_of(chunk, size)
            lhs = jnp.concatenate([kv_ref[rows, :], extra_ref[rows, :]], axis=1)
            scores = jnp.dot(lhs, score_rhs, preferred_element_type=jnp.float32)
            s_ref[rows, :] = scores
            return jnp.maximum(best, jnp.max(scores.reshape(size // 8, 8, block), axis=0))

        best = jnp.full((8, block), LOWEST, jnp.float32)
        for size, trips in sizes:
            best = lax.fori_loop(0, trips, functools.partial(score_pass, size), best)
        peak = jnp.max(best, axis=0, keepdims=True)

        def weight_pass(size, chunk, carried):
            total, out_t = carried
            rows = rows_of(chunk, size)
            weights = jnp.exp2(s_ref[rows, :] - peak)
            total = total + jnp.sum(weights.reshape(size // 8, 8, block), axis=0)
            weights = weights.astype(jnp.bfloat16)
            p_ref[rows, :] = weights
            out_t = out_t + jnp.dot(
                kvt_ref[half:, rows], weights, preferred_element_type=jnp.float32
            )
            return total, out_t

        carried = (jnp.zeros((8, block), jnp.float32), jnp.zeros((half, block), jnp.float32))
        for size, trips in sizes:
            carried = lax.fori_loop(0, trips, functools.partial(weight_pass, size), carried)
        total, out_t = carried
        inverse = 1.0 / jnp.sum(total, axis=0, keepdims=True)
        out_t = out_t * inverse
        grad_t = qgt[half:].astype(jnp.float32) * inverse
        delta = jnp.sum(out_t * grad_t, axis=0, keepdims=True) * scale
        grad_rhs = jnp.concatenate([zeros, (grad_t * scale).astype(jnp.bfloat16)], axis=0)
        grad_rows = jnp.concatenate([jnp.zeros_like(grad_t), grad_t], axis=0).T
        out_rhs = jnp.concatenate(
            [jnp.where(lane < half, qg, jnp.zeros_like(qg)), grad_rows.astype(jnp.bfloat16)], axis=0
        )

        def grad_pass(size, chunk, dq_t):
            rows = rows_of(chunk, size)
            prob_grad = jnp.dot(kv_ref[rows, :], grad_rhs, preferred_element_type=jnp.float32)
            weights = p_ref[rows, :]
            score_grad = (weights.astype(jnp.float32) * (prob_grad - delta)).astype(jnp.bfloat16)
            acc_ref[rows, :] += jnp.dot(
                jnp.concatenate([score_grad, weights], axis=1),
                out_rhs,
                preferred_element_type=jnp.float32,
            )
            return dq_t + jnp.dot(
                kvt_ref[:half, rows], score_grad, preferred_element_type=jnp.float32
            )

        dq_t = jnp.zeros((half, block), jnp.float32)
        for size, trips in sizes:
            dq_t = lax.fori_loop(0, trips, functools.partial(grad_pass, size), dq_t)
        result = jnp.concatenate([dq_t, out_t], axis=0).T.astype(jnp.bfloat16)
        rows_ref[pl.ds(pl.multiple_of(number * block, block), block), :] = result
        return 0

    lax.fori_loop(0, jnp.where(trips > 2, 2, 1), query_block, 0)
    for slot in range(4):
        start = pl.multiple_of(slot_of(slot) * pair, pair)
        rows_refs[slot][...] = rows_ref[pl.ds(start, tokens), :]
    if outs == 1:
        for which in range(8):
            for slot in range(4):
                for low, high, span in spans(slot_of(slot), which):
                    dkv_refs[0][which, slot, low:high, :] = acc_ref[span, :].astype(jnp.bfloat16)
    else:
        for ref, beside in zip(dkv_refs, (core, 1 - core)):
            for number in range(16):
                for low, high, span in spans(number // 4, 2 * (number % 4) + beside):
                    ref[number, low:high, :] = acc_ref[span, :].astype(jnp.bfloat16)


def attend(turn, info, mix, *kvs):
    width = mix[0].shape[-1]
    tokens = mix[0].shape[0] // 3
    keys = 8 * 4 * tokens
    block = 512
    vmem = pl.BlockSpec(memory_space=pltpu.VMEM)
    rows = jax.ShapeDtypeStruct((tokens, width), jnp.bfloat16)
    if len(kvs) == 2:
        grads = (jax.ShapeDtypeStruct((8, 4, tokens, width), jnp.bfloat16),)
    else:
        grads = (jax.ShapeDtypeStruct((16, tokens, width), jnp.bfloat16),) * 2
    kernel = functools.partial(attention_kernel, turn, len(kvs), block)
    arrays, late = ([*mix, *kvs], []) if len(kvs) == 2 else ([*mix], [*kvs])
    if late:
        kernel = fetching(kernel, 1 + len(arrays), 0, len(late), 4 + len(grads))
    results = pl.pallas_call(
        kernel,
        out_shape=(rows,) * 4 + grads,
        in_specs=[pl.BlockSpec(memory_space=pltpu.SMEM)]
        + [vmem] * len(arrays)
        + [pl.BlockSpec(memory_space=pltpu.HBM)] * len(late),
        out_specs=(vmem,) * (4 + len(grads)),
        scratch_shapes=(buffers_of(late) if late else [])
        + [
            pltpu.VMEM((keys, width), jnp.bfloat16),
            pltpu.VMEM((keys, width), jnp.bfloat16),
            pltpu.VMEM((width, keys), jnp.bfloat16),
            pltpu.VMEM((2 * block, width), jnp.bfloat16),
            pltpu.VMEM((2 * block, width), jnp.bfloat16),
            pltpu.VMEM((keys, block), jnp.float32),
            pltpu.VMEM((keys, block), jnp.bfloat16),
            pltpu.VMEM((keys, width), jnp.float32),
        ],
        compiler_params=pltpu.CompilerParams(vmem_limit_bytes=VMEM_ATTENTION),
        cost_estimate=pl.CostEstimate(
            flops=6 * 2 * 1024 * keys * 256,
            bytes_accessed=8 * 2**20,
            transcendentals=1024 * keys,
        ),
        name="attention",
    )(info, *arrays, *in_hbm(late))
    return results[:4], *results[4:]


def per_device(
    image,
    embedding,
    cotangent,
    valid_rows,
    orientation,
    gn1_gain,
    gn1_bias,
    conv1_weight,
    conv1_bias,
    time_weight,
    time_bias,
    gn2_gain,
    gn2_bias,
    conv2_weight,
    conv2_bias,
    gn3_gain,
    gn3_bias,
    qkv_weight,
    qv_bias,
    proj_weight,
    proj_bias,
):
    images, shard_rows, columns, channels = image.shape
    tokens = shard_rows * columns
    head_width = channels // HEAD_COUNT
    seq_index = lax.axis_index("seq")
    dp_index = lax.axis_index("dp")
    places = {"x": seq_index // 8, "y": seq_index // 2 % 4, "c": seq_index % 2, "z": dp_index}
    place_x, place_y, place_c = places["x"], places["y"], places["c"]
    col_valid = columns - 2 * columns // 5 * orientation
    info = jnp.stack(
        [
            jnp.asarray(number, jnp.int32)
            for number in (
                seq_index * shard_rows,
                valid_rows[0],
                valid_rows[1],
                col_valid[0],
                col_valid[1],
                place_x,
                place_c,
                0,
            )
        ]
    )
    counts = (valid_rows * col_valid).astype(jnp.float32) * (channels // GROUPS)
    scalars = (info, counts)
    gain1, bias1, gain2, bias2, gain3, bias3, conv1_bias, conv2_bias, proj_bias = (
        value[None]
        for value in (
            gn1_gain, gn1_bias, gn2_gain, gn2_bias, gn3_gain, gn3_bias, conv1_bias, conv2_bias, proj_bias,
        )
    )
    taps = conv1_weight.shape
    conv1_weight = conv1_weight.reshape(-1, channels)
    conv2_weight = conv2_weight.reshape(-1, channels)
    wide, low_kind = jnp.float32, jnp.bfloat16
    field = (images, shard_rows, columns, channels)
    edges = (2, images, 2, columns, channels)
    extended_field = (images, shard_rows + 2, columns, channels)

    by_head = jnp.transpose(
        qkv_weight.reshape(channels, 3, HEAD_COUNT, head_width), (2, 1, 0, 3)
    )
    proj_heads = proj_weight.reshape(HEAD_COUNT, head_width, channels)
    blank = jnp.zeros((HEAD_COUNT, channels, head_width), low_kind)
    key_weight = jnp.concatenate([by_head[:, 1], by_head[:, 2]], axis=2)
    query_weight = jnp.concatenate(
        [
            jnp.concatenate([by_head[:, 0], blank], axis=2),
            jnp.concatenate([blank, jnp.swapaxes(proj_heads, 1, 2)], axis=2),
        ],
        axis=1,
    )
    blank_rows = jnp.swapaxes(blank, 1, 2)
    turned = jnp.swapaxes(by_head, 2, 3)
    key_weight_t = jnp.concatenate([turned[:, 1], turned[:, 2]], axis=1)
    query_weight_t = jnp.concatenate([turned[:, 0], blank_rows], axis=1)
    proj_weight_t = jnp.concatenate([blank_rows, proj_heads], axis=1)
    head_bias = qv_bias.reshape(2, HEAD_COUNT, 1, head_width)
    blank_bias = jnp.zeros((HEAD_COUNT, 1, head_width), wide)
    query_bias = jnp.concatenate([head_bias[0], blank_bias], axis=2)
    key_bias = jnp.concatenate([blank_bias, head_bias[1]], axis=2)

    time_input = jax.nn.silu(embedding.astype(wide)).astype(low_kind)
    shifts = jnp.dot(time_input, time_weight, preferred_element_type=wide) + time_bias

    core_edges, next_edges, sums1 = run_kernel(
        start_kernel,
        (valid_rows, orientation),
        (),
        ((edges, low_kind), (edges, low_kind), ((4, channels), wide)),
        scratch=(pltpu.SMEM((8,), jnp.int32),),
        early=(image, cotangent),
    )
    core_edges, next_edges = swap_edges(core_edges, next_edges)
    sums1, next_edges = seq_total(sums1, next_edges)
    active1, hidden, sums2 = run_kernel(
        hidden_kernel,
        scalars,
        (core_edges, next_edges, sums1, gain1, bias1, conv1_bias, image, conv1_weight),
        ((extended_field, low_kind), (extended_field, wide), ((4, channels), wide)),
    )
    sums2 = seq_total(sums2)
    active2, residual, sums3 = run_kernel(
        residual_kernel,
        scalars,
        (hidden, sums2, gain2, bias2, shifts, conv2_bias, image, conv2_weight),
        ((extended_field, low_kind), (field, wide), ((4, channels), wide)),
    )
    sums3 = seq_total(sums3)

    third, proj_grad, placed_a, *slots = run_kernel(
        mixture_kernel,
        scalars,
        (residual, sums3, gain3, bias3, key_weight, query_weight, key_bias, query_bias),
        (((images * tokens, channels), low_kind),) * 2
        + (((16, tokens, 2 * head_width), low_kind),)
        + (((3 * tokens, 2 * head_width), low_kind),) * HEAD_COUNT,
        early=(cotangent,),
    )
    column = swap_places(placed_a)
    mix = [slots[0]] + [seq_shift(slots[d], d, 0, 0) for d in range(1, 4)]
    groups = [[x * 8 + place for place in range(8)] for x in range(4)]
    beside = seq_shift(column, 0, 0, 1)
    own_b = jnp.stack([part[:tokens] for part in mix])
    gathered_b = lax.all_gather(own_b, "seq", axis_index_groups=groups)
    rows_a, keys_a = attend(0, info, mix, column, beside)
    keys_a = lax.psum_scatter(keys_a, "seq", scatter_dimension=0, axis_index_groups=groups)
    rows_b, own_b, beside_b = attend(1, info, mix, gathered_b)
    keys_b = swap_places(low_sum(own_b, seq_shift(beside_b, 0, 0, 1)))

    rows = [jnp.stack(pair) for pair in zip(rows_a, rows_b)]
    rows = [rows[0]] + [seq_shift(rows[d], 4 - d, 0, 0) for d in range(1, 4)]
    keys_a = [keys_a[0]] + [seq_shift(keys_a[d], 4 - d, 0, 0) for d in range(1, 4)]
    output, third_grad, core_third, next_third, sums4, early_rest = run_kernel(
        output_kernel,
        scalars,
        (
            sums3, gain3, proj_bias, *rows, *keys_a, keys_b,
        ),
        (
            (field, low_kind), (field, wide), (edges, wide), (edges, wide), ((7, channels), wide),
            ((4, 2, HEAD_COUNT, head_width, channels // 2), low_kind),
        ),
        scratch=(pltpu.VMEM((2 * channels, 2 * head_width), wide),),
        early=(third, proj_grad, query_weight_t, key_weight_t, proj_weight_t),
        late=(residual,),
    )
    core_third, next_third = swap_edges(core_third, next_third)
    sums4, next_third = seq_total(sums4, next_third)
    residual_grad, early, norm2_grad, sums5 = run_kernel(
        branch_kernel,
        scalars,
        (
            core_third, next_third, core_edges, next_edges, sums3, gain3, sums4, sums2, gain2, bias2, shifts,
        ),
        (
            (field, wide), ((4, 2, 4, 208, channels // 2), low_kind), (extended_field, wide), ((5, channels), wide),
        ),
        early=(third_grad, residual, cotangent),
        late=(hidden, active2, conv2_weight, early_rest),
    )
    early = lax.psum_scatter(
        early.reshape((8,) + early.shape[2:]), "seq", scatter_dimension=0, axis_index_groups=groups
    )
    sums5 = seq_total(sums5)
    conv1_grad, norm1_grad, sums6 = run_kernel(
        hidden_grad_kernel,
        scalars,
        (
            sums2, gain2, shifts, sums5, sums1, gain1, bias1,
        ),
        (((2, 16, 144, channels // 2), low_kind), (field, wide), ((5, channels), wide)),
        early=(norm2_grad, hidden),
        late=(image, active1, conv1_weight),
    )
    late, early, sums6 = sums_over_seq(conv1_grad, sums6, early, places)
    both = jnp.concatenate([late, early])
    (image_grad,) = run_kernel(
        image_grad_kernel,
        scalars,
        (sums1, gain1, sums6),
        ((field, low_kind),),
        early=(image, norm1_grad, residual_grad),
    )

    scaling = shifts[:, :channels]
    scale_total = gain2 * sums5[2:4] + bias2 * sums5[:2]
    shift_low = jnp.concatenate([scale_total, sums5[:2]], axis=-1).astype(low_kind)
    embedding_grad = jnp.einsum(
        "ik,ek->ie", shift_low, time_weight, preferred_element_type=wide
    ) * silu_slope(embedding.astype(wide))
    rows = [
        sums6[2] + sums6[3],
        sums6[0] + sums6[1],
        sums6[4],
        jnp.sum((1.0 + scaling) * sums5[2:4], axis=0),
        jnp.sum((1.0 + scaling) * sums5[:2], axis=0),
        sums5[4],
        sums4[2] + sums4[3],
        sums4[0] + sums4[1],
        sums4[4],
        sums4[5],
        sums4[6],
    ]
    time_pair = jnp.concatenate([time_input, shift_low], axis=-1)
    both, totals, every_pair = sums_over_dp(
        both, jnp.stack(rows), time_pair.reshape(-1, channels // 2), places
    )
    every_input, every_shift = jnp.split(
        every_pair.reshape(-1, time_pair.shape[-1]), (time_input.shape[-1],), axis=-1
    )
    time_weight_grad = jnp.einsum(
        "ie,ik->ek", every_input, every_shift, preferred_element_type=wide
    )
    time_bias_grad = jnp.sum(every_shift, axis=0, dtype=wide)
    parts = gathered_over_seq(both, places)
    shapes = [conv1_weight.shape, conv2_weight.shape, (channels, 3 * channels), (channels, channels)]
    vmem = pl.BlockSpec(memory_space=pltpu.VMEM)
    conv1_total, conv2_total, qkv_total, proj_total = pl.pallas_call(
        weights_kernel,
        out_shape=tuple(jax.ShapeDtypeStruct(shape, wide) for shape in shapes),
        in_specs=[pl.BlockSpec(memory_space=pltpu.SMEM), vmem, vmem],
        out_specs=(pl.BlockSpec(memory_space=pltpu.HBM),) * 4,
        scratch_shapes=[pltpu.VMEM(shape, wide) for shape in shapes]
        + [pltpu.VMEM((4 * channels, channels), wide), pltpu.SemaphoreType.DMA((4,))],
        compiler_params=pltpu.CompilerParams(vmem_limit_bytes=VMEM_CONV),
        name="weights_kernel",
    )(info, *parts)
    return (
        output,
        image_grad,
        embedding_grad,
        totals[0],
        totals[1],
        conv1_total.reshape(taps),
        totals[2],
        time_weight_grad,
        time_bias_grad,
        totals[3],
        totals[4],
        conv2_total.reshape(taps),
        totals[5],
        totals[6],
        totals[7],
        qkv_total,
        jnp.concatenate([totals[8], totals[9]]),
        proj_total,
        totals[10],
    )


def solution(mesh):
    return jax.shard_map(
        per_device,
        mesh=mesh,
        in_specs=(
            P("dp", "seq", None, None),
            P("dp", None),
            P("dp", "seq", None, None),
            P("dp"),
            P("dp"),
            P(),
            P(),
            P(),
            P(),
            P(),
            P(),
            P(),
            P(),
            P(),
            P(),
            P(),
            P(),
            P(),
            P(),
            P(),
            P(),
        ),
        out_specs=(
            P("dp", "seq", None, None),
            P("dp", "seq", None, None),
            P("dp", None),
            P(),
            P(),
            P(),
            P(),
            P(),
            P(),
            P(),
            P(),
            P(),
            P(),
            P(),
            P(),
            P(),
            P(),
            P(),
            P(),
        ),
        check_vma=False,
    )
```
